256 devices in a mesh: ctx: 128 (over y, z, x), head: 2 (over core).
Axes of the slice: x: 4, y: 4, z: 8, core: 2. Of those that a mesh axis runs over, the one named last changes fastest.
Arguments:
- queries: bfloat16 [32768, 2560], P('ctx', 'head'), may hold values from -30 to 30
- keys: bfloat16 [32768, 512], P('ctx', 'head'), may hold values from -6 to 6
- values: bfloat16 [32768, 512], P('ctx', 'head'), may hold values from -6 to 6
- far_owners: int32 [256, 16], P('ctx'), may hold values from 0 to 127, as said below
- far_counts: int32 [256], P('ctx'), may hold values from 0 to 16, as said below
- pair_blocks: int32 [64, 128], replicated, may hold values from 0 to 255, as said below
Outputs:
- attended: bfloat16 [32768, 2560], P(('ctx', 'head'))
The draws below stay inside these ranges and needn't reach their ends.
Inputs may be any that keep to these rules, and one draw needn't show every extreme that they name: `far_owners`: entries j < far_counts[r] of row r are distinct shards before the shard that holds block r; the other entries are arbitrary shards. far_counts[r] is at most the index of the shard that holds block r. `pair_blocks`: entry [p, o] is a block held by shard o.
All inputs are finite; a program needn't handle non-finite values.
Results may differ from the reference program's by a relative error of at most 0.0049.
Values may be sent and summed in bfloat16 or wider, within the bound.
A program may use at most 128 MiB of HBM per device.

```python
import jax
import jax.numpy as jnp
from jax import lax

QUERY_HEADS = 20
KEY_VALUE_HEADS = 4
HEAD_WIDTH = 128
BLOCK_TOKENS = 128
TOK_DEV = 256
SHARDS = 128
PROMPT_TOKENS = 32768
BLOCK_COUNT = 256
BPD = 2
FMAX = 16


def count_rows(key):
    row_ids = jnp.arange(BLOCK_COUNT, dtype=jnp.int32)
    holder = row_ids // BPD
    half_cap = FMAX // 2
    ceiling = half_cap + (half_cap * (row_ids + 1) + BLOCK_COUNT - 1) // BLOCK_COUNT
    dropped = jax.random.randint(jax.random.fold_in(key, 17), (BLOCK_COUNT,), 0, 2, dtype=jnp.int32)
    dropped = jnp.where(row_ids == BLOCK_COUNT - 1, 0, dropped)
    return jnp.maximum(jnp.minimum(ceiling - dropped, holder), 0).astype(jnp.int32)


def owner_rows(key, counts):
    key = jax.random.fold_in(key, 6)
    row_ids = jnp.arange(BLOCK_COUNT, dtype=jnp.int32)
    holder = row_ids // BPD
    owner_ids = jnp.arange(SHARDS, dtype=jnp.int32)
    ranks = jax.random.randint(key, (BLOCK_COUNT, SHARDS), 0, 2 ** 20, dtype=jnp.int32) * SHARDS + owner_ids[None, :]
    ranks = jnp.where(owner_ids[None, :] < holder[:, None], ranks, ranks + 2 ** 28)
    ordered = jnp.argsort(ranks, axis=1, stable=True)[:, :FMAX].astype(jnp.int32)
    filler = jax.random.randint(jax.random.fold_in(key, 1), (BLOCK_COUNT, FMAX), 0, SHARDS, dtype=jnp.int32)
    slot_ids = jnp.arange(FMAX, dtype=jnp.int32)
    return jnp.where(slot_ids[None, :] < counts[:, None], ordered, filler)


def pair_table(key):
    key = jax.random.fold_in(key, 3)
    owner_ids = jnp.arange(SHARDS, dtype=jnp.int32)
    offsets = jax.random.randint(key, (SHARDS // 2, SHARDS), 0, BPD, dtype=jnp.int32)
    return owner_ids[None, :] * BPD + offsets


def draw_queries(key, part):
    device_key = jax.random.fold_in(key, 1)
    sampled_entries = jnp.clip(2.5 * jax.random.normal(device_key, (BLOCK_COUNT, BLOCK_TOKENS, QUERY_HEADS * HEAD_WIDTH), jnp.float32), -15.0, 15.0)
    return sampled_entries.reshape(PROMPT_TOKENS, QUERY_HEADS * HEAD_WIDTH).astype(jnp.bfloat16)


def draw_keys(key, part):
    device_key = jax.random.fold_in(key, 2)
    sampled_entries = jnp.clip(jax.random.normal(device_key, (BLOCK_COUNT, BLOCK_TOKENS, KEY_VALUE_HEADS * HEAD_WIDTH), jnp.float32), -6.0, 6.0)
    return sampled_entries.reshape(PROMPT_TOKENS, KEY_VALUE_HEADS * HEAD_WIDTH).astype(jnp.bfloat16)


def draw_far_counts(key, part):
    return count_rows(key)


def draw_far_owners(key, part):
    return owner_rows(key, count_rows(key))


def draw_pair_blocks(key, part):
    return pair_table(key)


def block_levels(key, dims, shards, least, high):
    def one(dim, shards_of):
        heights = jax.random.uniform(jax.random.fold_in(jax.random.fold_in(key, 6), dim), (shards_of,), jnp.float32, least / len(shards), high / len(shards))
        return jnp.repeat(jnp.exp(heights), dims[dim] // shards_of).reshape((-1,) + (1,) * (len(dims) - dim - 1))

    level = one(*shards[0])
    for cut in shards[1:]:
        level = level * one(*cut)
    return level


def bell_draw(key, dims, deviation, bound, pieces=(), kind=jnp.bfloat16):
    result = deviation * jax.random.normal(key, dims, jnp.float32)
    if pieces:
        result = result * block_levels(key, dims, pieces, -0.22, 0.18)
    return jnp.clip(result, -bound, bound).astype(kind)


def setup_inputs(seed: int = 0) -> dict:
    arg_keys = jax.random.split(jax.random.key(seed), 7)
    return {
        "queries": draw_queries(jax.random.fold_in(arg_keys[6], 71), 0),
        "keys": draw_keys(jax.random.fold_in(arg_keys[6], 71), 0),
        "values": bell_draw(arg_keys[2], (PROMPT_TOKENS, KEY_VALUE_HEADS * HEAD_WIDTH), 1.0, 6.0, ((0, 128), (1, 2))),
        "far_owners": draw_far_owners(jax.random.fold_in(arg_keys[6], 71), 0),
        "far_counts": draw_far_counts(jax.random.fold_in(arg_keys[6], 71), 0),
        "pair_blocks": draw_pair_blocks(jax.random.fold_in(arg_keys[6], 71), 0),
    }


def reference(queries, keys, values, far_owners, far_counts, pair_blocks):
    group_width = QUERY_HEADS // KEY_VALUE_HEADS
    score_scale = HEAD_WIDTH ** -0.5
    block_ids = jnp.arange(BLOCK_TOKENS, dtype=jnp.int32)
    local_ids = jnp.arange(TOK_DEV, dtype=jnp.int32)
    far_slots = jnp.arange(FMAX, dtype=jnp.int32)

    def one_row(row_index):
        device = row_index // BPD
        partner = jnp.minimum(device, SHARDS - 1 - device)
        start = (row_index * BLOCK_TOKENS).astype(jnp.int32)
        query_block_index = lax.dynamic_slice_in_dim(queries, start, BLOCK_TOKENS, 0).astype(jnp.float32)
        query_block_index = query_block_index.reshape(BLOCK_TOKENS, KEY_VALUE_HEADS, group_width, HEAD_WIDTH)
        shard_start = (device * TOK_DEV).astype(jnp.int32)
        resident_keys = lax.dynamic_slice_in_dim(keys, shard_start, TOK_DEV, 0)
        resident_values = lax.dynamic_slice_in_dim(values, shard_start, TOK_DEV, 0)
        far_ids = pair_blocks[partner][far_owners[row_index]]
        remote_tokens = (far_ids[:, None] * BLOCK_TOKENS + block_ids[None, :]).reshape(-1).astype(jnp.int32)
        gathered_keys = jnp.concatenate([resident_keys, keys[remote_tokens]], 0).astype(jnp.float32).reshape(-1, KEY_VALUE_HEADS, HEAD_WIDTH)
        gathered_values = jnp.concatenate([resident_values, values[remote_tokens]], 0).astype(jnp.float32).reshape(-1, KEY_VALUE_HEADS, HEAD_WIDTH)
        query_pos = (row_index % BPD) * BLOCK_TOKENS + block_ids
        local_seen = local_ids[None, :] <= query_pos[:, None]
        far_seen = jnp.repeat(far_slots < far_counts[row_index], BLOCK_TOKENS)
        far_seen = jnp.broadcast_to(far_seen[None, :], (BLOCK_TOKENS, FMAX * BLOCK_TOKENS))
        visible = jnp.concatenate([local_seen, far_seen], 1)
        scores = jnp.einsum("qhgd,khd->hgqk", query_block_index, gathered_keys) * score_scale
        scores = jnp.where(visible[None, None], scores, -jnp.inf)
        row_top = scores.max(-1, keepdims=True)
        raised = jnp.exp(scores - row_top)
        weights = (raised / raised.sum(-1, keepdims=True)).astype(jnp.bfloat16)
        mixed = jnp.einsum("hgqk,khd->qhgd", weights.astype(jnp.float32), gathered_values)
        return mixed.reshape(BLOCK_TOKENS, QUERY_HEADS * HEAD_WIDTH).astype(jnp.bfloat16)

    attended = lax.map(one_row, jnp.arange(BLOCK_COUNT, dtype=jnp.int32))
    return attended.reshape(PROMPT_TOKENS, QUERY_HEADS * HEAD_WIDTH)
```

```python
import functools

import jax
import jax.numpy as jnp
from jax import lax
from jax.experimental import pallas as pl
from jax.experimental.pallas import tpu as pltpu
from jax.sharding import Mesh, PartitionSpec as P

HEAD_WIDTH = 128
BLOCK_TOKENS = 128
GROUP = 5
QCOLS = GROUP * HEAD_WIDTH
NY, NZ, NX = 4, 8, 4
SHARDS = NY * NZ * NX
FMAX = 16
SLOTS = 32
ITEMS = 16
LIST = 20
STEP = 4
NEG = -1e30
EXP_SCALE = 1.4426950408889634 * HEAD_WIDTH ** (-0.5)


def attend_kernel(
    meta_ref, q_ref, kv_ref, o_ref, lse_ref,
    list_ref, count_ref, acc_ref, m_ref, l_ref,
):
    y, z, x = (lax.axis_index(a) for a in ("y", "z", "x"))

    def place(item):
        pattern, target, row = item >> 3, (item >> 1) & 3, item & 1
        along_x = pattern == 0
        own = jnp.where(along_x, target == x, target == y)
        own_slot = z * 4 + jnp.where(along_x, y, x)
        return pattern, target, row, along_x, own, own_slot

    def build(item, carry):
        pattern, target, row, along_x, own, own_slot = place(item)
        base = (item >> 1) * 1024 + row * 128
        at = item * LIST
        list_ref[at] = own_slot * 2
        n = jnp.logical_and(own, row == 1).astype(jnp.int32)
        for j in range(FMAX):
            code = meta_ref[base + j]
            oy, oz, ox = code >> 6, (code >> 3) & 7, (code >> 1) & 3
            list_ref[at + n] = oz * 8 + jnp.where(along_x, oy, ox) * 2 + (code & 1)
            mine = jnp.logical_and(code >= 0, jnp.where(along_x, ox == x, oy == y))
            n = n + mine.astype(jnp.int32)
        count_ref[item] = n
        return carry

    lax.fori_loop(0, ITEMS, build, 0)

    def one_item(item, carry):
        pattern, target, row, along_x, own, own_slot = place(item)

        total = count_ref[item]
        at = item * LIST
        tokens = pl.ds(pl.multiple_of(row * BLOCK_TOKENS, BLOCK_TOKENS), BLOCK_TOKENS)
        q = q_ref.at[pattern, target, tokens]
        acc_ref[...] = jnp.zeros_like(acc_ref)
        m_ref[...] = jnp.full_like(m_ref, NEG)
        l_ref[...] = jnp.zeros_like(l_ref)

        def rows_of(kind, blocks):
            starts = [pl.multiple_of((2 * kind + (b & 1)) * BLOCK_TOKENS, BLOCK_TOKENS) for b in blocks]
            return jnp.concatenate(
                [kv_ref[pattern, b >> 1, pl.ds(i, BLOCK_TOKENS)] for b, i in zip(blocks, starts)], 0
            )

        def absorb(blocks, masked):
            parts = [slice(i * BLOCK_TOKENS, (i + 1) * BLOCK_TOKENS) for i in range(len(blocks))]
            heads = jnp.concatenate(
                [q[:, g * HEAD_WIDTH : (g + 1) * HEAD_WIDTH] for g in range(GROUP)], 0
            )
            s = lax.dot_general(
                heads, rows_of(0, blocks), (((1,), (1,)), ((), ())),
                preferred_element_type=jnp.float32,
            )
            if masked:
                query_pos = lax.broadcasted_iota(jnp.int32, s.shape, 0) & (BLOCK_TOKENS - 1)
                key_pos = lax.broadcasted_iota(jnp.int32, s.shape, 1)
                s = jnp.where(key_pos <= query_pos, s, NEG)
            m_old = m_ref[...]
            top = functools.reduce(jnp.maximum, [s[:, c] for c in parts])
            m_new = jnp.maximum(m_old, jnp.max(top, axis=1, keepdims=True))
            alpha = jnp.exp2((m_old - m_new) * EXP_SCALE)
            p = [jnp.exp2((s[:, c] - m_new) * EXP_SCALE) for c in parts]
            m_ref[...] = m_new
            gained = jnp.sum(functools.reduce(jnp.add, p), axis=1, keepdims=True)
            l_ref[...] = l_ref[...] * alpha + gained
            acc_ref[...] = acc_ref[...] * alpha + jnp.dot(
                jnp.concatenate(p, 1).astype(jnp.bfloat16), rows_of(1, blocks),
                preferred_element_type=jnp.float32,
            )

        @pl.when(own)
        def _():
            absorb([own_slot * 2 + row], True)

        def many(i, carry):
            absorb([list_ref[at + STEP * i + k] for k in range(STEP)], False)
            return carry

        lax.fori_loop(0, total // STEP, many, 0)
        done = total - total % STEP
        for k in (2, 1):

            @pl.when((total & k) != 0)
            def _(k=k, done=done):
                absorb([list_ref[at + done + i] for i in range(k)], False)

            done = done + (total & k)

        lane = lax.broadcasted_iota(jnp.int32, (BLOCK_TOKENS, BLOCK_TOKENS), 1)
        tile = jnp.zeros((BLOCK_TOKENS, BLOCK_TOKENS), jnp.float32)
        for g in range(GROUP):
            part = slice(g * HEAD_WIDTH, (g + 1) * HEAD_WIDTH)
            l = l_ref[part]
            live = l > 0
            safe = jnp.where(live, l, 1.0)
            o_ref[item, :, part] = (acc_ref[part] * (1.0 / safe)).astype(jnp.bfloat16)
            lse = jnp.where(live, m_ref[part] * EXP_SCALE + jnp.log2(safe), NEG)
            tile = jnp.where(lane == g, lse, tile)
        lse_ref[item] = tile.T[:8]
        return carry

    lax.fori_loop(0, ITEMS, one_item, 0)


def attend(meta, q, kv):
    blocks = pl.BlockSpec(memory_space=pltpu.VMEM)
    scalars = pl.BlockSpec(memory_space=pltpu.SMEM)
    state = pltpu.VMEM((QCOLS, HEAD_WIDTH), jnp.float32)
    return pl.pallas_call(
        attend_kernel,
        in_specs=[scalars, blocks, blocks],
        out_specs=[blocks, blocks],
        out_shape=[
            jax.ShapeDtypeStruct((ITEMS, BLOCK_TOKENS, QCOLS), jnp.bfloat16),
            jax.ShapeDtypeStruct((ITEMS, 8, BLOCK_TOKENS), jnp.float32),
        ],
        scratch_shapes=[
            pltpu.SMEM((ITEMS * LIST,), jnp.int32),
            pltpu.SMEM((ITEMS,), jnp.int32),
            state, state, state,
        ],
        compiler_params=pltpu.CompilerParams(vmem_limit_bytes=32 * 1024 * 1024),
    )(meta, q, kv)


def return_kernel(o_in, lse_in, out_ref, o_got, lse_got, send, recv, lse_send, lse_recv):
    at = {"x": lax.axis_index("x"), "y": lax.axis_index("y")}
    core = lax.axis_index("head")
    axes = ("x", "y")
    others = [(p, step, e) for step in (1, 3, 2, 0) for e in range(2) for p in range(2)]
    others = [v for v in others if v[1:] != (0, 0)]

    def device(p, step, e):
        a = axes[p]
        return {a: (at[a] + step) % 4, "head": (core + e) % 2}

    barrier = pltpu.get_barrier_semaphore()
    met = [v for v in others if v != (1, 0, 1)]
    for v in met:
        pl.semaphore_signal(
            barrier, inc=1, device_id=device(*v), device_id_type=pl.DeviceIdType.MESH
        )
    pl.semaphore_wait(barrier, len(met))

    def copies(p, step, e):
        a = axes[p]
        target, row = (at[a] + step) % 4, (core + e) % 2
        i = (p * 4 + step) * 2 + e
        parts = (
            (o_in.at[(p * 4 + target) * 2 + row], o_got.at[p, core, at[a]], send, recv),
            (lse_in.at[(p * 4 + target) * 2 + row], lse_got.at[p, core, at[a]], lse_send, lse_recv),
        )
        if step == 0 and e == 0:
            return [pltpu.make_async_copy(s, d, r.at[i]) for s, d, _, r in parts]
        return [
            pltpu.make_async_remote_copy(
                src_ref=s, dst_ref=d, send_sem=w.at[i], recv_sem=r.at[i],
                device_id=device(p, step, e), device_id_type=pl.DeviceIdType.MESH,
            )
            for s, d, w, r in parts
        ]

    for v in others + [(0, 0, 0), (1, 0, 0)]:
        for c in copies(*v):
            c.start()
    for p in range(2):
        for e in range(2):
            for step in range(4):
                for c in copies(p, step, e):
                    if (step, e) == (0, 0):
                        c.wait()
                    else:
                        c.wait_recv()
    for p in range(2):
        for c in range(2):
            lse = [lse_got[p, c, i] for i in range(4)]
            top = functools.reduce(jnp.maximum, lse)
            w = [jnp.exp2(v - top) for v in lse]
            inv = 1.0 / functools.reduce(jnp.add, w)
            w = [v * inv for v in w]
            rest = jnp.zeros((BLOCK_TOKENS - 32, BLOCK_TOKENS), jnp.float32)
            w = jnp.concatenate(w + [rest], 0).T
            for g in range(GROUP):
                cols = slice(g * HEAD_WIDTH, (g + 1) * HEAD_WIDTH)
                mixed = sum(
                    o_got[p, c, i, :, cols].astype(jnp.float32) * w[:, i * 8 + g : i * 8 + g + 1]
                    for i in range(4)
                )
                start = (c * 2 + p) * QCOLS + g * HEAD_WIDTH
                out_ref[:, start : start + HEAD_WIDTH] = mixed.astype(jnp.bfloat16)
    for v in others:
        for c in copies(*v):
            c.wait_send()


def send_back(o, lse):
    dma = pltpu.SemaphoreType.DMA
    any_spec = pl.BlockSpec(memory_space=pl.ANY)
    return pl.pallas_call(
        return_kernel,
        in_specs=[any_spec] * 2,
        out_specs=pl.BlockSpec(memory_space=pltpu.VMEM),
        out_shape=jax.ShapeDtypeStruct((BLOCK_TOKENS, 4 * QCOLS), jnp.bfloat16),
        scratch_shapes=[
            pltpu.VMEM((2, 2, 4, BLOCK_TOKENS, QCOLS), jnp.bfloat16),
            pltpu.VMEM((2, 2, 4, 8, BLOCK_TOKENS), jnp.float32),
            dma((16,)), dma((16,)), dma((16,)), dma((16,)),
        ],
        compiler_params=pltpu.CompilerParams(
            collective_id=1, has_side_effects=True, vmem_limit_bytes=16 * 1024 * 1024
        ),
    )(o, lse)


def copy_to(src, dst, sems, device):
    return pltpu.make_async_remote_copy(
        src_ref=src, dst_ref=dst, send_sem=sems[0], recv_sem=sems[1],
        device_id=device, device_id_type=pl.DeviceIdType.MESH,
    )


MAIN = 3 * BLOCK_TOKENS
LAST = BLOCK_TOKENS
ORDER = (
    ("last near", 0, 0), ("last near", 0, 1), ("z", 1, 0), ("near", 0, 0), ("near", 0, 1),
    ("z", 1, 1), ("z", 2, 0), ("z", 2, 1), ("q", 0, 1), ("q", 0, 0), ("last far", 0, 0),
    ("z", 3, 0), ("last far", 0, 1), ("near", 1, 0), ("z", 3, 1), ("near", 1, 1), ("near", 2, 0),
    ("last z", 1, 0), ("near", 2, 1), ("z", 4, 0), ("near", 3, 0), ("near", 3, 1),
    ("last z", 1, 1), ("near", 4, 0), ("near", 4, 1), ("z", 4, 1), ("last z", 2, 0),
    ("near", 5, 0), ("near", 5, 1), ("last z", 2, 1), ("near", 6, 0), ("near", 6, 1),
    ("last z", 3, 0), ("last z", 3, 1), ("near", 7, 0), ("last z", 4, 0), ("near", 7, 1),
    ("last z", 4, 1),
)


def gather_kernel(
    q_hbm, k_hbm, v_hbm, owners_hbm, pairs_hbm, counts_in, q_all, kv_all, meta_all,
    q_in, k_in, v_in, owners_in, pairs_in, q_own, kv_own, meta_own, in_sem, local_sem,
    z_send, z_recv, near_send, near_recv, far_send, far_recv,
    lz_send, lz_recv, ln_send, ln_recv, lf_send, lf_recv,
    q_send, q_recv, qf_send, qf_recv, t_send, t_recv,
):
    at = {a: lax.axis_index(a) for a in ("y", "z", "x")}
    size = {"y": NY, "z": NZ, "x": NX}
    ring = {a: ((at[a] + 1) % size[a], (at[a] + size[a] - 1) % size[a]) for a in at}

    barrier = pltpu.get_barrier_semaphore()
    for a in at:
        for n in ring[a]:
            pl.semaphore_signal(
                barrier, inc=1, device_id={a: n}, device_id_type=pl.DeviceIdType.MESH
            )

    loads = [
        pltpu.make_async_copy(src, dst, in_sem.at[i])
        for i, (src, dst) in enumerate(
            (
                (k_hbm, k_in), (v_hbm, v_in), (q_hbm, q_in),
                (owners_hbm, owners_in), (pairs_hbm, pairs_in),
            )
        )
    ]
    for c in loads:
        c.start()

    side = ("y", "x")
    cross = ("x", "y")

    def slot(h, place, zo):
        return zo * 4 + place

    local = []

    def keep(src, dst):
        c = pltpu.make_async_copy(src, dst, local_sem.at[len(local)])
        c.start()
        local.append(c)

    sends = []

    def part(d):
        return pl.ds(d * (MAIN // 2), MAIN // 2)

    def z_copy(d, s, h):
        back = at["z"] - (s - 1) if d == 0 else at["z"] + (s - 1)
        rows = part(d) if s == 4 else pl.ds(0, MAIN)
        ref = kv_all.at[h, slot(h, at[side[h]], (back + NZ) % NZ), rows]
        i = (d * 4 + s - 1) * 2 + h
        src = kv_own.at[h, rows] if s == 1 else ref
        return copy_to(src, ref, (z_send.at[i], z_recv.at[i]), {"z": ring["z"][d]})

    def near_copy(h, i, zo, d):
        rows = pl.ds(0, MAIN)
        ref = kv_all.at[h, slot(h, at[side[h]], zo), rows]
        n = (h * 8 + i) * 2 + d
        src = kv_own.at[h, rows] if i == 0 else ref
        return copy_to(src, ref, (near_send.at[n], near_recv.at[n]), {side[h]: ring[side[h]][d]})

    def far_copy(h, i, zo, d):
        a = side[h]
        ref = kv_all.at[h, slot(h, ring[a][1 - d], zo), part(d)]
        n = (h * 8 + i) * 2 + d
        return copy_to(ref, ref, (far_send.at[n], far_recv.at[n]), {a: ring[a][d]})

    def last_near(h, d):
        a = side[h]
        rows = pl.ds(MAIN, LAST)
        ref = kv_all.at[h, slot(h, at[a], at["z"]), rows]
        n = h * 2 + d
        return copy_to(kv_own.at[h, rows], ref, (ln_send.at[n], ln_recv.at[n]), {a: ring[a][d]})

    def last_far(h, d):
        a = side[h]
        rows = pl.ds(MAIN + d * (LAST // 2), LAST // 2)
        ref = kv_all.at[h, slot(h, ring[a][1 - d], at["z"]), rows]
        n = h * 2 + d
        return copy_to(ref, ref, (lf_send.at[n], lf_recv.at[n]), {a: ring[a][d]})

    def last_z(d, s, h):
        back = at["z"] - (s - 1) if d == 0 else at["z"] + (s - 1)
        first = ((back + NZ) % NZ) * 4
        places = pl.ds(first + 2 * d, 2) if s == 4 else pl.ds(first, 4)
        ref = kv_all.at[h, places, pl.ds(MAIN, LAST)]
        i = (d * 4 + s - 1) * 2 + h
        return copy_to(ref, ref, (lz_send.at[i], lz_recv.at[i]), {"z": ring["z"][d]})

    def q_copy(h, d):
        a = cross[h]
        ref = q_all.at[h, at[a]]
        return copy_to(
            q_own.at[h], ref, (q_send.at[h * 2 + d], q_recv.at[h * 2 + d]), {a: ring[a][d]}
        )

    def qf_copy(h, d):
        a = cross[h]
        ref = q_all.at[h, ring[a][1 - d], pl.ds(d * BLOCK_TOKENS, BLOCK_TOKENS)]
        return copy_to(
            ref, ref, (qf_send.at[h * 2 + d], qf_recv.at[h * 2 + d]), {a: ring[a][d]}
        )

    def t_copy(h, d, relay):
        a = cross[h]
        ref = meta_all.at[h, ring[a][1 - d] if relay else at[a]]
        i = (h * 2 + d) * 2 + relay
        return copy_to(
            ref if relay else meta_own, ref, (t_send.at[i], t_recv.at[i]), {a: ring[a][d]}
        )

    def start(c):
        c.start()
        sends.append(c)

    both = [(h, d) for h in range(2) for d in range(2)]
    zs = [at["z"]]
    for s in range(1, 5):
        zs.append((at["z"] - s + NZ) % NZ)
        zs.append((at["z"] + s) % NZ)
    zs = zs[:8]

    for i, ref in enumerate((k_in, v_in)):
        loads[i].wait()
        for h in range(2):
            kv_own[h, i * 256 : i * 256 + 256] = ref[:, h * HEAD_WIDTH : (h + 1) * HEAD_WIDTH]
    pl.semaphore_wait(barrier, 6)
    for h, d in both:
        start(z_copy(d, 1, h))
    for h, d in both:
        start(last_near(h, d))
    for h, d in both:
        start(near_copy(h, 0, zs[0], d))
    for h in range(2):
        keep(kv_own.at[h], kv_all.at[h, slot(h, at[side[h]], at["z"])])
    loads[2].wait()
    for h in range(2):
        q_own[h] = q_in[:, h * QCOLS : (h + 1) * QCOLS]
    for h, d in both:
        start(q_copy(h, d))

    for c in loads[3:]:
        c.wait()
    meta_own[...] = jnp.zeros_like(meta_own)
    meta_own[0:2, 0:FMAX] = owners_in[...]
    owners = meta_own[...]
    shard = (at["y"] * NZ + at["z"]) * NX + at["x"]
    listed = pairs_in[pl.ds(jnp.minimum(shard, SHARDS - 1 - shard), 1), :]
    half = jnp.take_along_axis(jnp.broadcast_to(listed, (8, 128)), owners, axis=1) & 1
    row = lax.broadcasted_iota(jnp.int32, (8, 128), 0)
    lane = lax.broadcasted_iota(jnp.int32, (8, 128), 1)
    count = jnp.where(row == 0, counts_in[0], jnp.where(row == 1, counts_in[1], 0))
    meta_own[...] = jnp.where(lane < count, owners * 2 + half, -1)
    for h, d in both:
        start(t_copy(h, d, 0))
    for h in range(2):
        keep(q_own.at[h], q_all.at[h, at[cross[h]]])
        keep(meta_own, meta_all.at[h, at[cross[h]]])

    def arrived(kind, i, h):
        for d in range(2):
            if kind == "z":
                z_copy(d, i, h).wait_recv()
                if i < 4:
                    start(z_copy(d, i + 1, h))
                    for e in range(2):
                        start(near_copy(h, 2 * i - 1 + d, zs[2 * i - 1 + d], e))
                elif d == 1:
                    for e in range(2):
                        start(near_copy(h, 7, zs[7], e))
            elif kind == "near":
                near_copy(h, i, zs[i], d).wait_recv()
                start(far_copy(h, i, zs[i], d))
            elif kind == "q":
                q_copy(h, d).wait_recv()
                start(qf_copy(h, d))
            elif kind == "last near":
                last_near(h, d).wait_recv()
                start(last_far(h, d))
            elif kind == "last far":
                last_far(h, d).wait_recv()
                if d == 1:
                    local[h].wait()
                    for e in range(2):
                        start(last_z(e, 1, h))
            else:
                last_z(d, i, h).wait_recv()
                if i < 4:
                    start(last_z(d, i + 1, h))

    for event in ORDER:
        arrived(*event)
    for h in range(2):
        for d in range(2):
            t_copy(h, d, 0).wait_recv()
        start(t_copy(h, 0, 1))
    for h, d in both:
        qf_copy(h, d).wait_recv()
        for i in range(8):
            far_copy(h, i, zs[i], d).wait_recv()
    for h in range(2):
        t_copy(h, 0, 1).wait_recv()
    for c in sends:
        c.wait_send()
    for c in local[2:]:
        c.wait()


def gather_all(q, k, v, owners, counts, pairs):
    dma = pltpu.SemaphoreType.DMA
    any_spec = pl.BlockSpec(memory_space=pl.ANY)
    arrays = [pltpu.with_memory_space_constraint(a, pltpu.HBM) for a in (q, k, v, owners, pairs)]
    return pl.pallas_call(
        gather_kernel,
        in_specs=[any_spec] * 5 + [pl.BlockSpec(memory_space=pltpu.SMEM)],
        out_specs=[any_spec] * 3,
        out_shape=[
            jax.ShapeDtypeStruct((2, 4, 2 * BLOCK_TOKENS, QCOLS), jnp.bfloat16),
            jax.ShapeDtypeStruct((2, SLOTS, MAIN + LAST, HEAD_WIDTH), jnp.bfloat16),
            jax.ShapeDtypeStruct((2, 4, 8, 128), jnp.int32),
        ],
        scratch_shapes=[pltpu.VMEM(a.shape, a.dtype) for a in (q, k, v, owners, pairs)]
        + [
            pltpu.VMEM((2, 2 * BLOCK_TOKENS, QCOLS), jnp.bfloat16),
            pltpu.VMEM((2, MAIN + LAST, HEAD_WIDTH), jnp.bfloat16),
            pltpu.VMEM((8, 128), jnp.int32),
        ]
        + [dma((n,)) for n in (5, 6, 16, 16, 32, 32, 32, 32, 16, 16, 4, 4, 4, 4, 4, 4, 4, 4, 8, 8)],
        compiler_params=pltpu.CompilerParams(
            collective_id=0, has_side_effects=True, vmem_limit_bytes=16 * 1024 * 1024
        ),
    )(*arrays, counts)


def on_device(queries, keys, values, far_owners, far_counts, pair_blocks):
    q, kv, meta = gather_all(queries, keys, values, far_owners, far_counts, pair_blocks)
    o, lse = attend(meta.reshape(-1), q, kv)
    return send_back(o, lse)


def solution(mesh):
    grid = Mesh(mesh.devices.reshape(NY, NZ, NX, 2), ("y", "z", "x", "head"))
    ctx = ("y", "z", "x")
    placed = (P(ctx, "head"), P(ctx, "head"), P(ctx, "head"), P(ctx, None), P(ctx), P())
    return jax.shard_map(
        on_device,
        mesh=grid,
        in_specs=placed,
        out_specs=P((*ctx, "head"), None),
        check_vma=False,
    )
```

```python
import functools

import jax
import jax.numpy as jnp
from jax import lax
from jax.experimental import pallas as pl
from jax.experimental.pallas import tpu as pltpu
from jax.sharding import Mesh, PartitionSpec as P

HEAD_WIDTH = 128
BLOCK_TOKENS = 128
GROUP = 5
QCOLS = GROUP * HEAD_WIDTH
NY, NZ, NX = 4, 8, 4
SHARDS = NY * NZ * NX
FMAX = 16
SLOTS = 32
ITEMS = 16
STEP = 2
UNROLL = 4
NEG = -1e30
EXP_SCALE = 1.4426950408889634 * HEAD_WIDTH ** (-0.5)


def attend_kernel(
    codes_ref, q_in, kv_in, o_ref, stat_ref,
    count_ref, chunk_ref, q_ref, kv_ref, acc_ref, m_ref, l_ref, sem,
):
    y, z, x = (lax.axis_index(a) for a in ("y", "z", "x"))

    def loads(pattern):
        return [
            pltpu.make_async_copy(src.at[pattern], dst.at[pattern], sem.at[i, pattern])
            for i, (src, dst) in enumerate(((q_in, q_ref), (kv_in, kv_ref)))
        ]

    for c in loads(0) + loads(1):
        c.start()

    def base_of(pattern, item):
        return (item >> 1) * 1024 + (item & 1) * 128 + (x if pattern == 0 else y) * FMAX

    def build(pattern, item, chunks):
        n = codes_ref[base_of(pattern, item) + 2 * 128]
        count_ref[item] = n

        def note(i, chunks):
            chunk_ref[chunks] = item * 16 + i
            return chunks + 1

        return lax.fori_loop(0, (n + STEP - 1) // STEP, note, chunks)

    middle = lax.fori_loop(0, 8, functools.partial(build, 0), jnp.int32(0))
    end = lax.fori_loop(8, 16, functools.partial(build, 1), middle)

    def score(pattern, item, blocks):
        tokens = pl.ds(pl.multiple_of((item & 1) * BLOCK_TOKENS, BLOCK_TOKENS), BLOCK_TOKENS)
        q = q_ref.at[pattern, (item >> 1) & 3, tokens]
        heads = [q[:, g * HEAD_WIDTH : (g + 1) * HEAD_WIDTH] for g in range(GROUP)]
        return lax.dot_general(
            jnp.concatenate(heads, 0), rows_of(pattern, 0, blocks), (((1,), (1,)), ((), ())),
            preferred_element_type=jnp.float32,
        )

    def rows_of(pattern, kind, blocks):
        starts = [
            pl.multiple_of((2 * kind + (b & 1)) * BLOCK_TOKENS, BLOCK_TOKENS) for b in blocks
        ]
        return jnp.concatenate(
            [kv_ref[pattern, b >> 1, pl.ds(i, BLOCK_TOKENS)] for b, i in zip(blocks, starts)], 0
        )

    def split(s):
        return [
            s[:, i : i + BLOCK_TOKENS] for i in range(0, s.shape[1], BLOCK_TOKENS)
        ]

    def top_of(parts):
        return jnp.max(functools.reduce(jnp.maximum, parts), axis=1, keepdims=True)

    def mix(pattern, blocks, p):
        return jnp.dot(
            jnp.concatenate(p, 1).astype(jnp.bfloat16), rows_of(pattern, 1, blocks),
            preferred_element_type=jnp.float32,
        )

    def own_blocks(pattern, row):
        place = y if pattern == 0 else x
        item = (pattern * 4 + (x if pattern == 0 else y)) * 2 + row
        blocks = [(z * 4 + place) * 2 + i for i in range(row + 1)]
        parts = split(score(pattern, item, blocks))
        query_pos = lax.broadcasted_iota(jnp.int32, parts[0].shape, 0) & (BLOCK_TOKENS - 1)
        key_pos = lax.broadcasted_iota(jnp.int32, parts[0].shape, 1)
        parts[-1] = jnp.where(key_pos <= query_pos, parts[-1], NEG)
        m = top_of(parts)
        p = [jnp.exp2((v - m) * EXP_SCALE) for v in parts]
        m_ref[item] = jnp.broadcast_to(m, (QCOLS, HEAD_WIDTH))
        l_ref[item] = functools.reduce(jnp.add, p)
        acc_ref[item] = mix(pattern, blocks, p)

    def fetch(pattern, c):
        code = chunk_ref[c]
        item, i = code >> 4, code & 15
        at = base_of(pattern, item) + i * STEP
        blocks = [codes_ref[at + k] for k in range(STEP)]
        own = ((item >> 1) & 3) == (x if pattern == 0 else y)
        fresh = jnp.logical_and(i == 0, jnp.logical_not(own))
        return item, blocks, count_ref[item] - i * STEP, fresh

    def absorb(pattern, s, item, blocks, left, fresh):
        parts = split(s)
        m_old = jnp.where(fresh, NEG, m_ref[item])
        m_new = jnp.maximum(m_old, top_of(parts))
        alpha = jnp.exp2((m_old - m_new) * EXP_SCALE)
        off = m_new * EXP_SCALE
        p = [
            jnp.exp2(v * EXP_SCALE - (off if i == 0 else off + jnp.where(left > i, 0.0, -NEG)))
            for i, v in enumerate(parts)
        ]
        m_ref[item] = m_new
        l_ref[item] = jnp.where(fresh, 0.0, l_ref[item]) * alpha + functools.reduce(jnp.add, p)
        acc_ref[item] = jnp.where(fresh, 0.0, acc_ref[item]) * alpha + mix(pattern, blocks, p)

    for pattern, begin, stop in ((0, 0, middle), (1, middle, end)):
        for c in loads(pattern):
            c.wait()
        for row in range(2):
            own_blocks(pattern, row)

        def several(j, carry, pattern=pattern, begin=begin):
            got = [fetch(pattern, begin + j * UNROLL + u) for u in range(UNROLL)]
            scores = [score(pattern, g[0], g[1]) for g in got]
            for g, s in zip(got, scores):
                absorb(pattern, s, *g)
            return carry

        def single(c, carry, pattern=pattern):
            g = fetch(pattern, c)
            absorb(pattern, score(pattern, g[0], g[1]), *g)
            return carry

        whole = (stop - begin) // UNROLL
        lax.fori_loop(0, whole, several, 0)
        lax.fori_loop(begin + whole * UNROLL, stop, single, 0)

    lane = lax.broadcasted_iota(jnp.int32, (BLOCK_TOKENS, BLOCK_TOKENS), 1)

    def close(item, carry):
        own = ((item >> 1) & 3) == jnp.where(item < 8, x, y)
        read = jnp.logical_or(own, count_ref[item] > 0)

        @pl.when(read)
        def _():
            tops = jnp.zeros((BLOCK_TOKENS, BLOCK_TOKENS), jnp.float32)
            sums = jnp.zeros((BLOCK_TOKENS, BLOCK_TOKENS), jnp.float32)
            for g in range(GROUP):
                part = slice(g * HEAD_WIDTH, (g + 1) * HEAD_WIDTH)
                o_ref[item, :, part] = acc_ref[item, part].astype(jnp.bfloat16)
                tops = jnp.where(lane == g, m_ref[item, part], tops)
                sums = jnp.where(
                    lane == g, jnp.sum(l_ref[item, part], axis=1, keepdims=True), sums
                )
            stat_ref[item, 0:8] = tops.T[:8] * EXP_SCALE
            stat_ref[item, 8:16] = sums.T[:8]

        @pl.when(jnp.logical_not(read))
        def _():
            o_ref[item] = jnp.zeros((BLOCK_TOKENS, QCOLS), jnp.bfloat16)
            stat_ref[item, 0:8] = jnp.full((8, BLOCK_TOKENS), NEG, jnp.float32)
            stat_ref[item, 8:16] = jnp.zeros((8, BLOCK_TOKENS), jnp.float32)

        return carry

    lax.fori_loop(0, ITEMS, close, 0)


def attend(codes, q, kv):
    any_spec = pl.BlockSpec(memory_space=pl.ANY)
    blocks = pl.BlockSpec(memory_space=pltpu.VMEM)
    state = pltpu.VMEM((ITEMS, QCOLS, HEAD_WIDTH), jnp.float32)
    return pl.pallas_call(
        attend_kernel,
        in_specs=[pl.BlockSpec(memory_space=pltpu.SMEM), any_spec, any_spec],
        out_specs=[blocks, blocks],
        out_shape=[
            jax.ShapeDtypeStruct((ITEMS, BLOCK_TOKENS, QCOLS), jnp.bfloat16),
            jax.ShapeDtypeStruct((ITEMS, 16, BLOCK_TOKENS), jnp.float32),
        ],
        scratch_shapes=[
            pltpu.SMEM((ITEMS,), jnp.int32),
            pltpu.SMEM((ITEMS * FMAX,), jnp.int32),
            pltpu.VMEM(q.shape, q.dtype),
            pltpu.VMEM(kv.shape, kv.dtype),
            state, state, state,
            pltpu.SemaphoreType.DMA((2, 2)),
        ],
        compiler_params=pltpu.CompilerParams(vmem_limit_bytes=40 * 1024 * 1024),
    )(codes, q, kv)


def return_kernel(o_in, stat_in, out_ref, o_got, stat_got, send, recv, stat_send, stat_recv):
    at = {"x": lax.axis_index("x"), "y": lax.axis_index("y")}
    core = lax.axis_index("head")
    axes = ("x", "y")
    others = [(p, step, e) for step in (1, 3, 2, 0) for e in range(2) for p in range(2)]
    others = [v for v in others if v[1:] != (0, 0)]

    def device(p, step, e):
        a = axes[p]
        return {a: (at[a] + step) % 4, "head": (core + e) % 2}

    barrier = pltpu.get_barrier_semaphore()
    met = [v for v in others if v != (1, 0, 1)]
    for v in met:
        pl.semaphore_signal(
            barrier, inc=1, device_id=device(*v), device_id_type=pl.DeviceIdType.MESH
        )
    pl.semaphore_wait(barrier, len(met))

    def copies(p, step, e):
        a = axes[p]
        target, row = (at[a] + step) % 4, (core + e) % 2
        i = (p * 4 + step) * 2 + e
        parts = (
            (o_in.at[(p * 4 + target) * 2 + row], o_got.at[p, core, at[a]], send, recv),
            (stat_in.at[(p * 4 + target) * 2 + row], stat_got.at[p, core, at[a]], stat_send, stat_recv),
        )
        if step == 0 and e == 0:
            return [pltpu.make_async_copy(s, d, r.at[i]) for s, d, _, r in parts]
        return [
            pltpu.make_async_remote_copy(
                src_ref=s, dst_ref=d, send_sem=w.at[i], recv_sem=r.at[i],
                device_id=device(p, step, e), device_id_type=pl.DeviceIdType.MESH,
            )
            for s, d, w, r in parts
        ]

    for v in others + [(0, 0, 0), (1, 0, 0)]:
        for c in copies(*v):
            c.start()
    for p in range(2):
        for e in range(2):
            for step in range(4):
                for c in copies(p, step, e):
                    if (step, e) == (0, 0):
                        c.wait()
                    else:
                        c.wait_recv()
    for p in range(2):
        for c in range(2):
            stats = [stat_got[p, c, i] for i in range(4)]
            top = functools.reduce(jnp.maximum, [v[:8] for v in stats])
            w = [jnp.exp2(v[:8] - top) for v in stats]
            total = functools.reduce(jnp.add, [v[8:] * f for v, f in zip(stats, w)])
            inv = 1.0 / jnp.where(total > 0, total, 1.0)
            w = [v * inv for v in w]
            rest = jnp.zeros((BLOCK_TOKENS - 32, BLOCK_TOKENS), jnp.float32)
            w = jnp.concatenate(w + [rest], 0).T
            for g in range(GROUP):
                cols = slice(g * HEAD_WIDTH, (g + 1) * HEAD_WIDTH)
                mixed = sum(
                    o_got[p, c, i, :, cols].astype(jnp.float32) * w[:, i * 8 + g : i * 8 + g + 1]
                    for i in range(4)
                )
                start = (c * 2 + p) * QCOLS + g * HEAD_WIDTH
                out_ref[:, start : start + HEAD_WIDTH] = mixed.astype(jnp.bfloat16)
    for v in others:
        for c in copies(*v):
            c.wait_send()


def send_back(o, stats):
    dma = pltpu.SemaphoreType.DMA
    any_spec = pl.BlockSpec(memory_space=pl.ANY)
    return pl.pallas_call(
        return_kernel,
        in_specs=[any_spec] * 2,
        out_specs=pl.BlockSpec(memory_space=pltpu.VMEM),
        out_shape=jax.ShapeDtypeStruct((BLOCK_TOKENS, 4 * QCOLS), jnp.bfloat16),
        scratch_shapes=[
            pltpu.VMEM((2, 2, 4, BLOCK_TOKENS, QCOLS), jnp.bfloat16),
            pltpu.VMEM((2, 2, 4, 16, BLOCK_TOKENS), jnp.float32),
            dma((16,)), dma((16,)), dma((16,)), dma((16,)),
        ],
        compiler_params=pltpu.CompilerParams(
            collective_id=1, has_side_effects=True, vmem_limit_bytes=16 * 1024 * 1024
        ),
    )(o, stats)


def copy_to(src, dst, sems, device):
    return pltpu.make_async_remote_copy(
        src_ref=src, dst_ref=dst, send_sem=sems[0], recv_sem=sems[1],
        device_id=device, device_id_type=pl.DeviceIdType.MESH,
    )


MAIN = 3 * BLOCK_TOKENS
LAST = BLOCK_TOKENS
ORDER = (
    ("last near", 0, 0), ("last near", 0, 1), ("z", 1, 0), ("near", 0, 0), ("near", 0, 1),
    ("z", 1, 1), ("z", 2, 0), ("z", 2, 1), ("q", 0, 1), ("q", 0, 0), ("last far", 0, 0),
    ("z", 3, 0), ("last far", 0, 1), ("near", 1, 0), ("z", 3, 1), ("near", 1, 1), ("near", 2, 0),
    ("last z", 1, 0), ("near", 2, 1), ("z", 4, 0), ("near", 3, 0), ("near", 3, 1),
    ("last z", 1, 1), ("near", 4, 0), ("near", 4, 1), ("z", 4, 1), ("last z", 2, 0),
    ("near", 5, 0), ("near", 5, 1), ("last z", 2, 1), ("near", 6, 0), ("near", 6, 1),
    ("last z", 3, 0), ("last z", 3, 1), ("near", 7, 0), ("last z", 4, 0), ("near", 7, 1),
    ("last z", 4, 1),
)


def gather_kernel(
    q_hbm, k_hbm, v_hbm, owners_hbm, pairs_hbm, counts_in, q_all, kv_all, meta_all,
    q_in, k_in, v_in, owners_in, pairs_in, q_own, kv_own, meta_own, in_sem, local_sem,
    z_send, z_recv, near_send, near_recv, far_send, far_recv,
    lz_send, lz_recv, ln_send, ln_recv, lf_send, lf_recv,
    q_send, q_recv, qf_send, qf_recv, t_send, t_recv,
):
    at = {a: lax.axis_index(a) for a in ("y", "z", "x")}
    size = {"y": NY, "z": NZ, "x": NX}
    ring = {a: ((at[a] + 1) % size[a], (at[a] + size[a] - 1) % size[a]) for a in at}

    barrier = pltpu.get_barrier_semaphore()
    for a in at:
        for n in ring[a]:
            pl.semaphore_signal(
                barrier, inc=1, device_id={a: n}, device_id_type=pl.DeviceIdType.MESH
            )

    loads = [
        pltpu.make_async_copy(src, dst, in_sem.at[i])
        for i, (src, dst) in enumerate(
            (
                (k_hbm, k_in), (v_hbm, v_in), (q_hbm, q_in),
                (owners_hbm, owners_in), (pairs_hbm, pairs_in),
            )
        )
    ]
    for c in loads:
        c.start()

    side = ("y", "x")
    cross = ("x", "y")

    def slot(h, place, zo):
        return zo * 4 + place

    local = []

    def keep(src, dst):
        c = pltpu.make_async_copy(src, dst, local_sem.at[len(local)])
        c.start()
        local.append(c)

    sends = []

    def part(d):
        return pl.ds(d * (MAIN // 2), MAIN // 2)

    def z_copy(d, s, h):
        back = at["z"] - (s - 1) if d == 0 else at["z"] + (s - 1)
        rows = part(d) if s == 4 else pl.ds(0, MAIN)
        ref = kv_all.at[h, slot(h, at[side[h]], (back + NZ) % NZ), rows]
        i = (d * 4 + s - 1) * 2 + h
        src = kv_own.at[h, rows] if s == 1 else ref
        return copy_to(src, ref, (z_send.at[i], z_recv.at[i]), {"z": ring["z"][d]})

    def near_copy(h, i, zo, d):
        rows = pl.ds(0, MAIN)
        ref = kv_all.at[h, slot(h, at[side[h]], zo), rows]
        n = (h * 8 + i) * 2 + d
        src = kv_own.at[h, rows] if i == 0 else ref
        return copy_to(src, ref, (near_send.at[n], near_recv.at[n]), {side[h]: ring[side[h]][d]})

    def far_copy(h, i, zo, d):
        a = side[h]
        ref = kv_all.at[h, slot(h, ring[a][1 - d], zo), part(d)]
        n = (h * 8 + i) * 2 + d
        return copy_to(ref, ref, (far_send.at[n], far_recv.at[n]), {a: ring[a][d]})

    def last_near(h, d):
        a = side[h]
        rows = pl.ds(MAIN, LAST)
        ref = kv_all.at[h, slot(h, at[a], at["z"]), rows]
        n = h * 2 + d
        return copy_to(kv_own.at[h, rows], ref, (ln_send.at[n], ln_recv.at[n]), {a: ring[a][d]})

    def last_far(h, d):
        a = side[h]
        rows = pl.ds(MAIN + d * (LAST // 2), LAST // 2)
        ref = kv_all.at[h, slot(h, ring[a][1 - d], at["z"]), rows]
        n = h * 2 + d
        return copy_to(ref, ref, (lf_send.at[n], lf_recv.at[n]), {a: ring[a][d]})

    def last_z(d, s, h):
        back = at["z"] - (s - 1) if d == 0 else at["z"] + (s - 1)
        first = ((back + NZ) % NZ) * 4
        places = pl.ds(first + 2 * d, 2) if s == 4 else pl.ds(first, 4)
        ref = kv_all.at[h, places, pl.ds(MAIN, LAST)]
        i = (d * 4 + s - 1) * 2 + h
        return copy_to(ref, ref, (lz_send.at[i], lz_recv.at[i]), {"z": ring["z"][d]})

    def q_copy(h, d):
        a = cross[h]
        ref = q_all.at[h, at[a]]
        return copy_to(
            q_own.at[h], ref, (q_send.at[h * 2 + d], q_recv.at[h * 2 + d]), {a: ring[a][d]}
        )

    def qf_copy(h, d):
        a = cross[h]
        ref = q_all.at[h, ring[a][1 - d], pl.ds(d * BLOCK_TOKENS, BLOCK_TOKENS)]
        return copy_to(
            ref, ref, (qf_send.at[h * 2 + d], qf_recv.at[h * 2 + d]), {a: ring[a][d]}
        )

    def t_copy(h, d, relay):
        a = cross[h]
        ref = meta_all.at[h, ring[a][1 - d] if relay else at[a]]
        i = (h * 2 + d) * 2 + relay
        return copy_to(
            ref if relay else meta_own.at[h], ref, (t_send.at[i], t_recv.at[i]), {a: ring[a][d]}
        )

    def start(c):
        c.start()
        sends.append(c)

    both = [(h, d) for h in range(2) for d in range(2)]
    zs = [at["z"]]
    for s in range(1, 5):
        zs.append((at["z"] - s + NZ) % NZ)
        zs.append((at["z"] + s) % NZ)
    zs = zs[:8]

    for i, ref in enumerate((k_in, v_in)):
        loads[i].wait()
        for h in range(2):
            kv_own[h, i * 256 : i * 256 + 256] = ref[:, h * HEAD_WIDTH : (h + 1) * HEAD_WIDTH]
    pl.semaphore_wait(barrier, 6)
    for h, d in both:
        start(z_copy(d, 1, h))
    for h, d in both:
        start(last_near(h, d))
    for h, d in both:
        start(near_copy(h, 0, zs[0], d))
    for h in range(2):
        keep(kv_own.at[h], kv_all.at[h, slot(h, at[side[h]], at["z"])])
    loads[2].wait()
    for h in range(2):
        q_own[h] = q_in[:, h * QCOLS : (h + 1) * QCOLS]
    for h, d in both:
        start(q_copy(h, d))

    for c in loads[3:]:
        c.wait()
    meta_own[...] = jnp.zeros_like(meta_own)
    meta_own[0, 0:2, 0:FMAX] = owners_in[...]
    owners = meta_own[0]
    shard = (at["y"] * NZ + at["z"]) * NX + at["x"]
    listed = pairs_in[pl.ds(jnp.minimum(shard, SHARDS - 1 - shard), 1), :]
    half = jnp.take_along_axis(jnp.broadcast_to(listed, (8, 128)), owners, axis=1) & 1
    row = lax.broadcasted_iota(jnp.int32, (8, 128), 0)
    lane = lax.broadcasted_iota(jnp.int32, (8, 128), 1)
    count = jnp.where(row == 0, counts_in[0], jnp.where(row == 1, counts_in[1], 0))
    place, rest = lane >> 4, lane & (FMAX - 1)
    lists = [jnp.zeros((8, 128), jnp.int32)] * 2
    found = [jnp.zeros((8, 128), jnp.int32)] * 2
    for j in range(FMAX):
        owner, which, live = (
            jnp.sum(jnp.where(lane == j, v, 0), axis=1, keepdims=True)
            for v in (owners, half, (lane < count).astype(jnp.int32))
        )
        oy, oz, ox = owner >> 5, (owner >> 2) & 7, owner & 3
        for h, (holder, spot) in enumerate(((ox, oy), (oy, ox))):
            hit = jnp.logical_and(holder == place, live > 0)
            put = jnp.logical_and(hit, jnp.logical_or(found[h] == 0, found[h] == rest))
            lists[h] = jnp.where(put, oz * 8 + spot * 2 + which, lists[h])
            found[h] = found[h] + hit.astype(jnp.int32)
    for h in range(2):
        meta_own[h, 0:2] = lists[h][0:2]
        meta_own[h, 2:4] = found[h][0:2]
    for h, d in both:
        start(t_copy(h, d, 0))
    for h in range(2):
        keep(q_own.at[h], q_all.at[h, at[cross[h]]])
        keep(meta_own.at[h], meta_all.at[h, at[cross[h]]])

    def arrived(kind, i, h):
        for d in range(2):
            if kind == "z":
                z_copy(d, i, h).wait_recv()
                if i < 4:
                    start(z_copy(d, i + 1, h))
                    for e in range(2):
                        start(near_copy(h, 2 * i - 1 + d, zs[2 * i - 1 + d], e))
                elif d == 1:
                    for e in range(2):
                        start(near_copy(h, 7, zs[7], e))
            elif kind == "near":
                near_copy(h, i, zs[i], d).wait_recv()
                start(far_copy(h, i, zs[i], d))
            elif kind == "q":
                q_copy(h, d).wait_recv()
                start(qf_copy(h, d))
            elif kind == "last near":
                last_near(h, d).wait_recv()
                start(last_far(h, d))
            elif kind == "last far":
                last_far(h, d).wait_recv()
                if d == 1:
                    local[h].wait()
                    for e in range(2):
                        start(last_z(e, 1, h))
            else:
                last_z(d, i, h).wait_recv()
                if i < 4:
                    start(last_z(d, i + 1, h))

    for event in ORDER:
        arrived(*event)
    for h in range(2):
        for d in range(2):
            t_copy(h, d, 0).wait_recv()
        start(t_copy(h, 0, 1))
    for h, d in both:
        qf_copy(h, d).wait_recv()
        for i in range(8):
            far_copy(h, i, zs[i], d).wait_recv()
    for h in range(2):
        t_copy(h, 0, 1).wait_recv()
    for c in sends:
        c.wait_send()
    for c in local[2:]:
        c.wait()


def gather_all(q, k, v, owners, counts, pairs):
    dma = pltpu.SemaphoreType.DMA
    any_spec = pl.BlockSpec(memory_space=pl.ANY)
    arrays = [pltpu.with_memory_space_constraint(a, pltpu.HBM) for a in (q, k, v, owners, pairs)]
    return pl.pallas_call(
        gather_kernel,
        in_specs=[any_spec] * 5 + [pl.BlockSpec(memory_space=pltpu.SMEM)],
        out_specs=[any_spec] * 3,
        out_shape=[
            jax.ShapeDtypeStruct((2, 4, 2 * BLOCK_TOKENS, QCOLS), jnp.bfloat16),
            jax.ShapeDtypeStruct((2, SLOTS, MAIN + LAST, HEAD_WIDTH), jnp.bfloat16),
            jax.ShapeDtypeStruct((2, 4, 8, 128), jnp.int32),
        ],
        scratch_shapes=[pltpu.VMEM(a.shape, a.dtype) for a in (q, k, v, owners, pairs)]
        + [
            pltpu.VMEM((2, 2 * BLOCK_TOKENS, QCOLS), jnp.bfloat16),
            pltpu.VMEM((2, MAIN + LAST, HEAD_WIDTH), jnp.bfloat16),
            pltpu.VMEM((2, 8, 128), jnp.int32),
        ]
        + [dma((n,)) for n in (5, 6, 16, 16, 32, 32, 32, 32, 16, 16, 4, 4, 4, 4, 4, 4, 4, 4, 8, 8)],
        compiler_params=pltpu.CompilerParams(
            collective_id=0, has_side_effects=True, vmem_limit_bytes=16 * 1024 * 1024
        ),
    )(*arrays, counts)


def on_device(queries, keys, values, far_owners, far_counts, pair_blocks):
    q, kv, codes = gather_all(queries, keys, values, far_owners, far_counts, pair_blocks)
    o, stats = attend(codes.reshape(-1), q, kv)
    return send_back(o, stats)


def solution(mesh):
    grid = Mesh(mesh.devices.reshape(NY, NZ, NX, 2), ("y", "z", "x", "head"))
    ctx = ("y", "z", "x")
    placed = (P(ctx, "head"), P(ctx, "head"), P(ctx, "head"), P(ctx, None), P(ctx), P())
    return jax.shard_map(
        on_device,
        mesh=grid,
        in_specs=placed,
        out_specs=P((*ctx, "head"), None),
        check_vma=False,
    )
```

```python
import functools

import jax
import jax.numpy as jnp
from jax import lax
from jax.experimental import pallas as pl
from jax.experimental.pallas import tpu as pltpu
from jax.sharding import Mesh, PartitionSpec as P

HEAD_WIDTH = 128
BLOCK_TOKENS = 128
GROUP = 5
QCOLS = GROUP * HEAD_WIDTH
NY, NZ, NX = 4, 8, 4
SHARDS = NY * NZ * NX
FMAX = 16
SLOTS = 32
ITEMS = 16
STEP = 2
UNROLL = 4
NEG = -1e30
EXP_SCALE = 1.4426950408889634 * HEAD_WIDTH ** (-0.5)


def attend_kernel(
    codes_ref, q_in, kv_in, o_ref, stat_ref,
    count_ref, chunk_ref, q_ref, kv_ref, acc_ref, m_ref, l_ref, sem,
):
    y, z, x = (lax.axis_index(a) for a in ("y", "z", "x"))

    def loads(pattern):
        return [
            pltpu.make_async_copy(src.at[pattern], dst.at[pattern], sem.at[i, pattern])
            for i, (src, dst) in enumerate(((q_in, q_ref), (kv_in, kv_ref)))
        ]

    for c in loads(0) + loads(1):
        c.start()

    def base_of(pattern, item):
        return (item >> 1) * 1024 + (item & 1) * 128 + (x if pattern == 0 else y) * FMAX

    def build(pattern, item, chunks):
        n = codes_ref[base_of(pattern, item) + 2 * 128]
        count_ref[item] = n

        def note(i, chunks):
            chunk_ref[chunks] = item * 16 + i
            return chunks + 1

        return lax.fori_loop(0, (n + STEP - 1) // STEP, note, chunks)

    middle = lax.fori_loop(0, 8, functools.partial(build, 0), jnp.int32(0))
    end = lax.fori_loop(8, 16, functools.partial(build, 1), middle)

    def score(pattern, item, blocks):
        tokens = pl.ds(pl.multiple_of((item & 1) * BLOCK_TOKENS, BLOCK_TOKENS), BLOCK_TOKENS)
        q = q_ref.at[pattern, (item >> 1) & 3, tokens]
        heads = [q[:, g * HEAD_WIDTH : (g + 1) * HEAD_WIDTH] for g in range(GROUP)]
        return lax.dot_general(
            jnp.concatenate(heads, 0), rows_of(pattern, 0, blocks), (((1,), (1,)), ((), ())),
            preferred_element_type=jnp.float32,
        )

    def rows_of(pattern, kind, blocks):
        starts = [
            pl.multiple_of((2 * kind + (b & 1)) * BLOCK_TOKENS, BLOCK_TOKENS) for b in blocks
        ]
        return jnp.concatenate(
            [kv_ref[pattern, b >> 1, pl.ds(i, BLOCK_TOKENS)] for b, i in zip(blocks, starts)], 0
        )

    def split(s):
        return [
            s[:, i : i + BLOCK_TOKENS] for i in range(0, s.shape[1], BLOCK_TOKENS)
        ]

    def top_of(parts):
        return jnp.max(functools.reduce(jnp.maximum, parts), axis=1, keepdims=True)

    def mix(pattern, blocks, p):
        return jnp.dot(
            jnp.concatenate(p, 1).astype(jnp.bfloat16), rows_of(pattern, 1, blocks),
            preferred_element_type=jnp.float32,
        )

    def own_blocks(pattern, row):
        place = y if pattern == 0 else x
        item = (pattern * 4 + (x if pattern == 0 else y)) * 2 + row
        blocks = [(z * 4 + place) * 2 + i for i in range(row + 1)]
        parts = split(score(pattern, item, blocks))
        query_pos = lax.broadcasted_iota(jnp.int32, parts[0].shape, 0) & (BLOCK_TOKENS - 1)
        key_pos = lax.broadcasted_iota(jnp.int32, parts[0].shape, 1)
        parts[-1] = jnp.where(key_pos <= query_pos, parts[-1], NEG)
        m = top_of(parts)
        p = [jnp.exp2((v - m) * EXP_SCALE) for v in parts]
        m_ref[item] = jnp.broadcast_to(m, (QCOLS, HEAD_WIDTH))
        l_ref[item] = functools.reduce(jnp.add, p)
        acc_ref[item] = mix(pattern, blocks, p)

    def fetch(pattern, c):
        code = chunk_ref[c]
        item, i = code >> 4, code & 15
        at = base_of(pattern, item) + i * STEP
        blocks = [codes_ref[at + k] for k in range(STEP)]
        own = ((item >> 1) & 3) == (x if pattern == 0 else y)
        fresh = jnp.logical_and(i == 0, jnp.logical_not(own))
        return item, blocks, count_ref[item] - i * STEP, fresh

    def absorb(pattern, s, item, blocks, left, fresh):
        parts = split(s)
        m_old = jnp.where(fresh, NEG, m_ref[item])
        m_new = jnp.maximum(m_old, top_of(parts))
        alpha = jnp.exp2((m_old - m_new) * EXP_SCALE)
        off = m_new * EXP_SCALE
        p = [
            jnp.exp2(v * EXP_SCALE - (off if i == 0 else off + jnp.where(left > i, 0.0, -NEG)))
            for i, v in enumerate(parts)
        ]
        m_ref[item] = m_new
        l_ref[item] = jnp.where(fresh, 0.0, l_ref[item]) * alpha + functools.reduce(jnp.add, p)
        acc_ref[item] = jnp.where(fresh, 0.0, acc_ref[item]) * alpha + mix(pattern, blocks, p)

    for pattern, begin, stop in ((0, 0, middle), (1, middle, end)):
        for c in loads(pattern):
            c.wait()
        for row in range(2):
            own_blocks(pattern, row)

        def several(j, carry, pattern=pattern, begin=begin):
            got = [fetch(pattern, begin + j * UNROLL + u) for u in range(UNROLL)]
            scores = [score(pattern, g[0], g[1]) for g in got]
            for g, s in zip(got, scores):
                absorb(pattern, s, *g)
            return carry

        def single(c, carry, pattern=pattern):
            g = fetch(pattern, c)
            absorb(pattern, score(pattern, g[0], g[1]), *g)
            return carry

        whole = (stop - begin) // UNROLL
        lax.fori_loop(0, whole, several, 0)
        lax.fori_loop(begin + whole * UNROLL, stop, single, 0)

    lane = lax.broadcasted_iota(jnp.int32, (BLOCK_TOKENS, BLOCK_TOKENS), 1)

    def close(item, carry):
        own = ((item >> 1) & 3) == jnp.where(item < 8, x, y)
        read = jnp.logical_or(own, count_ref[item] > 0)

        @pl.when(read)
        def _():
            tops = jnp.zeros((BLOCK_TOKENS, BLOCK_TOKENS), jnp.float32)
            sums = jnp.zeros((BLOCK_TOKENS, BLOCK_TOKENS), jnp.float32)
            for g in range(GROUP):
                part = slice(g * HEAD_WIDTH, (g + 1) * HEAD_WIDTH)
                o_ref[item, :, part] = acc_ref[item, part].astype(jnp.bfloat16)
                tops = jnp.where(lane == g, m_ref[item, part], tops)
                sums = jnp.where(
                    lane == g, jnp.sum(l_ref[item, part], axis=1, keepdims=True), sums
                )
            stat_ref[item, 0:8] = tops.T[:8] * EXP_SCALE
            stat_ref[item, 8:16] = sums.T[:8]

        @pl.when(jnp.logical_not(read))
        def _():
            o_ref[item] = jnp.zeros((BLOCK_TOKENS, QCOLS), jnp.bfloat16)
            stat_ref[item, 0:8] = jnp.full((8, BLOCK_TOKENS), NEG, jnp.float32)
            stat_ref[item, 8:16] = jnp.zeros((8, BLOCK_TOKENS), jnp.float32)

        return carry

    lax.fori_loop(0, ITEMS, close, 0)


def attend(codes, q, kv):
    any_spec = pl.BlockSpec(memory_space=pl.ANY)
    blocks = pl.BlockSpec(memory_space=pltpu.VMEM)
    state = pltpu.VMEM((ITEMS, QCOLS, HEAD_WIDTH), jnp.float32)
    return pl.pallas_call(
        attend_kernel,
        in_specs=[pl.BlockSpec(memory_space=pltpu.SMEM), any_spec, any_spec],
        out_specs=[blocks, blocks],
        out_shape=[
            jax.ShapeDtypeStruct((ITEMS, BLOCK_TOKENS, QCOLS), jnp.bfloat16),
            jax.ShapeDtypeStruct((ITEMS, 16, BLOCK_TOKENS), jnp.float32),
        ],
        scratch_shapes=[
            pltpu.SMEM((ITEMS,), jnp.int32),
            pltpu.SMEM((ITEMS * FMAX,), jnp.int32),
            pltpu.VMEM(q.shape, q.dtype),
            pltpu.VMEM(kv.shape, kv.dtype),
            state, state, state,
            pltpu.SemaphoreType.DMA((2, 2)),
        ],
        compiler_params=pltpu.CompilerParams(vmem_limit_bytes=40 * 1024 * 1024),
    )(codes, q, kv)


def columns(rows):
    rest = jnp.zeros((BLOCK_TOKENS - 8 * len(rows), BLOCK_TOKENS), jnp.float32)
    return jnp.concatenate([*rows, rest], 0).T


def combine(parts, w, g):
    cols = slice(g * HEAD_WIDTH, (g + 1) * HEAD_WIDTH)
    return sum(
        part[:, cols].astype(jnp.float32) * w[:, i * 8 + g : i * 8 + g + 1]
        for i, part in enumerate(parts)
    )


def return_kernel(
    o_in, stat_in, out_ref,
    o_got, stat_got, o_relay, stat_relay, o_mine, stat_mine, o_sum, stat_sum,
    send, recv, relay_send, relay_recv, own_sem,
):
    at = {"x": lax.axis_index("x"), "y": lax.axis_index("y")}
    core = lax.axis_index("head")
    axes = ("x", "y")

    def chip(p, step):
        return (at[axes[p]] + step) % 4

    barrier = pltpu.get_barrier_semaphore()
    met = [{axes[p]: chip(p, step), "head": k} for p in range(2) for step in (1, 3) for k in range(2)]
    met.append({"head": 1 - core})
    for device in met:
        pl.semaphore_signal(barrier, inc=1, device_id=device, device_id_type=pl.DeviceIdType.MESH)

    def item(p, step, row):
        return (p * 4 + chip(p, step)) * 2 + row

    def own_copies(p, row):
        i = item(p, 3 if row == 0 else 1, row)
        return [
            pltpu.make_async_copy(o_in.at[i], o_mine.at[p, row], own_sem.at[p, row, 0]),
            pltpu.make_async_copy(stat_in.at[i], stat_mine.at[p, row], own_sem.at[p, row, 1]),
        ]

    def kept_copies(p):
        i = item(p, 0, core)
        return [
            pltpu.make_async_copy(o_in.at[i], o_got.at[p, core, 2], own_sem.at[p, 2, 0]),
            pltpu.make_async_copy(stat_in.at[i], stat_got.at[p, core, 2], own_sem.at[p, 2, 1]),
        ]

    def relay_copies(p, row):
        i = item(p, 2, row)
        device = {axes[p]: chip(p, 3 if row == 0 else 1)}
        return [
            copy_to(src.at[i], dst.at[p, row], (relay_send.at[p, row, n], relay_recv.at[p, row, n]), device)
            for n, (src, dst) in enumerate(((o_in, o_relay), (stat_in, stat_relay)))
        ]

    def copies(p, place, row, o_src, stat_src, n):
        device = {"head": row} if place == 2 else {axes[p]: chip(p, 3 - 2 * place), "head": row}
        return [
            copy_to(src, dst.at[p, core, place], (send.at[p, n, k], recv.at[p, place, core, k]), device)
            for k, (src, dst) in enumerate(((o_src, o_got), (stat_src, stat_got)))
        ]

    def plain(p, place):
        row = (1, 0, 1 - core)[place]
        i = item(p, (3, 1, 0)[place], row)
        return copies(p, place, row, o_in.at[i], stat_in.at[i], place)

    def summed(p, row):
        return copies(p, row, row, o_sum.at[p, row], stat_sum.at[p, row], 3 + row)

    both = [(p, row) for row in range(2) for p in range(2)]
    for p, row in both:
        for c in own_copies(p, row):
            c.start()
    for p in range(2):
        for c in kept_copies(p):
            c.start()
    pl.semaphore_wait(barrier, len(met))
    for p, row in both:
        for c in relay_copies(p, row):
            c.start()
    for place in range(3):
        for p in range(2):
            for c in plain(p, place):
                c.start()
    for p, row in both:
        for c in own_copies(p, row):
            c.wait()
        for c in relay_copies(p, row):
            c.wait_recv()
        stats = [stat_mine[p, row], stat_relay[p, row]]
        top = jnp.maximum(stats[0][:8], stats[1][:8])
        f = [jnp.exp2(v[:8] - top) for v in stats]
        stat_sum[p, row, 0:8] = top
        stat_sum[p, row, 8:16] = stats[0][8:] * f[0] + stats[1][8:] * f[1]
        w = columns(f)
        for g in range(GROUP):
            cols = slice(g * HEAD_WIDTH, (g + 1) * HEAD_WIDTH)
            mixed = combine([o_mine.at[p, row], o_relay.at[p, row]], w, g)
            o_sum[p, row, :, cols] = mixed.astype(jnp.bfloat16)
        for c in summed(p, row):
            c.start()

    def arrival(p, place, c, k):
        dst = (o_got, stat_got)[k].at[p, c, place]
        return copy_to(dst, dst, (send.at[p, 0, k], recv.at[p, place, c, k]), {"head": 1 - core})

    for p in range(2):
        for c in kept_copies(p):
            c.wait()
        for k in range(2):
            arrival(p, 2, 1 - core, k).wait_recv()
            for c in range(2):
                for place in range(2):
                    arrival(p, place, c, k).wait_recv()
        for c in range(2):
            stats = [stat_got[p, c, i] for i in range(3)]
            top = functools.reduce(jnp.maximum, [v[:8] for v in stats])
            f = [jnp.exp2(v[:8] - top) for v in stats]
            total = functools.reduce(jnp.add, [v[8:] * u for v, u in zip(stats, f)])
            inv = 1.0 / jnp.where(total > 0, total, 1.0)
            w = columns([v * inv for v in f])
            for g in range(GROUP):
                start = (c * 2 + p) * QCOLS + g * HEAD_WIDTH
                mixed = combine([o_got.at[p, c, i] for i in range(3)], w, g)
                out_ref[:, start : start + HEAD_WIDTH] = mixed.astype(jnp.bfloat16)
    for p, row in both:
        for c in relay_copies(p, row) + summed(p, row):
            c.wait_send()
    for p in range(2):
        for place in range(3):
            for c in plain(p, place):
                c.wait_send()


def send_back(o, stats):
    dma = pltpu.SemaphoreType.DMA
    any_spec = pl.BlockSpec(memory_space=pl.ANY)
    partial, figures = (BLOCK_TOKENS, QCOLS), (16, BLOCK_TOKENS)
    pairs = [pltpu.VMEM((2, 2, *partial), jnp.bfloat16), pltpu.VMEM((2, 2, *figures), jnp.float32)]
    return pl.pallas_call(
        return_kernel,
        in_specs=[any_spec] * 2,
        out_specs=pl.BlockSpec(memory_space=pltpu.VMEM),
        out_shape=jax.ShapeDtypeStruct((BLOCK_TOKENS, 4 * QCOLS), jnp.bfloat16),
        scratch_shapes=[
            pltpu.VMEM((2, 2, 3, *partial), jnp.bfloat16),
            pltpu.VMEM((2, 2, 3, *figures), jnp.float32),
            *(pairs * 3),
            dma((2, 5, 2)), dma((2, 3, 2, 2)), dma((2, 2, 2)), dma((2, 2, 2)), dma((2, 3, 2)),
        ],
        compiler_params=pltpu.CompilerParams(
            collective_id=1, has_side_effects=True, vmem_limit_bytes=16 * 1024 * 1024
        ),
    )(o, stats)


def copy_to(src, dst, sems, device):
    return pltpu.make_async_remote_copy(
        src_ref=src, dst_ref=dst, send_sem=sems[0], recv_sem=sems[1],
        device_id=device, device_id_type=pl.DeviceIdType.MESH,
    )


MAIN = 3 * BLOCK_TOKENS
LAST = BLOCK_TOKENS
ORDER = (
    ("last near", 0, 0), ("last near", 0, 1), ("z", 1, 0), ("near", 0, 0), ("near", 0, 1),
    ("z", 1, 1), ("z", 2, 0), ("z", 2, 1), ("q", 0, 1), ("q", 0, 0), ("last far", 0, 0),
    ("z", 3, 0), ("last far", 0, 1), ("near", 1, 0), ("z", 3, 1), ("near", 1, 1), ("near", 2, 0),
    ("last z", 1, 0), ("near", 2, 1), ("z", 4, 0), ("near", 3, 0), ("near", 3, 1),
    ("last z", 1, 1), ("near", 4, 0), ("near", 4, 1), ("z", 4, 1), ("last z", 2, 0),
    ("near", 5, 0), ("near", 5, 1), ("last z", 2, 1), ("near", 6, 0), ("near", 6, 1),
    ("last z", 3, 0), ("last z", 3, 1), ("near", 7, 0), ("last z", 4, 0), ("near", 7, 1),
    ("last z", 4, 1),
)


def gather_kernel(
    q_hbm, k_hbm, v_hbm, owners_hbm, pairs_hbm, counts_in, q_all, kv_all, meta_all,
    q_in, k_in, v_in, owners_in, pairs_in, q_own, kv_own, meta_own, in_sem, local_sem,
    z_send, z_recv, near_send, near_recv, far_send, far_recv,
    lz_send, lz_recv, ln_send, ln_recv, lf_send, lf_recv,
    q_send, q_recv, qf_send, qf_recv, t_send, t_recv,
):
    at = {a: lax.axis_index(a) for a in ("y", "z", "x")}
    size = {"y": NY, "z": NZ, "x": NX}
    ring = {a: ((at[a] + 1) % size[a], (at[a] + size[a] - 1) % size[a]) for a in at}

    barrier = pltpu.get_barrier_semaphore()
    for a in at:
        for n in ring[a]:
            pl.semaphore_signal(
                barrier, inc=1, device_id={a: n}, device_id_type=pl.DeviceIdType.MESH
            )

    loads = [
        pltpu.make_async_copy(src, dst, in_sem.at[i])
        for i, (src, dst) in enumerate(
            (
                (k_hbm, k_in), (v_hbm, v_in), (q_hbm, q_in),
                (owners_hbm, owners_in), (pairs_hbm, pairs_in),
            )
        )
    ]
    for c in loads:
        c.start()

    side = ("y", "x")
    cross = ("x", "y")

    def slot(h, place, zo):
        return zo * 4 + place

    local = []

    def keep(src, dst):
        c = pltpu.make_async_copy(src, dst, local_sem.at[len(local)])
        c.start()
        local.append(c)

    sends = []

    def part(d):
        return pl.ds(d * (MAIN // 2), MAIN // 2)

    def z_copy(d, s, h):
        back = at["z"] - (s - 1) if d == 0 else at["z"] + (s - 1)
        rows = part(d) if s == 4 else pl.ds(0, MAIN)
        ref = kv_all.at[h, slot(h, at[side[h]], (back + NZ) % NZ), rows]
        i = (d * 4 + s - 1) * 2 + h
        src = kv_own.at[h, rows] if s == 1 else ref
        return copy_to(src, ref, (z_send.at[i], z_recv.at[i]), {"z": ring["z"][d]})

    def near_copy(h, i, zo, d):
        rows = pl.ds(0, MAIN)
        ref = kv_all.at[h, slot(h, at[side[h]], zo), rows]
        n = (h * 8 + i) * 2 + d
        src = kv_own.at[h, rows] if i == 0 else ref
        return copy_to(src, ref, (near_send.at[n], near_recv.at[n]), {side[h]: ring[side[h]][d]})

    def far_copy(h, i, zo, d):
        a = side[h]
        ref = kv_all.at[h, slot(h, ring[a][1 - d], zo), part(d)]
        n = (h * 8 + i) * 2 + d
        return copy_to(ref, ref, (far_send.at[n], far_recv.at[n]), {a: ring[a][d]})

    def last_near(h, d):
        a = side[h]
        rows = pl.ds(MAIN, LAST)
        ref = kv_all.at[h, slot(h, at[a], at["z"]), rows]
        n = h * 2 + d
        return copy_to(kv_own.at[h, rows], ref, (ln_send.at[n], ln_recv.at[n]), {a: ring[a][d]})

    def last_far(h, d):
        a = side[h]
        rows = pl.ds(MAIN + d * (LAST // 2), LAST // 2)
        ref = kv_all.at[h, slot(h, ring[a][1 - d], at["z"]), rows]
        n = h * 2 + d
        return copy_to(ref, ref, (lf_send.at[n], lf_recv.at[n]), {a: ring[a][d]})

    def last_z(d, s, h):
        back = at["z"] - (s - 1) if d == 0 else at["z"] + (s - 1)
        first = ((back + NZ) % NZ) * 4
        places = pl.ds(first + 2 * d, 2) if s == 4 else pl.ds(first, 4)
        ref = kv_all.at[h, places, pl.ds(MAIN, LAST)]
        i = (d * 4 + s - 1) * 2 + h
        return copy_to(ref, ref, (lz_send.at[i], lz_recv.at[i]), {"z": ring["z"][d]})

    def q_copy(h, d):
        a = cross[h]
        ref = q_all.at[h, at[a]]
        return copy_to(
            q_own.at[h], ref, (q_send.at[h * 2 + d], q_recv.at[h * 2 + d]), {a: ring[a][d]}
        )

    def qf_copy(h, d):
        a = cross[h]
        ref = q_all.at[h, ring[a][1 - d], pl.ds(d * BLOCK_TOKENS, BLOCK_TOKENS)]
        return copy_to(
            ref, ref, (qf_send.at[h * 2 + d], qf_recv.at[h * 2 + d]), {a: ring[a][d]}
        )

    def t_copy(h, d, relay):
        a = cross[h]
        ref = meta_all.at[h, ring[a][1 - d] if relay else at[a]]
        i = (h * 2 + d) * 2 + relay
        return copy_to(
            ref if relay else meta_own.at[h], ref, (t_send.at[i], t_recv.at[i]), {a: ring[a][d]}
        )

    def start(c):
        c.start()
        sends.append(c)

    both = [(h, d) for h in range(2) for d in range(2)]
    zs = [at["z"]]
    for s in range(1, 5):
        zs.append((at["z"] - s + NZ) % NZ)
        zs.append((at["z"] + s) % NZ)
    zs = zs[:8]

    for i, ref in enumerate((k_in, v_in)):
        loads[i].wait()
        for h in range(2):
            kv_own[h, i * 256 : i * 256 + 256] = ref[:, h * HEAD_WIDTH : (h + 1) * HEAD_WIDTH]
    pl.semaphore_wait(barrier, 6)
    for h, d in both:
        start(z_copy(d, 1, h))
    for h, d in both:
        start(last_near(h, d))
    for h, d in both:
        start(near_copy(h, 0, zs[0], d))
    for h in range(2):
        keep(kv_own.at[h], kv_all.at[h, slot(h, at[side[h]], at["z"])])
    loads[2].wait()
    for h in range(2):
        q_own[h] = q_in[:, h * QCOLS : (h + 1) * QCOLS]
    for h, d in both:
        start(q_copy(h, d))

    for c in loads[3:]:
        c.wait()
    meta_own[...] = jnp.zeros_like(meta_own)
    meta_own[0, 0:2, 0:FMAX] = owners_in[...]
    owners = meta_own[0]
    shard = (at["y"] * NZ + at["z"]) * NX + at["x"]
    listed = pairs_in[pl.ds(jnp.minimum(shard, SHARDS - 1 - shard), 1), :]
    half = jnp.take_along_axis(jnp.broadcast_to(listed, (8, 128)), owners, axis=1) & 1
    row = lax.broadcasted_iota(jnp.int32, (8, 128), 0)
    lane = lax.broadcasted_iota(jnp.int32, (8, 128), 1)
    count = jnp.where(row == 0, counts_in[0], jnp.where(row == 1, counts_in[1], 0))
    place, rest = lane >> 4, lane & (FMAX - 1)
    lists = [jnp.zeros((8, 128), jnp.int32)] * 2
    found = [jnp.zeros((8, 128), jnp.int32)] * 2
    for j in range(FMAX):
        owner, which, live = (
            jnp.sum(jnp.where(lane == j, v, 0), axis=1, keepdims=True)
            for v in (owners, half, (lane < count).astype(jnp.int32))
        )
        oy, oz, ox = owner >> 5, (owner >> 2) & 7, owner & 3
        for h, (holder, spot) in enumerate(((ox, oy), (oy, ox))):
            hit = jnp.logical_and(holder == place, live > 0)
            put = jnp.logical_and(hit, jnp.logical_or(found[h] == 0, found[h] == rest))
            lists[h] = jnp.where(put, oz * 8 + spot * 2 + which, lists[h])
            found[h] = found[h] + hit.astype(jnp.int32)
    for h in range(2):
        meta_own[h, 0:2] = lists[h][0:2]
        meta_own[h, 2:4] = found[h][0:2]
    for h, d in both:
        start(t_copy(h, d, 0))
    for h in range(2):
        keep(q_own.at[h], q_all.at[h, at[cross[h]]])
        keep(meta_own.at[h], meta_all.at[h, at[cross[h]]])

    def arrived(kind, i, h):
        for d in range(2):
            if kind == "z":
                z_copy(d, i, h).wait_recv()
                if i < 4:
                    start(z_copy(d, i + 1, h))
                    for e in range(2):
                        start(near_copy(h, 2 * i - 1 + d, zs[2 * i - 1 + d], e))
                elif d == 1:
                    for e in range(2):
                        start(near_copy(h, 7, zs[7], e))
            elif kind == "near":
                near_copy(h, i, zs[i], d).wait_recv()
                start(far_copy(h, i, zs[i], d))
            elif kind == "q":
                q_copy(h, d).wait_recv()
                start(qf_copy(h, d))
            elif kind == "last near":
                last_near(h, d).wait_recv()
                start(last_far(h, d))
            elif kind == "last far":
                last_far(h, d).wait_recv()
                if d == 1:
                    local[h].wait()
                    for e in range(2):
                        start(last_z(e, 1, h))
            else:
                last_z(d, i, h).wait_recv()
                if i < 4:
                    start(last_z(d, i + 1, h))

    for event in ORDER:
        arrived(*event)
    for h in range(2):
        for d in range(2):
            t_copy(h, d, 0).wait_recv()
        start(t_copy(h, 0, 1))
    for h, d in both:
        qf_copy(h, d).wait_recv()
        for i in range(8):
            far_copy(h, i, zs[i], d).wait_recv()
    for h in range(2):
        t_copy(h, 0, 1).wait_recv()
    for c in sends:
        c.wait_send()
    for c in local[2:]:
        c.wait()


def gather_all(q, k, v, owners, counts, pairs):
    dma = pltpu.SemaphoreType.DMA
    any_spec = pl.BlockSpec(memory_space=pl.ANY)
    arrays = [pltpu.with_memory_space_constraint(a, pltpu.HBM) for a in (q, k, v, owners, pairs)]
    return pl.pallas_call(
        gather_kernel,
        in_specs=[any_spec] * 5 + [pl.BlockSpec(memory_space=pltpu.SMEM)],
        out_specs=[any_spec] * 3,
        out_shape=[
            jax.ShapeDtypeStruct((2, 4, 2 * BLOCK_TOKENS, QCOLS), jnp.bfloat16),
            jax.ShapeDtypeStruct((2, SLOTS, MAIN + LAST, HEAD_WIDTH), jnp.bfloat16),
            jax.ShapeDtypeStruct((2, 4, 8, 128), jnp.int32),
        ],
        scratch_shapes=[pltpu.VMEM(a.shape, a.dtype) for a in (q, k, v, owners, pairs)]
        + [
            pltpu.VMEM((2, 2 * BLOCK_TOKENS, QCOLS), jnp.bfloat16),
            pltpu.VMEM((2, MAIN + LAST, HEAD_WIDTH), jnp.bfloat16),
            pltpu.VMEM((2, 8, 128), jnp.int32),
        ]
        + [dma((n,)) for n in (5, 6, 16, 16, 32, 32, 32, 32, 16, 16, 4, 4, 4, 4, 4, 4, 4, 4, 8, 8)],
        compiler_params=pltpu.CompilerParams(
            collective_id=0, has_side_effects=True, vmem_limit_bytes=16 * 1024 * 1024
        ),
    )(*arrays, counts)


def on_device(queries, keys, values, far_owners, far_counts, pair_blocks):
    q, kv, codes = gather_all(queries, keys, values, far_owners, far_counts, pair_blocks)
    o, stats = attend(codes.reshape(-1), q, kv)
    return send_back(o, stats)


def solution(mesh):
    grid = Mesh(mesh.devices.reshape(NY, NZ, NX, 2), ("y", "z", "x", "head"))
    ctx = ("y", "z", "x")
    placed = (P(ctx, "head"), P(ctx, "head"), P(ctx, "head"), P(ctx, None), P(ctx), P())
    return jax.shard_map(
        on_device,
        mesh=grid,
        in_specs=placed,
        out_specs=P((*ctx, "head"), None),
        check_vma=False,
    )
```

```python
import functools

import jax
import jax.numpy as jnp
from jax import lax
from jax.experimental import pallas as pl
from jax.experimental.pallas import tpu as pltpu
from jax.sharding import Mesh, PartitionSpec as P

HEAD_WIDTH = 128
BLOCK_TOKENS = 128
GROUP = 5
QCOLS = GROUP * HEAD_WIDTH
NY, NZ, NX = 4, 8, 4
SHARDS = NY * NZ * NX
FMAX = 16
SLOTS = 32
ITEMS = 16
STEP = 2
UNROLL = 4
NEG = -1e30
EXP_SCALE = 1.4426950408889634 * HEAD_WIDTH ** (-0.5)


def attend_kernel(
    codes_ref, q_in, kv_in, o_ref, stat_ref,
    count_ref, chunk_ref, q_ref, kv_ref, acc_ref, m_ref, l_ref, sem,
):
    y, z, x = (lax.axis_index(a) for a in ("y", "z", "x"))

    def loads(pattern):
        return [
            pltpu.make_async_copy(src.at[pattern], dst.at[pattern], sem.at[i, pattern])
            for i, (src, dst) in enumerate(((q_in, q_ref), (kv_in, kv_ref)))
        ]

    for c in loads(0):
        c.start()

    def base_of(pattern, item):
        return (item >> 1) * 1024 + (item & 1) * 128 + (x if pattern == 0 else y) * FMAX

    def build(pattern, item, chunks):
        n = codes_ref[base_of(pattern, item) + 2 * 128]
        count_ref[item] = n

        def note(i, chunks):
            chunk_ref[chunks] = item * 16 + i
            return chunks + 1

        return lax.fori_loop(0, (n + STEP - 1) // STEP, note, chunks)

    middle = lax.fori_loop(0, 8, functools.partial(build, 0), jnp.int32(0))
    end = lax.fori_loop(8, 16, functools.partial(build, 1), middle)

    def score(pattern, item, blocks):
        tokens = pl.ds(pl.multiple_of((item & 1) * BLOCK_TOKENS, BLOCK_TOKENS), BLOCK_TOKENS)
        q = q_ref.at[pattern, (item >> 1) & 3, tokens]
        heads = [q[:, g * HEAD_WIDTH : (g + 1) * HEAD_WIDTH] for g in range(GROUP)]
        return lax.dot_general(
            jnp.concatenate(heads, 0), rows_of(pattern, 0, blocks), (((1,), (1,)), ((), ())),
            preferred_element_type=jnp.float32,
        )

    def rows_of(pattern, kind, blocks):
        starts = [
            pl.multiple_of((2 * kind + (b & 1)) * BLOCK_TOKENS, BLOCK_TOKENS) for b in blocks
        ]
        return jnp.concatenate(
            [kv_ref[pattern, b >> 1, pl.ds(i, BLOCK_TOKENS)] for b, i in zip(blocks, starts)], 0
        )

    def split(s):
        return [
            s[:, i : i + BLOCK_TOKENS] for i in range(0, s.shape[1], BLOCK_TOKENS)
        ]

    def top_of(parts):
        return jnp.max(functools.reduce(jnp.maximum, parts), axis=1, keepdims=True)

    def mix(pattern, blocks, p):
        return jnp.dot(
            jnp.concatenate(p, 1).astype(jnp.bfloat16), rows_of(pattern, 1, blocks),
            preferred_element_type=jnp.float32,
        )

    def own_blocks(pattern, row):
        place = y if pattern == 0 else x
        item = (pattern * 4 + (x if pattern == 0 else y)) * 2 + row
        blocks = [(z * 4 + place) * 2 + i for i in range(row + 1)]
        parts = split(score(pattern, item, blocks))
        query_pos = lax.broadcasted_iota(jnp.int32, parts[0].shape, 0) & (BLOCK_TOKENS - 1)
        key_pos = lax.broadcasted_iota(jnp.int32, parts[0].shape, 1)
        parts[-1] = jnp.where(key_pos <= query_pos, parts[-1], NEG)
        m = top_of(parts)
        p = [jnp.exp2((v - m) * EXP_SCALE) for v in parts]
        m_ref[item] = jnp.broadcast_to(m, (QCOLS, HEAD_WIDTH))
        l_ref[item] = functools.reduce(jnp.add, p)
        acc_ref[item] = mix(pattern, blocks, p)

    def fetch(pattern, c):
        code = chunk_ref[c]
        item, i = code >> 4, code & 15
        at = base_of(pattern, item) + i * STEP
        blocks = [codes_ref[at + k] for k in range(STEP)]
        own = ((item >> 1) & 3) == (x if pattern == 0 else y)
        fresh = jnp.logical_and(i == 0, jnp.logical_not(own))
        return item, blocks, count_ref[item] - i * STEP, fresh

    def absorb(pattern, s, item, blocks, left, fresh):
        parts = split(s)
        m_old = jnp.where(fresh, NEG, m_ref[item])
        m_new = jnp.maximum(m_old, top_of(parts))
        alpha = jnp.exp2((m_old - m_new) * EXP_SCALE)
        off = m_new * EXP_SCALE
        p = [
            jnp.exp2(v * EXP_SCALE - (off if i == 0 else off + jnp.where(left > i, 0.0, -NEG)))
            for i, v in enumerate(parts)
        ]
        m_ref[item] = m_new
        l_ref[item] = jnp.where(fresh, 0.0, l_ref[item]) * alpha + functools.reduce(jnp.add, p)
        acc_ref[item] = jnp.where(fresh, 0.0, acc_ref[item]) * alpha + mix(pattern, blocks, p)

    for pattern, begin, stop in ((0, 0, middle), (1, middle, end)):
        for c in loads(pattern):
            c.wait()
        if pattern == 0:
            for c in loads(1):
                c.start()
        for row in range(2):
            own_blocks(pattern, row)

        def several(j, carry, pattern=pattern, begin=begin):
            got = [fetch(pattern, begin + j * UNROLL + u) for u in range(UNROLL)]
            scores = [score(pattern, g[0], g[1]) for g in got]
            for g, s in zip(got, scores):
                absorb(pattern, s, *g)
            return carry

        def single(c, carry, pattern=pattern):
            g = fetch(pattern, c)
            absorb(pattern, score(pattern, g[0], g[1]), *g)
            return carry

        whole = (stop - begin) // UNROLL
        lax.fori_loop(0, whole, several, 0)
        lax.fori_loop(begin + whole * UNROLL, stop, single, 0)

    lane = lax.broadcasted_iota(jnp.int32, (BLOCK_TOKENS, BLOCK_TOKENS), 1)

    def close(item, carry):
        own = ((item >> 1) & 3) == jnp.where(item < 8, x, y)
        read = jnp.logical_or(own, count_ref[item] > 0)

        @pl.when(read)
        def _():
            tops = jnp.zeros((BLOCK_TOKENS, BLOCK_TOKENS), jnp.float32)
            sums = jnp.zeros((BLOCK_TOKENS, BLOCK_TOKENS), jnp.float32)
            for g in range(GROUP):
                part = slice(g * HEAD_WIDTH, (g + 1) * HEAD_WIDTH)
                o_ref[item, :, part] = acc_ref[item, part].astype(jnp.bfloat16)
                tops = jnp.where(lane == g, m_ref[item, part], tops)
                sums = jnp.where(
                    lane == g, jnp.sum(l_ref[item, part], axis=1, keepdims=True), sums
                )
            stat_ref[item, 0:8] = tops.T[:8] * EXP_SCALE
            stat_ref[item, 8:16] = sums.T[:8]

        @pl.when(jnp.logical_not(read))
        def _():
            o_ref[item] = jnp.zeros((BLOCK_TOKENS, QCOLS), jnp.bfloat16)
            stat_ref[item, 0:8] = jnp.full((8, BLOCK_TOKENS), NEG, jnp.float32)
            stat_ref[item, 8:16] = jnp.zeros((8, BLOCK_TOKENS), jnp.float32)

        return carry

    lax.fori_loop(0, ITEMS, close, 0)


def attend(codes, q, kv):
    any_spec = pl.BlockSpec(memory_space=pl.ANY)
    blocks = pl.BlockSpec(memory_space=pltpu.VMEM)
    state = pltpu.VMEM((ITEMS, QCOLS, HEAD_WIDTH), jnp.float32)
    return pl.pallas_call(
        attend_kernel,
        in_specs=[pl.BlockSpec(memory_space=pltpu.SMEM), any_spec, any_spec],
        out_specs=[blocks, blocks],
        out_shape=[
            jax.ShapeDtypeStruct((ITEMS, BLOCK_TOKENS, QCOLS), jnp.bfloat16),
            jax.ShapeDtypeStruct((ITEMS, 16, BLOCK_TOKENS), jnp.float32),
        ],
        scratch_shapes=[
            pltpu.SMEM((ITEMS,), jnp.int32),
            pltpu.SMEM((ITEMS * FMAX,), jnp.int32),
            pltpu.VMEM(q.shape, q.dtype),
            pltpu.VMEM(kv.shape, kv.dtype),
            state, state, state,
            pltpu.SemaphoreType.DMA((2, 2)),
        ],
        compiler_params=pltpu.CompilerParams(vmem_limit_bytes=40 * 1024 * 1024),
    )(codes, q, kv)


def columns(rows):
    rest = jnp.zeros((BLOCK_TOKENS - 8 * len(rows), BLOCK_TOKENS), jnp.float32)
    return jnp.concatenate([*rows, rest], 0).T


def combine(parts, w, g):
    cols = slice(g * HEAD_WIDTH, (g + 1) * HEAD_WIDTH)
    return sum(
        part[:, cols].astype(jnp.float32) * w[:, i * 8 + g : i * 8 + g + 1]
        for i, part in enumerate(parts)
    )


def return_kernel(
    o_in, stat_in, out_ref,
    o_got, stat_got, o_relay, stat_relay, o_mine, stat_mine, o_sum, stat_sum,
    send, recv, relay_send, relay_recv, own_sem,
):
    at = {"x": lax.axis_index("x"), "y": lax.axis_index("y")}
    core = lax.axis_index("head")
    axes = ("x", "y")

    def chip(p, step):
        return (at[axes[p]] + step) % 4

    barrier = pltpu.get_barrier_semaphore()
    met = [{axes[p]: chip(p, step), "head": k} for p in range(2) for step in (1, 3) for k in range(2)]
    met.append({"head": 1 - core})
    for device in met:
        pl.semaphore_signal(barrier, inc=1, device_id=device, device_id_type=pl.DeviceIdType.MESH)

    def item(p, step, row):
        return (p * 4 + chip(p, step)) * 2 + row

    def own_copies(p, row):
        i = item(p, 3 if row == 0 else 1, row)
        return [
            pltpu.make_async_copy(o_in.at[i], o_mine.at[p, row], own_sem.at[p, row, 0]),
            pltpu.make_async_copy(stat_in.at[i], stat_mine.at[p, row], own_sem.at[p, row, 1]),
        ]

    def kept_copies(p):
        i = item(p, 0, core)
        return [
            pltpu.make_async_copy(o_in.at[i], o_got.at[p, core, 2], own_sem.at[p, 2, 0]),
            pltpu.make_async_copy(stat_in.at[i], stat_got.at[p, core, 2], own_sem.at[p, 2, 1]),
        ]

    def relay_copies(p, row):
        i = item(p, 2, row)
        device = {axes[p]: chip(p, 3 if row == 0 else 1)}
        return [
            copy_to(src.at[i], dst.at[p, row], (relay_send.at[p, row, n], relay_recv.at[p, row, n]), device)
            for n, (src, dst) in enumerate(((o_in, o_relay), (stat_in, stat_relay)))
        ]

    def copies(p, place, row, o_src, stat_src, n):
        device = {"head": row} if place == 2 else {axes[p]: chip(p, 3 - 2 * place), "head": row}
        return [
            copy_to(src, dst.at[p, core, place], (send.at[p, n, k], recv.at[p, place, core, k]), device)
            for k, (src, dst) in enumerate(((o_src, o_got), (stat_src, stat_got)))
        ]

    def plain(p, place):
        row = (1, 0, 1 - core)[place]
        i = item(p, (3, 1, 0)[place], row)
        return copies(p, place, row, o_in.at[i], stat_in.at[i], place)

    def summed(p, row):
        return copies(p, row, row, o_sum.at[p, row], stat_sum.at[p, row], 3 + row)

    both = [(p, row) for row in range(2) for p in range(2)]
    for p, row in both:
        for c in own_copies(p, row):
            c.start()
    for p in range(2):
        for c in kept_copies(p):
            c.start()
    pl.semaphore_wait(barrier, len(met))
    for p, row in both:
        for c in relay_copies(p, row):
            c.start()
    for place in range(3):
        for p in range(2):
            for c in plain(p, place):
                c.start()
    for p, row in both:
        for c in own_copies(p, row):
            c.wait()
        for c in relay_copies(p, row):
            c.wait_recv()
        stats = [stat_mine[p, row], stat_relay[p, row]]
        top = jnp.maximum(stats[0][:8], stats[1][:8])
        f = [jnp.exp2(v[:8] - top) for v in stats]
        stat_sum[p, row, 0:8] = top
        stat_sum[p, row, 8:16] = stats[0][8:] * f[0] + stats[1][8:] * f[1]
        w = columns(f)
        for g in range(GROUP):
            cols = slice(g * HEAD_WIDTH, (g + 1) * HEAD_WIDTH)
            mixed = combine([o_mine.at[p, row], o_relay.at[p, row]], w, g)
            o_sum[p, row, :, cols] = mixed.astype(jnp.bfloat16)
        for c in summed(p, row):
            c.start()

    def arrival(p, place, c, k):
        dst = (o_got, stat_got)[k].at[p, c, place]
        return copy_to(dst, dst, (send.at[p, 0, k], recv.at[p, place, c, k]), {"head": 1 - core})

    for p in range(2):
        for c in kept_copies(p):
            c.wait()
        for k in range(2):
            arrival(p, 2, 1 - core, k).wait_recv()
            for c in range(2):
                for place in range(2):
                    arrival(p, place, c, k).wait_recv()
        for c in range(2):
            stats = [stat_got[p, c, i] for i in range(3)]
            top = functools.reduce(jnp.maximum, [v[:8] for v in stats])
            f = [jnp.exp2(v[:8] - top) for v in stats]
            total = functools.reduce(jnp.add, [v[8:] * u for v, u in zip(stats, f)])
            inv = 1.0 / jnp.where(total > 0, total, 1.0)
            w = columns([v * inv for v in f])
            for g in range(GROUP):
                start = (c * 2 + p) * QCOLS + g * HEAD_WIDTH
                mixed = combine([o_got.at[p, c, i] for i in range(3)], w, g)
                out_ref[:, start : start + HEAD_WIDTH] = mixed.astype(jnp.bfloat16)
    for p, row in both:
        for c in relay_copies(p, row) + summed(p, row):
            c.wait_send()
    for p in range(2):
        for place in range(3):
            for c in plain(p, place):
                c.wait_send()


def send_back(o, stats):
    dma = pltpu.SemaphoreType.DMA
    any_spec = pl.BlockSpec(memory_space=pl.ANY)
    partial, figures = (BLOCK_TOKENS, QCOLS), (16, BLOCK_TOKENS)
    pairs = [pltpu.VMEM((2, 2, *partial), jnp.bfloat16), pltpu.VMEM((2, 2, *figures), jnp.float32)]
    return pl.pallas_call(
        return_kernel,
        in_specs=[any_spec] * 2,
        out_specs=pl.BlockSpec(memory_space=pltpu.VMEM),
        out_shape=jax.ShapeDtypeStruct((BLOCK_TOKENS, 4 * QCOLS), jnp.bfloat16),
        scratch_shapes=[
            pltpu.VMEM((2, 2, 3, *partial), jnp.bfloat16),
            pltpu.VMEM((2, 2, 3, *figures), jnp.float32),
            *(pairs * 3),
            dma((2, 5, 2)), dma((2, 3, 2, 2)), dma((2, 2, 2)), dma((2, 2, 2)), dma((2, 3, 2)),
        ],
        compiler_params=pltpu.CompilerParams(
            collective_id=1, has_side_effects=True, vmem_limit_bytes=16 * 1024 * 1024
        ),
    )(o, stats)


def copy_to(src, dst, sems, device):
    return pltpu.make_async_remote_copy(
        src_ref=src, dst_ref=dst, send_sem=sems[0], recv_sem=sems[1],
        device_id=device, device_id_type=pl.DeviceIdType.MESH,
    )


MAIN = 3 * BLOCK_TOKENS
LAST = BLOCK_TOKENS
ORDER = (
    ("last near", 0, 0), ("last near", 0, 1), ("z", 1, 0), ("near", 0, 0), ("near", 0, 1),
    ("z", 1, 1), ("z", 2, 0), ("z", 2, 1), ("q", 0, 1), ("q", 0, 0), ("last far", 0, 0),
    ("z", 3, 0), ("last far", 0, 1), ("near", 1, 0), ("z", 3, 1), ("near", 1, 1), ("near", 2, 0),
    ("last z", 1, 0), ("near", 2, 1), ("z", 4, 0), ("near", 3, 0), ("near", 3, 1),
    ("last z", 1, 1), ("near", 4, 0), ("near", 4, 1), ("z", 4, 1), ("last z", 2, 0),
    ("near", 5, 0), ("near", 5, 1), ("last z", 2, 1), ("near", 6, 0), ("near", 6, 1),
    ("last z", 3, 0), ("last z", 3, 1), ("near", 7, 0), ("last z", 4, 0), ("near", 7, 1),
    ("last z", 4, 1),
)


def gather_kernel(
    q_hbm, k_hbm, v_hbm, owners_hbm, pairs_hbm, counts_hbm, q_all, kv_all, meta_all,
    q_in, k_in, v_in, owners_in, pairs_in, counts_in, q_own, kv_own, meta_own, in_sem, local_sem,
    z_send, z_recv, near_send, near_recv, far_send, far_recv,
    lz_send, lz_recv, ln_send, ln_recv, lf_send, lf_recv,
    q_send, q_recv, qf_send, qf_recv, t_send, t_recv,
):
    at = {a: lax.axis_index(a) for a in ("y", "z", "x")}
    size = {"y": NY, "z": NZ, "x": NX}
    ring = {a: ((at[a] + 1) % size[a], (at[a] + size[a] - 1) % size[a]) for a in at}

    barrier = pltpu.get_barrier_semaphore()
    for a in at:
        for n in ring[a]:
            pl.semaphore_signal(
                barrier, inc=1, device_id={a: n}, device_id_type=pl.DeviceIdType.MESH
            )

    loads = [
        pltpu.make_async_copy(src, dst, in_sem.at[i])
        for i, (src, dst) in enumerate(
            (
                (k_hbm, k_in), (v_hbm, v_in), (q_hbm, q_in),
                (owners_hbm, owners_in), (pairs_hbm, pairs_in), (counts_hbm, counts_in),
            )
        )
    ]
    for c in loads:
        c.start()

    side = ("y", "x")
    cross = ("x", "y")

    def slot(h, place, zo):
        return zo * 4 + place

    local = []

    def keep(src, dst):
        c = pltpu.make_async_copy(src, dst, local_sem.at[len(local)])
        c.start()
        local.append(c)

    sends = []

    def part(d):
        return pl.ds(d * (MAIN // 2), MAIN // 2)

    def z_copy(d, s, h):
        back = at["z"] - (s - 1) if d == 0 else at["z"] + (s - 1)
        rows = part(d) if s == 4 else pl.ds(0, MAIN)
        ref = kv_all.at[h, slot(h, at[side[h]], (back + NZ) % NZ), rows]
        i = (d * 4 + s - 1) * 2 + h
        src = kv_own.at[h, rows] if s == 1 else ref
        return copy_to(src, ref, (z_send.at[i], z_recv.at[i]), {"z": ring["z"][d]})

    def near_copy(h, i, zo, d):
        rows = pl.ds(0, MAIN)
        ref = kv_all.at[h, slot(h, at[side[h]], zo), rows]
        n = (h * 8 + i) * 2 + d
        src = kv_own.at[h, rows] if i == 0 else ref
        return copy_to(src, ref, (near_send.at[n], near_recv.at[n]), {side[h]: ring[side[h]][d]})

    def far_copy(h, i, zo, d):
        a = side[h]
        ref = kv_all.at[h, slot(h, ring[a][1 - d], zo), part(d)]
        n = (h * 8 + i) * 2 + d
        return copy_to(ref, ref, (far_send.at[n], far_recv.at[n]), {a: ring[a][d]})

    def last_near(h, d):
        a = side[h]
        rows = pl.ds(MAIN, LAST)
        ref = kv_all.at[h, slot(h, at[a], at["z"]), rows]
        n = h * 2 + d
        return copy_to(kv_own.at[h, rows], ref, (ln_send.at[n], ln_recv.at[n]), {a: ring[a][d]})

    def last_far(h, d):
        a = side[h]
        rows = pl.ds(MAIN + d * (LAST // 2), LAST // 2)
        ref = kv_all.at[h, slot(h, ring[a][1 - d], at["z"]), rows]
        n = h * 2 + d
        return copy_to(ref, ref, (lf_send.at[n], lf_recv.at[n]), {a: ring[a][d]})

    def last_z(d, s, h):
        back = at["z"] - (s - 1) if d == 0 else at["z"] + (s - 1)
        first = ((back + NZ) % NZ) * 4
        places = pl.ds(first + 2 * d, 2) if s == 4 else pl.ds(first, 4)
        ref = kv_all.at[h, places, pl.ds(MAIN, LAST)]
        i = (d * 4 + s - 1) * 2 + h
        return copy_to(ref, ref, (lz_send.at[i], lz_recv.at[i]), {"z": ring["z"][d]})

    def q_copy(h, d):
        a = cross[h]
        ref = q_all.at[h, at[a]]
        return copy_to(
            q_own.at[h], ref, (q_send.at[h * 2 + d], q_recv.at[h * 2 + d]), {a: ring[a][d]}
        )

    def qf_copy(h, d):
        a = cross[h]
        ref = q_all.at[h, ring[a][1 - d], pl.ds(d * BLOCK_TOKENS, BLOCK_TOKENS)]
        return copy_to(
            ref, ref, (qf_send.at[h * 2 + d], qf_recv.at[h * 2 + d]), {a: ring[a][d]}
        )

    def t_copy(h, d, relay):
        a = cross[h]
        ref = meta_all.at[h, ring[a][1 - d] if relay else at[a]]
        i = (h * 2 + d) * 2 + relay
        return copy_to(
            ref if relay else meta_own.at[h], ref, (t_send.at[i], t_recv.at[i]), {a: ring[a][d]}
        )

    def start(c):
        c.start()
        sends.append(c)

    both = [(h, d) for h in range(2) for d in range(2)]
    zs = [at["z"]]
    for s in range(1, 5):
        zs.append((at["z"] - s + NZ) % NZ)
        zs.append((at["z"] + s) % NZ)
    zs = zs[:8]

    for i, ref in enumerate((k_in, v_in)):
        loads[i].wait()
        for h in range(2):
            kv_own[h, i * 256 : i * 256 + 256] = ref[:, h * HEAD_WIDTH : (h + 1) * HEAD_WIDTH]
    pl.semaphore_wait(barrier, 6)
    for h, d in both:
        start(z_copy(d, 1, h))
    for h, d in both:
        start(last_near(h, d))
    for h, d in both:
        start(near_copy(h, 0, zs[0], d))
    for h in range(2):
        keep(kv_own.at[h], kv_all.at[h, slot(h, at[side[h]], at["z"])])
    loads[2].wait()
    for h in range(2):
        q_own[h] = q_in[:, h * QCOLS : (h + 1) * QCOLS]
    for h, d in both:
        start(q_copy(h, d))

    for c in loads[3:]:
        c.wait()
    meta_own[...] = jnp.zeros_like(meta_own)
    meta_own[0, 0:2, 0:FMAX] = owners_in[...]
    owners = meta_own[0]
    shard = (at["y"] * NZ + at["z"]) * NX + at["x"]
    listed = pairs_in[pl.ds(jnp.minimum(shard, SHARDS - 1 - shard), 1), :]
    half = jnp.take_along_axis(jnp.broadcast_to(listed, (8, 128)), owners, axis=1) & 1
    row = lax.broadcasted_iota(jnp.int32, (8, 128), 0)
    lane = lax.broadcasted_iota(jnp.int32, (8, 128), 1)
    count = jnp.where(row == 0, counts_in[0], jnp.where(row == 1, counts_in[1], 0))
    place, rest = lane >> 4, lane & (FMAX - 1)
    lists = [jnp.zeros((8, 128), jnp.int32)] * 2
    found = [jnp.zeros((8, 128), jnp.int32)] * 2
    for j in range(FMAX):
        owner, which, live = (
            jnp.sum(jnp.where(lane == j, v, 0), axis=1, keepdims=True)
            for v in (owners, half, (lane < count).astype(jnp.int32))
        )
        oy, oz, ox = owner >> 5, (owner >> 2) & 7, owner & 3
        for h, (holder, spot) in enumerate(((ox, oy), (oy, ox))):
            hit = jnp.logical_and(holder == place, live > 0)
            put = jnp.logical_and(hit, jnp.logical_or(found[h] == 0, found[h] == rest))
            lists[h] = jnp.where(put, oz * 8 + spot * 2 + which, lists[h])
            found[h] = found[h] + hit.astype(jnp.int32)
    for h in range(2):
        meta_own[h, 0:2] = lists[h][0:2]
        meta_own[h, 2:4] = found[h][0:2]
    for h, d in both:
        start(t_copy(h, d, 0))
    for h in range(2):
        keep(q_own.at[h], q_all.at[h, at[cross[h]]])
        keep(meta_own.at[h], meta_all.at[h, at[cross[h]]])

    def arrived(kind, i, h):
        for d in range(2):
            if kind == "z":
                z_copy(d, i, h).wait_recv()
                if i < 4:
                    start(z_copy(d, i + 1, h))
                    for e in range(2):
                        start(near_copy(h, 2 * i - 1 + d, zs[2 * i - 1 + d], e))
                elif d == 1:
                    for e in range(2):
                        start(near_copy(h, 7, zs[7], e))
            elif kind == "near":
                near_copy(h, i, zs[i], d).wait_recv()
                start(far_copy(h, i, zs[i], d))
            elif kind == "q":
                q_copy(h, d).wait_recv()
                start(qf_copy(h, d))
            elif kind == "last near":
                last_near(h, d).wait_recv()
                start(last_far(h, d))
            elif kind == "last far":
                last_far(h, d).wait_recv()
                if d == 1:
                    local[h].wait()
                    for e in range(2):
                        start(last_z(e, 1, h))
            else:
                last_z(d, i, h).wait_recv()
                if i < 4:
                    start(last_z(d, i + 1, h))

    for event in ORDER:
        arrived(*event)
    for h in range(2):
        for d in range(2):
            t_copy(h, d, 0).wait_recv()
        start(t_copy(h, 0, 1))
    for h, d in both:
        qf_copy(h, d).wait_recv()
        for i in range(8):
            far_copy(h, i, zs[i], d).wait_recv()
    for h in range(2):
        t_copy(h, 0, 1).wait_recv()
    for c in sends:
        c.wait_send()
    for c in local[2:]:
        c.wait()


def gather_all(q, k, v, owners, counts, pairs):
    dma = pltpu.SemaphoreType.DMA
    any_spec = pl.BlockSpec(memory_space=pl.ANY)
    arrays = [pltpu.with_memory_space_constraint(a, pltpu.HBM) for a in (q, k, v, owners, pairs, counts)]
    return pl.pallas_call(
        gather_kernel,
        in_specs=[any_spec] * 6,
        out_specs=[any_spec] * 3,
        out_shape=[
            jax.ShapeDtypeStruct((2, 4, 2 * BLOCK_TOKENS, QCOLS), jnp.bfloat16),
            jax.ShapeDtypeStruct((2, SLOTS, MAIN + LAST, HEAD_WIDTH), jnp.bfloat16),
            jax.ShapeDtypeStruct((2, 4, 8, 128), jnp.int32),
        ],
        scratch_shapes=[pltpu.VMEM(a.shape, a.dtype) for a in (q, k, v, owners, pairs)]
        + [
            pltpu.SMEM(counts.shape, counts.dtype),
            pltpu.VMEM((2, 2 * BLOCK_TOKENS, QCOLS), jnp.bfloat16),
            pltpu.VMEM((2, MAIN + LAST, HEAD_WIDTH), jnp.bfloat16),
            pltpu.VMEM((2, 8, 128), jnp.int32),
        ]
        + [dma((n,)) for n in (6, 6, 16, 16, 32, 32, 32, 32, 16, 16, 4, 4, 4, 4, 4, 4, 4, 4, 8, 8)],
        compiler_params=pltpu.CompilerParams(
            collective_id=0, has_side_effects=True, vmem_limit_bytes=16 * 1024 * 1024
        ),
    )(*arrays)


def on_device(queries, keys, values, far_owners, far_counts, pair_blocks):
    q, kv, codes = gather_all(queries, keys, values, far_owners, far_counts, pair_blocks)
    o, stats = attend(codes.reshape(-1), q, kv)
    return send_back(o, stats)


def solution(mesh):
    grid = Mesh(mesh.devices.reshape(NY, NZ, NX, 2), ("y", "z", "x", "head"))
    ctx = ("y", "z", "x")
    placed = (P(ctx, "head"), P(ctx, "head"), P(ctx, "head"), P(ctx, None), P(ctx), P())
    return jax.shard_map(
        on_device,
        mesh=grid,
        in_specs=placed,
        out_specs=P((*ctx, "head"), None),
        check_vma=False,
    )
```

```python
import functools

import jax
import jax.numpy as jnp
from jax import lax
from jax.experimental import pallas as pl
from jax.experimental.pallas import tpu as pltpu
from jax.sharding import Mesh, PartitionSpec as P

HEAD_WIDTH = 128
BLOCK_TOKENS = 128
GROUP = 5
QCOLS = GROUP * HEAD_WIDTH
NY, NZ, NX = 4, 8, 4
SHARDS = NY * NZ * NX
FMAX = 16
SLOTS = 32
ITEMS = 16
STEP = 2
UNROLL = 4
NEG = -1e30
EXP_SCALE = 1.4426950408889634 * HEAD_WIDTH ** (-0.5)


def attend_kernel(
    codes_ref, q_in, kv_in, o_ref, stat_ref,
    count_ref, chunk_ref, q_ref, kv_ref, acc_ref, m_ref, l_ref, sem,
):
    y, z, x = (lax.axis_index(a) for a in ("y", "z", "x"))

    def loads(pattern):
        return [
            pltpu.make_async_copy(src.at[pattern], dst.at[pattern], sem.at[i, pattern])
            for i, (src, dst) in enumerate(((q_in, q_ref), (kv_in, kv_ref)))
        ]

    for c in loads(0):
        c.start()

    def base_of(pattern, item):
        return (item >> 1) * 1024 + (item & 1) * 128 + (x if pattern == 0 else y) * FMAX

    def build(pattern, item, chunks):
        n = codes_ref[base_of(pattern, item) + 2 * 128]
        count_ref[item] = n

        def note(i, chunks):
            chunk_ref[chunks] = item * 16 + i
            return chunks + 1

        return lax.fori_loop(0, (n + STEP - 1) // STEP, note, chunks)

    middle = lax.fori_loop(0, 8, functools.partial(build, 0), jnp.int32(0))
    end = lax.fori_loop(8, 16, functools.partial(build, 1), middle)

    def clear(item, carry):
        m_ref[item] = jnp.full((QCOLS, HEAD_WIDTH), NEG, jnp.float32)
        l_ref[item] = jnp.zeros((QCOLS, HEAD_WIDTH), jnp.float32)
        acc_ref[item] = jnp.zeros((QCOLS, HEAD_WIDTH), jnp.float32)
        return carry

    lax.fori_loop(0, ITEMS, clear, 0)

    def score(pattern, item, blocks):
        tokens = pl.ds(pl.multiple_of((item & 1) * BLOCK_TOKENS, BLOCK_TOKENS), BLOCK_TOKENS)
        q = q_ref.at[pattern, (item >> 1) & 3, tokens]
        heads = [q[:, g * HEAD_WIDTH : (g + 1) * HEAD_WIDTH] for g in range(GROUP)]
        return lax.dot_general(
            jnp.concatenate(heads, 0), rows_of(pattern, 0, blocks), (((1,), (1,)), ((), ())),
            preferred_element_type=jnp.float32,
        )

    def rows_of(pattern, kind, blocks):
        starts = [
            pl.multiple_of((2 * kind + (b & 1)) * BLOCK_TOKENS, BLOCK_TOKENS) for b in blocks
        ]
        return jnp.concatenate(
            [kv_ref[pattern, b >> 1, pl.ds(i, BLOCK_TOKENS)] for b, i in zip(blocks, starts)], 0
        )

    def split(s):
        return [
            s[:, i : i + BLOCK_TOKENS] for i in range(0, s.shape[1], BLOCK_TOKENS)
        ]

    def top_of(parts):
        return jnp.max(functools.reduce(jnp.maximum, parts), axis=1, keepdims=True)

    def mix(pattern, blocks, p):
        return jnp.dot(
            jnp.concatenate(p, 1).astype(jnp.bfloat16), rows_of(pattern, 1, blocks),
            preferred_element_type=jnp.float32,
        )

    def own_blocks(pattern, row):
        place = y if pattern == 0 else x
        item = (pattern * 4 + (x if pattern == 0 else y)) * 2 + row
        blocks = [(z * 4 + place) * 2 + i for i in range(row + 1)]
        parts = split(score(pattern, item, blocks))
        query_pos = lax.broadcasted_iota(jnp.int32, parts[0].shape, 0) & (BLOCK_TOKENS - 1)
        key_pos = lax.broadcasted_iota(jnp.int32, parts[0].shape, 1)
        parts[-1] = jnp.where(key_pos <= query_pos, parts[-1], NEG)
        m = top_of(parts)
        p = [jnp.exp2((v - m) * EXP_SCALE) for v in parts]
        m_ref[item] = jnp.broadcast_to(m, (QCOLS, HEAD_WIDTH))
        l_ref[item] = functools.reduce(jnp.add, p)
        acc_ref[item] = mix(pattern, blocks, p)

    def fetch(pattern, c):
        code = chunk_ref[c]
        item, i = code >> 4, code & 15
        at = base_of(pattern, item) + i * STEP
        blocks = [codes_ref[at + k] for k in range(STEP)]
        return item, blocks, count_ref[item] - i * STEP

    def absorb(pattern, s, item, blocks, left):
        parts = split(s)
        m_old = m_ref[item]
        m_new = jnp.maximum(m_old, top_of(parts))
        alpha = jnp.exp2((m_old - m_new) * EXP_SCALE)
        off = m_new * EXP_SCALE
        p = [
            jnp.exp2(v * EXP_SCALE - (off if i == 0 else off + jnp.where(left > i, 0.0, -NEG)))
            for i, v in enumerate(parts)
        ]
        m_ref[item] = m_new
        l_ref[item] = l_ref[item] * alpha + functools.reduce(jnp.add, p)
        acc_ref[item] = acc_ref[item] * alpha + mix(pattern, blocks, p)

    for pattern, begin, stop in ((0, 0, middle), (1, middle, end)):
        for c in loads(pattern):
            c.wait()
        if pattern == 0:
            for c in loads(1):
                c.start()
        for row in range(2):
            own_blocks(pattern, row)

        def several(j, carry, pattern=pattern, begin=begin):
            got = [fetch(pattern, begin + j * UNROLL + u) for u in range(UNROLL)]
            scores = [score(pattern, g[0], g[1]) for g in got]
            for g, s in zip(got, scores):
                absorb(pattern, s, *g)
            return carry

        def single(c, carry, pattern=pattern):
            g = fetch(pattern, c)
            absorb(pattern, score(pattern, g[0], g[1]), *g)
            return carry

        whole = (stop - begin) // UNROLL
        lax.fori_loop(0, whole, several, 0)
        lax.fori_loop(begin + whole * UNROLL, stop, single, 0)

    lane = lax.broadcasted_iota(jnp.int32, (BLOCK_TOKENS, BLOCK_TOKENS), 1)

    def close(item, carry):
        tops = jnp.zeros((BLOCK_TOKENS, BLOCK_TOKENS), jnp.float32)
        sums = jnp.zeros((BLOCK_TOKENS, BLOCK_TOKENS), jnp.float32)
        for g in range(GROUP):
            part = slice(g * HEAD_WIDTH, (g + 1) * HEAD_WIDTH)
            o_ref[item, :, part] = acc_ref[item, part].astype(jnp.bfloat16)
            tops = jnp.where(lane == g, m_ref[item, part], tops)
            sums = jnp.where(lane == g, jnp.sum(l_ref[item, part], axis=1, keepdims=True), sums)
        stat_ref[item, 0:8] = tops.T[:8] * EXP_SCALE
        stat_ref[item, 8:16] = sums.T[:8]
        return carry

    lax.fori_loop(0, ITEMS, close, 0, unroll=2)


def attend(codes, q, kv):
    any_spec = pl.BlockSpec(memory_space=pl.ANY)
    blocks = pl.BlockSpec(memory_space=pltpu.VMEM)
    state = pltpu.VMEM((ITEMS, QCOLS, HEAD_WIDTH), jnp.float32)
    return pl.pallas_call(
        attend_kernel,
        in_specs=[pl.BlockSpec(memory_space=pltpu.SMEM), any_spec, any_spec],
        out_specs=[blocks, blocks],
        out_shape=[
            jax.ShapeDtypeStruct((ITEMS, BLOCK_TOKENS, QCOLS), jnp.bfloat16),
            jax.ShapeDtypeStruct((ITEMS, 16, BLOCK_TOKENS), jnp.float32),
        ],
        scratch_shapes=[
            pltpu.SMEM((ITEMS,), jnp.int32),
            pltpu.SMEM((ITEMS * FMAX,), jnp.int32),
            pltpu.VMEM(q.shape, q.dtype),
            pltpu.VMEM(kv.shape, kv.dtype),
            state, state, state,
            pltpu.SemaphoreType.DMA((2, 2)),
        ],
        compiler_params=pltpu.CompilerParams(vmem_limit_bytes=40 * 1024 * 1024),
    )(codes, q, kv)


def columns(rows):
    rest = jnp.zeros((BLOCK_TOKENS - 8 * len(rows), BLOCK_TOKENS), jnp.float32)
    return jnp.concatenate([*rows, rest], 0).T


def combine(parts, w, g):
    cols = slice(g * HEAD_WIDTH, (g + 1) * HEAD_WIDTH)
    return sum(
        part[:, cols].astype(jnp.float32) * w[:, i * 8 + g : i * 8 + g + 1]
        for i, part in enumerate(parts)
    )


def return_kernel(
    o_in, stat_in, out_ref,
    o_got, stat_got, o_relay, stat_relay, o_mine, stat_mine, o_sum, stat_sum,
    send, recv, relay_send, relay_recv, own_sem,
):
    at = {"x": lax.axis_index("x"), "y": lax.axis_index("y")}
    core = lax.axis_index("head")
    axes = ("x", "y")

    def chip(p, step):
        return (at[axes[p]] + step) % 4

    barrier = pltpu.get_barrier_semaphore()
    met = [{axes[p]: chip(p, step), "head": k} for p in range(2) for step in (1, 3) for k in range(2)]
    met.append({"head": 1 - core})
    for device in met:
        pl.semaphore_signal(barrier, inc=1, device_id=device, device_id_type=pl.DeviceIdType.MESH)

    def item(p, step, row):
        return (p * 4 + chip(p, step)) * 2 + row

    def own_copies(p, row):
        i = item(p, 3 if row == 0 else 1, row)
        return [
            pltpu.make_async_copy(o_in.at[i], o_mine.at[p, row], own_sem.at[p, row, 0]),
            pltpu.make_async_copy(stat_in.at[i], stat_mine.at[p, row], own_sem.at[p, row, 1]),
        ]

    def kept_copies(p):
        i = item(p, 0, core)
        return [
            pltpu.make_async_copy(o_in.at[i], o_got.at[p, core, 2], own_sem.at[p, 2, 0]),
            pltpu.make_async_copy(stat_in.at[i], stat_got.at[p, core, 2], own_sem.at[p, 2, 1]),
        ]

    def relay_copies(p, row):
        i = item(p, 2, row)
        device = {axes[p]: chip(p, 3 if row == 0 else 1)}
        return [
            copy_to(src.at[i], dst.at[p, row], (relay_send.at[p, row, n], relay_recv.at[p, row, n]), device)
            for n, (src, dst) in enumerate(((o_in, o_relay), (stat_in, stat_relay)))
        ]

    def copies(p, place, row, o_src, stat_src, n):
        device = {"head": row} if place == 2 else {axes[p]: chip(p, 3 - 2 * place), "head": row}
        return [
            copy_to(src, dst.at[p, core, place], (send.at[p, n, k], recv.at[p, place, core, k]), device)
            for k, (src, dst) in enumerate(((o_src, o_got), (stat_src, stat_got)))
        ]

    def plain(p, place):
        row = (1, 0, 1 - core)[place]
        i = item(p, (3, 1, 0)[place], row)
        return copies(p, place, row, o_in.at[i], stat_in.at[i], place)

    def summed(p, row):
        return copies(p, row, row, o_sum.at[p, row], stat_sum.at[p, row], 3 + row)

    both = [(p, row) for row in range(2) for p in range(2)]
    for p, row in both:
        for c in own_copies(p, row):
            c.start()
    for p in range(2):
        for c in kept_copies(p):
            c.start()
    pl.semaphore_wait(barrier, len(met))
    for p, row in both:
        for c in relay_copies(p, row):
            c.start()
    for place in range(3):
        for p in range(2):
            for c in plain(p, place):
                c.start()
    for p, row in both:
        for c in own_copies(p, row):
            c.wait()
        for c in relay_copies(p, row):
            c.wait_recv()
        stats = [stat_mine[p, row], stat_relay[p, row]]
        top = jnp.maximum(stats[0][:8], stats[1][:8])
        f = [jnp.exp2(v[:8] - top) for v in stats]
        stat_sum[p, row, 0:8] = top
        stat_sum[p, row, 8:16] = stats[0][8:] * f[0] + stats[1][8:] * f[1]
        w = columns(f)
        for g in range(GROUP):
            cols = slice(g * HEAD_WIDTH, (g + 1) * HEAD_WIDTH)
            mixed = combine([o_mine.at[p, row], o_relay.at[p, row]], w, g)
            o_sum[p, row, :, cols] = mixed.astype(jnp.bfloat16)
        for c in summed(p, row):
            c.start()

    def arrival(p, place, c, k):
        dst = (o_got, stat_got)[k].at[p, c, place]
        return copy_to(dst, dst, (send.at[p, 0, k], recv.at[p, place, c, k]), {"head": 1 - core})

    for p in range(2):
        for c in kept_copies(p):
            c.wait()
        for k in range(2):
            arrival(p, 2, 1 - core, k).wait_recv()
            for c in range(2):
                for place in range(2):
                    arrival(p, place, c, k).wait_recv()
        for c in range(2):
            stats = [stat_got[p, c, i] for i in range(3)]
            top = functools.reduce(jnp.maximum, [v[:8] for v in stats])
            f = [jnp.exp2(v[:8] - top) for v in stats]
            total = functools.reduce(jnp.add, [v[8:] * u for v, u in zip(stats, f)])
            inv = 1.0 / jnp.where(total > 0, total, 1.0)
            w = columns([v * inv for v in f])
            for g in range(GROUP):
                start = (c * 2 + p) * QCOLS + g * HEAD_WIDTH
                mixed = combine([o_got.at[p, c, i] for i in range(3)], w, g)
                out_ref[:, start : start + HEAD_WIDTH] = mixed.astype(jnp.bfloat16)
    for p, row in both:
        for c in relay_copies(p, row) + summed(p, row):
            c.wait_send()
    for p in range(2):
        for place in range(3):
            for c in plain(p, place):
                c.wait_send()


def send_back(o, stats):
    dma = pltpu.SemaphoreType.DMA
    any_spec = pl.BlockSpec(memory_space=pl.ANY)
    partial, figures = (BLOCK_TOKENS, QCOLS), (16, BLOCK_TOKENS)
    pairs = [pltpu.VMEM((2, 2, *partial), jnp.bfloat16), pltpu.VMEM((2, 2, *figures), jnp.float32)]
    return pl.pallas_call(
        return_kernel,
        in_specs=[any_spec] * 2,
        out_specs=pl.BlockSpec(memory_space=pltpu.VMEM),
        out_shape=jax.ShapeDtypeStruct((BLOCK_TOKENS, 4 * QCOLS), jnp.bfloat16),
        scratch_shapes=[
            pltpu.VMEM((2, 2, 3, *partial), jnp.bfloat16),
            pltpu.VMEM((2, 2, 3, *figures), jnp.float32),
            *(pairs * 3),
            dma((2, 5, 2)), dma((2, 3, 2, 2)), dma((2, 2, 2)), dma((2, 2, 2)), dma((2, 3, 2)),
        ],
        compiler_params=pltpu.CompilerParams(
            collective_id=1, has_side_effects=True, vmem_limit_bytes=16 * 1024 * 1024
        ),
    )(o, stats)


def copy_to(src, dst, sems, device):
    return pltpu.make_async_remote_copy(
        src_ref=src, dst_ref=dst, send_sem=sems[0], recv_sem=sems[1],
        device_id=device, device_id_type=pl.DeviceIdType.MESH,
    )


MAIN = 3 * BLOCK_TOKENS
LAST = BLOCK_TOKENS
ORDER = (
    ("last near", 0, 0), ("last near", 0, 1), ("z", 1, 0), ("near", 0, 0), ("near", 0, 1),
    ("z", 1, 1), ("z", 2, 0), ("z", 2, 1), ("q", 0, 1), ("q", 0, 0), ("last far", 0, 0),
    ("z", 3, 0), ("last far", 0, 1), ("near", 1, 0), ("z", 3, 1), ("near", 1, 1), ("near", 2, 0),
    ("last z", 1, 0), ("near", 2, 1), ("z", 4, 0), ("near", 3, 0), ("near", 3, 1),
    ("last z", 1, 1), ("near", 4, 0), ("near", 4, 1), ("z", 4, 1), ("last z", 2, 0),
    ("near", 5, 0), ("near", 5, 1), ("last z", 2, 1), ("near", 6, 0), ("near", 6, 1),
    ("last z", 3, 0), ("last z", 3, 1), ("near", 7, 0), ("last z", 4, 0), ("near", 7, 1),
    ("last z", 4, 1),
)


def gather_kernel(
    q_hbm, k_hbm, v_hbm, owners_hbm, pairs_hbm, counts_hbm, q_all, kv_all, meta_all,
    q_in, k_in, v_in, owners_in, pairs_in, counts_in, q_own, kv_own, meta_own, in_sem, local_sem,
    z_send, z_recv, near_send, near_recv, far_send, far_recv,
    lz_send, lz_recv, ln_send, ln_recv, lf_send, lf_recv,
    q_send, q_recv, qf_send, qf_recv, t_send, t_recv,
):
    at = {a: lax.axis_index(a) for a in ("y", "z", "x")}
    size = {"y": NY, "z": NZ, "x": NX}
    ring = {a: ((at[a] + 1) % size[a], (at[a] + size[a] - 1) % size[a]) for a in at}

    barrier = pltpu.get_barrier_semaphore()
    for a in at:
        for n in ring[a]:
            pl.semaphore_signal(
                barrier, inc=1, device_id={a: n}, device_id_type=pl.DeviceIdType.MESH
            )

    loads = [
        pltpu.make_async_copy(src, dst, in_sem.at[i])
        for i, (src, dst) in enumerate(
            (
                (k_hbm, k_in), (v_hbm, v_in), (q_hbm, q_in),
                (owners_hbm, owners_in), (pairs_hbm, pairs_in), (counts_hbm, counts_in),
            )
        )
    ]
    for c in loads:
        c.start()

    side = ("y", "x")
    cross = ("x", "y")

    def slot(h, place, zo):
        return zo * 4 + place

    local = []

    def keep(src, dst):
        c = pltpu.make_async_copy(src, dst, local_sem.at[len(local)])
        c.start()
        local.append(c)

    sends = []

    def part(d):
        return pl.ds(d * (MAIN // 2), MAIN // 2)

    def z_copy(d, s, h):
        back = at["z"] - (s - 1) if d == 0 else at["z"] + (s - 1)
        rows = part(d) if s == 4 else pl.ds(0, MAIN)
        ref = kv_all.at[h, slot(h, at[side[h]], (back + NZ) % NZ), rows]
        i = (d * 4 + s - 1) * 2 + h
        src = kv_own.at[h, rows] if s == 1 else ref
        return copy_to(src, ref, (z_send.at[i], z_recv.at[i]), {"z": ring["z"][d]})

    def near_copy(h, i, zo, d):
        rows = pl.ds(0, MAIN)
        ref = kv_all.at[h, slot(h, at[side[h]], zo), rows]
        n = (h * 8 + i) * 2 + d
        src = kv_own.at[h, rows] if i == 0 else ref
        return copy_to(src, ref, (near_send.at[n], near_recv.at[n]), {side[h]: ring[side[h]][d]})

    def far_copy(h, i, zo, d):
        a = side[h]
        ref = kv_all.at[h, slot(h, ring[a][1 - d], zo), part(d)]
        n = (h * 8 + i) * 2 + d
        return copy_to(ref, ref, (far_send.at[n], far_recv.at[n]), {a: ring[a][d]})

    def last_near(h, d):
        a = side[h]
        rows = pl.ds(MAIN, LAST)
        ref = kv_all.at[h, slot(h, at[a], at["z"]), rows]
        n = h * 2 + d
        return copy_to(kv_own.at[h, rows], ref, (ln_send.at[n], ln_recv.at[n]), {a: ring[a][d]})

    def last_far(h, d):
        a = side[h]
        rows = pl.ds(MAIN + d * (LAST // 2), LAST // 2)
        ref = kv_all.at[h, slot(h, ring[a][1 - d], at["z"]), rows]
        n = h * 2 + d
        return copy_to(ref, ref, (lf_send.at[n], lf_recv.at[n]), {a: ring[a][d]})

    def last_z(d, s, h):
        back = at["z"] - (s - 1) if d == 0 else at["z"] + (s - 1)
        first = ((back + NZ) % NZ) * 4
        places = pl.ds(first + 2 * d, 2) if s == 4 else pl.ds(first, 4)
        ref = kv_all.at[h, places, pl.ds(MAIN, LAST)]
        i = (d * 4 + s - 1) * 2 + h
        return copy_to(ref, ref, (lz_send.at[i], lz_recv.at[i]), {"z": ring["z"][d]})

    def q_copy(h, d):
        a = cross[h]
        ref = q_all.at[h, at[a]]
        return copy_to(
            q_own.at[h], ref, (q_send.at[h * 2 + d], q_recv.at[h * 2 + d]), {a: ring[a][d]}
        )

    def qf_copy(h, d):
        a = cross[h]
        ref = q_all.at[h, ring[a][1 - d], pl.ds(d * BLOCK_TOKENS, BLOCK_TOKENS)]
        return copy_to(
            ref, ref, (qf_send.at[h * 2 + d], qf_recv.at[h * 2 + d]), {a: ring[a][d]}
        )

    def t_copy(h, d, relay):
        a = cross[h]
        ref = meta_all.at[h, ring[a][1 - d] if relay else at[a]]
        i = (h * 2 + d) * 2 + relay
        return copy_to(
            ref if relay else meta_own.at[h], ref, (t_send.at[i], t_recv.at[i]), {a: ring[a][d]}
        )

    def start(c):
        c.start()
        sends.append(c)

    both = [(h, d) for h in range(2) for d in range(2)]
    zs = [at["z"]]
    for s in range(1, 5):
        zs.append((at["z"] - s + NZ) % NZ)
        zs.append((at["z"] + s) % NZ)
    zs = zs[:8]

    for i, ref in enumerate((k_in, v_in)):
        loads[i].wait()
        for h in range(2):
            kv_own[h, i * 256 : i * 256 + 256] = ref[:, h * HEAD_WIDTH : (h + 1) * HEAD_WIDTH]
    pl.semaphore_wait(barrier, 6)
    for h, d in both:
        start(z_copy(d, 1, h))
    for h, d in both:
        start(last_near(h, d))
    for h, d in both:
        start(near_copy(h, 0, zs[0], d))
    for h in range(2):
        keep(kv_own.at[h], kv_all.at[h, slot(h, at[side[h]], at["z"])])
    loads[2].wait()
    for h in range(2):
        q_own[h] = q_in[:, h * QCOLS : (h + 1) * QCOLS]
    for h, d in both:
        start(q_copy(h, d))

    for c in loads[3:]:
        c.wait()
    meta_own[...] = jnp.zeros_like(meta_own)
    meta_own[0, 0:2, 0:FMAX] = owners_in[...]
    owners = meta_own[0]
    shard = (at["y"] * NZ + at["z"]) * NX + at["x"]
    listed = pairs_in[pl.ds(jnp.minimum(shard, SHARDS - 1 - shard), 1), :]
    half = jnp.take_along_axis(jnp.broadcast_to(listed, (8, 128)), owners, axis=1) & 1
    row = lax.broadcasted_iota(jnp.int32, (8, 128), 0)
    lane = lax.broadcasted_iota(jnp.int32, (8, 128), 1)
    count = jnp.where(row == 0, counts_in[0], jnp.where(row == 1, counts_in[1], 0))
    place, rest = lane >> 4, lane & (FMAX - 1)
    lists = [jnp.zeros((8, 128), jnp.int32)] * 2
    found = [jnp.zeros((8, 128), jnp.int32)] * 2
    for j in range(FMAX):
        owner, which, live = (
            jnp.sum(jnp.where(lane == j, v, 0), axis=1, keepdims=True)
            for v in (owners, half, (lane < count).astype(jnp.int32))
        )
        oy, oz, ox = owner >> 5, (owner >> 2) & 7, owner & 3
        for h, (holder, spot) in enumerate(((ox, oy), (oy, ox))):
            hit = jnp.logical_and(holder == place, live > 0)
            put = jnp.logical_and(hit, jnp.logical_or(found[h] == 0, found[h] == rest))
            lists[h] = jnp.where(put, oz * 8 + spot * 2 + which, lists[h])
            found[h] = found[h] + hit.astype(jnp.int32)
    for h in range(2):
        meta_own[h, 0:2] = lists[h][0:2]
        meta_own[h, 2:4] = found[h][0:2]
    for h, d in both:
        start(t_copy(h, d, 0))
    for h in range(2):
        keep(q_own.at[h], q_all.at[h, at[cross[h]]])
        keep(meta_own.at[h], meta_all.at[h, at[cross[h]]])

    def arrived(kind, i, h):
        for d in range(2):
            if kind == "z":
                z_copy(d, i, h).wait_recv()
                if i < 4:
                    start(z_copy(d, i + 1, h))
                    for e in range(2):
                        start(near_copy(h, 2 * i - 1 + d, zs[2 * i - 1 + d], e))
                elif d == 1:
                    for e in range(2):
                        start(near_copy(h, 7, zs[7], e))
            elif kind == "near":
                near_copy(h, i, zs[i], d).wait_recv()
                start(far_copy(h, i, zs[i], d))
            elif kind == "q":
                q_copy(h, d).wait_recv()
                start(qf_copy(h, d))
            elif kind == "last near":
                last_near(h, d).wait_recv()
                start(last_far(h, d))
            elif kind == "last far":
                last_far(h, d).wait_recv()
                if d == 1:
                    local[h].wait()
                    for e in range(2):
                        start(last_z(e, 1, h))
            else:
                last_z(d, i, h).wait_recv()
                if i < 4:
                    start(last_z(d, i + 1, h))

    for event in ORDER:
        arrived(*event)
    for h in range(2):
        for d in range(2):
            t_copy(h, d, 0).wait_recv()
        start(t_copy(h, 0, 1))
    for h, d in both:
        qf_copy(h, d).wait_recv()
        for i in range(8):
            far_copy(h, i, zs[i], d).wait_recv()
    for h in range(2):
        t_copy(h, 0, 1).wait_recv()
    for c in sends:
        c.wait_send()
    for c in local[2:]:
        c.wait()


def gather_all(q, k, v, owners, counts, pairs):
    dma = pltpu.SemaphoreType.DMA
    any_spec = pl.BlockSpec(memory_space=pl.ANY)
    arrays = [pltpu.with_memory_space_constraint(a, pltpu.HBM) for a in (q, k, v, owners, pairs, counts)]
    return pl.pallas_call(
        gather_kernel,
        in_specs=[any_spec] * 6,
        out_specs=[any_spec] * 3,
        out_shape=[
            jax.ShapeDtypeStruct((2, 4, 2 * BLOCK_TOKENS, QCOLS), jnp.bfloat16),
            jax.ShapeDtypeStruct((2, SLOTS, MAIN + LAST, HEAD_WIDTH), jnp.bfloat16),
            jax.ShapeDtypeStruct((2, 4, 8, 128), jnp.int32),
        ],
        scratch_shapes=[pltpu.VMEM(a.shape, a.dtype) for a in (q, k, v, owners, pairs)]
        + [
            pltpu.SMEM(counts.shape, counts.dtype),
            pltpu.VMEM((2, 2 * BLOCK_TOKENS, QCOLS), jnp.bfloat16),
            pltpu.VMEM((2, MAIN + LAST, HEAD_WIDTH), jnp.bfloat16),
            pltpu.VMEM((2, 8, 128), jnp.int32),
        ]
        + [dma((n,)) for n in (6, 6, 16, 16, 32, 32, 32, 32, 16, 16, 4, 4, 4, 4, 4, 4, 4, 4, 8, 8)],
        compiler_params=pltpu.CompilerParams(
            collective_id=0, has_side_effects=True, vmem_limit_bytes=16 * 1024 * 1024
        ),
    )(*arrays)


def on_device(queries, keys, values, far_owners, far_counts, pair_blocks):
    q, kv, codes = gather_all(queries, keys, values, far_owners, far_counts, pair_blocks)
    o, stats = attend(codes.reshape(-1), q, kv)
    return send_back(o, stats)


def solution(mesh):
    grid = Mesh(mesh.devices.reshape(NY, NZ, NX, 2), ("y", "z", "x", "head"))
    ctx = ("y", "z", "x")
    placed = (P(ctx, "head"), P(ctx, "head"), P(ctx, "head"), P(ctx, None), P(ctx), P())
    return jax.shard_map(
        on_device,
        mesh=grid,
        in_specs=placed,
        out_specs=P((*ctx, "head"), None),
        check_vma=False,
    )
```

```python
import functools

import jax
import jax.numpy as jnp
from jax import lax
from jax.experimental import pallas as pl
from jax.experimental.pallas import tpu as pltpu
from jax.sharding import Mesh, PartitionSpec as P

HEAD_WIDTH = 128
BLOCK_TOKENS = 128
GROUP = 5
QCOLS = GROUP * HEAD_WIDTH
NY, NZ, NX = 4, 8, 4
SHARDS = NY * NZ * NX
FMAX = 16
SLOTS = 32
ITEMS = 16
STEP = 2
UNROLL = 4
NEG = -1e30
EXP_SCALE = 1.4426950408889634 * HEAD_WIDTH ** (-0.5)


def attend_kernel(
    codes_ref, q_in, kv_in, o_ref, stat_ref,
    count_ref, chunk_ref, q_ref, kv_ref, acc_ref, m_ref, l_ref, sem,
):
    y, z, x = (lax.axis_index(a) for a in ("y", "z", "x"))

    def loads(pattern):
        return [
            pltpu.make_async_copy(src.at[pattern], dst.at[pattern], sem.at[i, pattern])
            for i, (src, dst) in enumerate(((q_in, q_ref), (kv_in, kv_ref)))
        ]

    for c in loads(0):
        c.start()

    def base_of(pattern, item):
        return (item >> 1) * 1024 + (item & 1) * 128 + (x if pattern == 0 else y) * FMAX

    def build(pattern, item, chunks):
        n = codes_ref[base_of(pattern, item) + 2 * 128]
        count_ref[item] = n

        def note(i, chunks):
            chunk_ref[chunks] = item * 16 + i
            return chunks + 1

        return lax.fori_loop(0, (n + STEP - 1) // STEP, note, chunks)

    middle = lax.fori_loop(0, 8, functools.partial(build, 0), jnp.int32(0))
    end = lax.fori_loop(8, 16, functools.partial(build, 1), middle)

    def clear(item, carry):
        @pl.when(((item >> 1) & 3) != jnp.where(item < 8, x, y))
        def _():
            m_ref[item] = jnp.full((QCOLS, HEAD_WIDTH), NEG, jnp.float32)
            l_ref[item] = jnp.zeros((QCOLS, HEAD_WIDTH), jnp.float32)
            acc_ref[item] = jnp.zeros((QCOLS, HEAD_WIDTH), jnp.float32)

        return carry

    lax.fori_loop(0, ITEMS, clear, 0)

    def score(pattern, item, blocks):
        tokens = pl.ds(pl.multiple_of((item & 1) * BLOCK_TOKENS, BLOCK_TOKENS), BLOCK_TOKENS)
        q = q_ref.at[pattern, (item >> 1) & 3, tokens]
        heads = [q[:, g * HEAD_WIDTH : (g + 1) * HEAD_WIDTH] for g in range(GROUP)]
        return lax.dot_general(
            jnp.concatenate(heads, 0), rows_of(pattern, 0, blocks), (((1,), (1,)), ((), ())),
            preferred_element_type=jnp.float32,
        )

    def rows_of(pattern, kind, blocks):
        starts = [
            pl.multiple_of((2 * kind + (b & 1)) * BLOCK_TOKENS, BLOCK_TOKENS) for b in blocks
        ]
        return jnp.concatenate(
            [kv_ref[pattern, b >> 1, pl.ds(i, BLOCK_TOKENS)] for b, i in zip(blocks, starts)], 0
        )

    def split(s):
        return [
            s[:, i : i + BLOCK_TOKENS] for i in range(0, s.shape[1], BLOCK_TOKENS)
        ]

    def top_of(parts):
        return jnp.max(functools.reduce(jnp.maximum, parts), axis=1, keepdims=True)

    def mix(pattern, blocks, p):
        return jnp.dot(
            jnp.concatenate(p, 1).astype(jnp.bfloat16), rows_of(pattern, 1, blocks),
            preferred_element_type=jnp.float32,
        )

    def own_blocks(pattern, row):
        place = y if pattern == 0 else x
        item = (pattern * 4 + (x if pattern == 0 else y)) * 2 + row
        blocks = [(z * 4 + place) * 2 + i for i in range(row + 1)]
        parts = split(score(pattern, item, blocks))
        query_pos = lax.broadcasted_iota(jnp.int32, parts[0].shape, 0) & (BLOCK_TOKENS - 1)
        key_pos = lax.broadcasted_iota(jnp.int32, parts[0].shape, 1)
        parts[-1] = jnp.where(key_pos <= query_pos, parts[-1], NEG)
        m = top_of(parts)
        p = [jnp.exp2((v - m) * EXP_SCALE) for v in parts]
        m_ref[item] = jnp.broadcast_to(m, (QCOLS, HEAD_WIDTH))
        l_ref[item] = functools.reduce(jnp.add, p)
        acc_ref[item] = mix(pattern, blocks, p)

    def fetch(pattern, c):
        code = chunk_ref[c]
        item, i = code >> 4, code & 15
        at = base_of(pattern, item) + i * STEP
        blocks = [codes_ref[at + k] for k in range(STEP)]
        return item, blocks, count_ref[item] - i * STEP

    def absorb(pattern, s, item, blocks, left):
        parts = split(s)
        m_old = m_ref[item]
        m_new = jnp.maximum(m_old, top_of(parts))
        alpha = jnp.exp2((m_old - m_new) * EXP_SCALE)
        off = m_new * EXP_SCALE
        p = [
            jnp.exp2(v * EXP_SCALE - (off if i == 0 else off + jnp.where(left > i, 0.0, -NEG)))
            for i, v in enumerate(parts)
        ]
        m_ref[item] = m_new
        l_ref[item] = l_ref[item] * alpha + functools.reduce(jnp.add, p)
        acc_ref[item] = acc_ref[item] * alpha + mix(pattern, blocks, p)

    for pattern, begin, stop in ((0, 0, middle), (1, middle, end)):
        for c in loads(pattern):
            c.wait()
        if pattern == 0:
            for c in loads(1):
                c.start()
        for row in range(2):
            own_blocks(pattern, row)

        for width in (UNROLL, 2, 1):

            def several(j, carry, pattern=pattern, begin=begin, width=width):
                got = [fetch(pattern, begin + j * width + u) for u in range(width)]
                scores = [score(pattern, g[0], g[1]) for g in got]
                for g, s in zip(got, scores):
                    absorb(pattern, s, *g)
                return carry

            turns = (stop - begin) // width
            lax.fori_loop(0, turns, several, 0)
            begin = begin + turns * width

    lane = lax.broadcasted_iota(jnp.int32, (BLOCK_TOKENS, BLOCK_TOKENS), 1)

    def close(item, carry):
        tops = jnp.zeros((BLOCK_TOKENS, BLOCK_TOKENS), jnp.float32)
        sums = jnp.zeros((BLOCK_TOKENS, BLOCK_TOKENS), jnp.float32)
        for g in range(GROUP):
            part = slice(g * HEAD_WIDTH, (g + 1) * HEAD_WIDTH)
            o_ref[item, :, part] = acc_ref[item, part].astype(jnp.bfloat16)
            tops = jnp.where(lane == g, m_ref[item, part], tops)
            sums = jnp.where(lane == g, jnp.sum(l_ref[item, part], axis=1, keepdims=True), sums)
        stat_ref[item, 0:8] = tops.T[:8] * EXP_SCALE
        stat_ref[item, 8:16] = sums.T[:8]
        return carry

    lax.fori_loop(0, ITEMS, close, 0, unroll=2)


def attend(codes, q, kv):
    any_spec = pl.BlockSpec(memory_space=pl.ANY)
    blocks = pl.BlockSpec(memory_space=pltpu.VMEM)
    state = pltpu.VMEM((ITEMS, QCOLS, HEAD_WIDTH), jnp.float32)
    return pl.pallas_call(
        attend_kernel,
        in_specs=[pl.BlockSpec(memory_space=pltpu.SMEM), any_spec, any_spec],
        out_specs=[blocks, blocks],
        out_shape=[
            jax.ShapeDtypeStruct((ITEMS, BLOCK_TOKENS, QCOLS), jnp.bfloat16),
            jax.ShapeDtypeStruct((ITEMS, 16, BLOCK_TOKENS), jnp.float32),
        ],
        scratch_shapes=[
            pltpu.SMEM((ITEMS,), jnp.int32),
            pltpu.SMEM((ITEMS * FMAX,), jnp.int32),
            pltpu.VMEM(q.shape, q.dtype),
            pltpu.VMEM(kv.shape, kv.dtype),
            state, state, state,
            pltpu.SemaphoreType.DMA((2, 2)),
        ],
        compiler_params=pltpu.CompilerParams(vmem_limit_bytes=40 * 1024 * 1024),
    )(codes, q, kv)


def columns(rows):
    rest = jnp.zeros((BLOCK_TOKENS - 8 * len(rows), BLOCK_TOKENS), jnp.float32)
    return jnp.concatenate([*rows, rest], 0).T


def combine(parts, w, g):
    cols = slice(g * HEAD_WIDTH, (g + 1) * HEAD_WIDTH)
    return sum(
        part[:, cols].astype(jnp.float32) * w[:, i * 8 + g : i * 8 + g + 1]
        for i, part in enumerate(parts)
    )


def return_kernel(
    o_in, stat_in, out_ref,
    o_got, stat_got, o_early, o_relay, stat_relay, o_mine, stat_mine, o_sum, stat_sum,
    send, recv, relay_send, relay_recv, own_sem,
):
    at = {"x": lax.axis_index("x"), "y": lax.axis_index("y")}
    core = lax.axis_index("head")
    axes = ("x", "y")

    def chip(p, step):
        return (at[axes[p]] + step) % 4

    barrier = pltpu.get_barrier_semaphore()
    met = [{axes[p]: chip(p, step), "head": k} for p in range(2) for step in (1, 3) for k in range(2)]
    met.append({"head": 1 - core})
    for device in met:
        pl.semaphore_signal(barrier, inc=1, device_id=device, device_id_type=pl.DeviceIdType.MESH)

    def item(p, step, row):
        return (p * 4 + chip(p, step)) * 2 + row

    def own_copies(p, row):
        i = item(p, 3 if row == 0 else 1, row)
        return [
            pltpu.make_async_copy(o_in.at[i], o_mine.at[p, row], own_sem.at[p, row, 0]),
            pltpu.make_async_copy(stat_in.at[i], stat_mine.at[p, row], own_sem.at[p, row, 1]),
        ]

    def kept_copies(p):
        i = item(p, 0, core)
        return [
            pltpu.make_async_copy(o_in.at[i], o_got.at[p, core, 2], own_sem.at[p, 2, 0]),
            pltpu.make_async_copy(stat_in.at[i], stat_got.at[p, core, 2], own_sem.at[p, 2, 1]),
        ]

    def relay_copies(p, row):
        i = item(p, 2, row)
        device = {axes[p]: chip(p, 3 if row == 0 else 1)}
        return [
            copy_to(src.at[i], dst.at[p, row], (relay_send.at[p, row, n], relay_recv.at[p, row, n]), device)
            for n, (src, dst) in enumerate(((o_in, o_relay), (stat_in, stat_relay)))
        ]

    def copies(p, place, row, o_src, stat_src, n):
        device = {"head": row} if place == 2 else {axes[p]: chip(p, 3 - 2 * place), "head": row}
        return [
            copy_to(src, dst.at[p, core, place], (send.at[p, n, k], recv.at[p, place, core, k]), device)
            for k, (src, dst) in enumerate(((o_src, o_got), (stat_src, stat_got)))
        ]

    def plain(p, place):
        row = (1, 0, 1 - core)[place]
        i = item(p, (3, 1, 0)[place], row)
        return copies(p, place, row, o_in.at[i], stat_in.at[i], place)

    def summed(p, row):
        return copies(p, row, row, o_sum.at[p, row], stat_sum.at[p, row], 3 + row)

    both = [(p, row) for row in range(2) for p in range(2)]
    for p, row in both:
        for c in own_copies(p, row):
            c.start()
    for p in range(2):
        for c in kept_copies(p):
            c.start()
    pl.semaphore_wait(barrier, len(met))
    for p, row in both:
        for c in relay_copies(p, row):
            c.start()
    for place in range(3):
        for p in range(2):
            for c in plain(p, place):
                c.start()
    for p, row in both:
        for c in own_copies(p, row):
            c.wait()
        for c in relay_copies(p, row):
            c.wait_recv()
        stats = [stat_mine[p, row], stat_relay[p, row]]
        top = jnp.maximum(stats[0][:8], stats[1][:8])
        f = [jnp.exp2(v[:8] - top) for v in stats]
        stat_sum[p, row, 0:8] = top
        stat_sum[p, row, 8:16] = stats[0][8:] * f[0] + stats[1][8:] * f[1]
        w = columns(f)
        for g in range(GROUP):
            cols = slice(g * HEAD_WIDTH, (g + 1) * HEAD_WIDTH)
            mixed = combine([o_mine.at[p, row], o_relay.at[p, row]], w, g)
            o_sum[p, row, :, cols] = mixed.astype(jnp.bfloat16)
        for c in summed(p, row):
            c.start()

    def arrival(p, place, c, k):
        dst = (o_got, stat_got)[k].at[p, c, place]
        return copy_to(dst, dst, (send.at[p, 0, k], recv.at[p, place, c, k]), {"head": 1 - core})

    tops, sums = {}, {}
    for p in range(2):
        for c in kept_copies(p):
            c.wait()
        for k in range(2):
            arrival(p, 2, 1 - core, k).wait_recv()
            for c in range(2):
                arrival(p, 1 - core, c, k).wait_recv()
        for c in range(2):
            stats = [stat_got[p, c, 2], stat_got[p, c, 1 - core]]
            tops[p, c] = jnp.maximum(stats[0][:8], stats[1][:8])
            f = [jnp.exp2(v[:8] - tops[p, c]) for v in stats]
            sums[p, c] = stats[0][8:] * f[0] + stats[1][8:] * f[1]
            w = columns(f)
            for g in range(GROUP):
                cols = slice(g * HEAD_WIDTH, (g + 1) * HEAD_WIDTH)
                o_early[p, c, :, cols] = combine(
                    [o_got.at[p, c, 2], o_got.at[p, c, 1 - core]], w, g
                )
    for p in range(2):
        for c in range(2):
            for k in range(2):
                arrival(p, core, c, k).wait_recv()
            stat = stat_got[p, c, core]
            top = jnp.maximum(tops[p, c], stat[:8])
            f = [jnp.exp2(tops[p, c] - top), jnp.exp2(stat[:8] - top)]
            total = sums[p, c] * f[0] + stat[8:] * f[1]
            inv = 1.0 / jnp.where(total > 0, total, 1.0)
            w = columns([v * inv for v in f])
            for g in range(GROUP):
                start = (c * 2 + p) * QCOLS + g * HEAD_WIDTH
                mixed = combine([o_early.at[p, c], o_got.at[p, c, core]], w, g)
                out_ref[:, start : start + HEAD_WIDTH] = mixed.astype(jnp.bfloat16)
    for p, row in both:
        for c in relay_copies(p, row) + summed(p, row):
            c.wait_send()
    for p in range(2):
        for place in range(3):
            for c in plain(p, place):
                c.wait_send()


def send_back(o, stats):
    dma = pltpu.SemaphoreType.DMA
    any_spec = pl.BlockSpec(memory_space=pl.ANY)
    partial, figures = (BLOCK_TOKENS, QCOLS), (16, BLOCK_TOKENS)
    pairs = [pltpu.VMEM((2, 2, *partial), jnp.bfloat16), pltpu.VMEM((2, 2, *figures), jnp.float32)]
    return pl.pallas_call(
        return_kernel,
        in_specs=[any_spec] * 2,
        out_specs=pl.BlockSpec(memory_space=pltpu.VMEM),
        out_shape=jax.ShapeDtypeStruct((BLOCK_TOKENS, 4 * QCOLS), jnp.bfloat16),
        scratch_shapes=[
            pltpu.VMEM((2, 2, 3, *partial), jnp.bfloat16),
            pltpu.VMEM((2, 2, 3, *figures), jnp.float32),
            pltpu.VMEM((2, 2, *partial), jnp.float32),
            *(pairs * 3),
            dma((2, 5, 2)), dma((2, 3, 2, 2)), dma((2, 2, 2)), dma((2, 2, 2)), dma((2, 3, 2)),
        ],
        compiler_params=pltpu.CompilerParams(
            collective_id=1, has_side_effects=True, vmem_limit_bytes=16 * 1024 * 1024
        ),
    )(o, stats)


def copy_to(src, dst, sems, device):
    return pltpu.make_async_remote_copy(
        src_ref=src, dst_ref=dst, send_sem=sems[0], recv_sem=sems[1],
        device_id=device, device_id_type=pl.DeviceIdType.MESH,
    )


MAIN = 3 * BLOCK_TOKENS
LAST = BLOCK_TOKENS
ORDER = (
    ("last near", 0, 0), ("last near", 0, 1), ("z", 1, 0), ("near", 0, 0), ("near", 0, 1),
    ("z", 1, 1), ("z", 2, 0), ("z", 2, 1), ("q", 0, 1), ("q", 0, 0), ("last far", 0, 0),
    ("z", 3, 0), ("last far", 0, 1), ("near", 1, 0), ("z", 3, 1), ("near", 1, 1), ("near", 2, 0),
    ("last z", 1, 0), ("near", 2, 1), ("z", 4, 0), ("near", 3, 0), ("near", 3, 1),
    ("last z", 1, 1), ("near", 4, 0), ("near", 4, 1), ("z", 4, 1), ("last z", 2, 0),
    ("near", 5, 0), ("near", 5, 1), ("last z", 2, 1), ("near", 6, 0), ("near", 6, 1),
    ("last z", 3, 0), ("last z", 3, 1), ("near", 7, 0), ("last z", 4, 0), ("near", 7, 1),
    ("last z", 4, 1),
)


def gather_kernel(
    q_hbm, k_hbm, v_hbm, owners_hbm, pairs_hbm, counts_hbm, q_all, kv_all, meta_all,
    q_in, k_in, v_in, owners_in, pairs_in, counts_in, q_own, kv_own, meta_own, in_sem, local_sem,
    z_send, z_recv, near_send, near_recv, far_send, far_recv,
    lz_send, lz_recv, ln_send, ln_recv, lf_send, lf_recv,
    q_send, q_recv, qf_send, qf_recv, t_send, t_recv,
):
    at = {a: lax.axis_index(a) for a in ("y", "z", "x")}
    size = {"y": NY, "z": NZ, "x": NX}
    ring = {a: ((at[a] + 1) % size[a], (at[a] + size[a] - 1) % size[a]) for a in at}

    barrier = pltpu.get_barrier_semaphore()
    for a in at:
        for n in ring[a]:
            pl.semaphore_signal(
                barrier, inc=1, device_id={a: n}, device_id_type=pl.DeviceIdType.MESH
            )

    loads = [
        pltpu.make_async_copy(src, dst, in_sem.at[i])
        for i, (src, dst) in enumerate(
            (
                (k_hbm, k_in), (v_hbm, v_in), (q_hbm, q_in),
                (owners_hbm, owners_in), (pairs_hbm, pairs_in), (counts_hbm, counts_in),
            )
        )
    ]
    for c in loads:
        c.start()

    side = ("y", "x")
    cross = ("x", "y")

    def slot(h, place, zo):
        return zo * 4 + place

    local = []

    def keep(src, dst):
        c = pltpu.make_async_copy(src, dst, local_sem.at[len(local)])
        c.start()
        local.append(c)

    sends = []

    def part(d):
        return pl.ds(d * (MAIN // 2), MAIN // 2)

    def z_copy(d, s, h):
        back = at["z"] - (s - 1) if d == 0 else at["z"] + (s - 1)
        rows = part(d) if s == 4 else pl.ds(0, MAIN)
        ref = kv_all.at[h, slot(h, at[side[h]], (back + NZ) % NZ), rows]
        i = (d * 4 + s - 1) * 2 + h
        src = kv_own.at[h, rows] if s == 1 else ref
        return copy_to(src, ref, (z_send.at[i], z_recv.at[i]), {"z": ring["z"][d]})

    def near_copy(h, i, zo, d):
        rows = pl.ds(0, MAIN)
        ref = kv_all.at[h, slot(h, at[side[h]], zo), rows]
        n = (h * 8 + i) * 2 + d
        src = kv_own.at[h, rows] if i == 0 else ref
        return copy_to(src, ref, (near_send.at[n], near_recv.at[n]), {side[h]: ring[side[h]][d]})

    def far_copy(h, i, zo, d):
        a = side[h]
        ref = kv_all.at[h, slot(h, ring[a][1 - d], zo), part(d)]
        n = (h * 8 + i) * 2 + d
        return copy_to(ref, ref, (far_send.at[n], far_recv.at[n]), {a: ring[a][d]})

    def last_near(h, d):
        a = side[h]
        rows = pl.ds(MAIN, LAST)
        ref = kv_all.at[h, slot(h, at[a], at["z"]), rows]
        n = h * 2 + d
        return copy_to(kv_own.at[h, rows], ref, (ln_send.at[n], ln_recv.at[n]), {a: ring[a][d]})

    def last_far(h, d):
        a = side[h]
        rows = pl.ds(MAIN + d * (LAST // 2), LAST // 2)
        ref = kv_all.at[h, slot(h, ring[a][1 - d], at["z"]), rows]
        n = h * 2 + d
        return copy_to(ref, ref, (lf_send.at[n], lf_recv.at[n]), {a: ring[a][d]})

    def last_z(d, s, h):
        back = at["z"] - (s - 1) if d == 0 else at["z"] + (s - 1)
        first = ((back + NZ) % NZ) * 4
        places = pl.ds(first + 2 * d, 2) if s == 4 else pl.ds(first, 4)
        ref = kv_all.at[h, places, pl.ds(MAIN, LAST)]
        i = (d * 4 + s - 1) * 2 + h
        return copy_to(ref, ref, (lz_send.at[i], lz_recv.at[i]), {"z": ring["z"][d]})

    def q_copy(h, d):
        a = cross[h]
        ref = q_all.at[h, at[a]]
        return copy_to(
            q_own.at[h], ref, (q_send.at[h * 2 + d], q_recv.at[h * 2 + d]), {a: ring[a][d]}
        )

    def qf_copy(h, d):
        a = cross[h]
        ref = q_all.at[h, ring[a][1 - d], pl.ds(d * BLOCK_TOKENS, BLOCK_TOKENS)]
        return copy_to(
            ref, ref, (qf_send.at[h * 2 + d], qf_recv.at[h * 2 + d]), {a: ring[a][d]}
        )

    def t_copy(h, d, relay):
        a = cross[h]
        ref = meta_all.at[h, ring[a][1 - d] if relay else at[a]]
        i = (h * 2 + d) * 2 + relay
        return copy_to(
            ref if relay else meta_own.at[h], ref, (t_send.at[i], t_recv.at[i]), {a: ring[a][d]}
        )

    def start(c):
        c.start()
        sends.append(c)

    both = [(h, d) for h in range(2) for d in range(2)]
    zs = [at["z"]]
    for s in range(1, 5):
        zs.append((at["z"] - s + NZ) % NZ)
        zs.append((at["z"] + s) % NZ)
    zs = zs[:8]

    for i, ref in enumerate((k_in, v_in)):
        loads[i].wait()
        for h in range(2):
            kv_own[h, i * 256 : i * 256 + 256] = ref[:, h * HEAD_WIDTH : (h + 1) * HEAD_WIDTH]
    pl.semaphore_wait(barrier, 6)
    for h, d in both:
        start(z_copy(d, 1, h))
    for h, d in both:
        start(last_near(h, d))
    for h, d in both:
        start(near_copy(h, 0, zs[0], d))
    for h in range(2):
        keep(kv_own.at[h], kv_all.at[h, slot(h, at[side[h]], at["z"])])
    loads[2].wait()
    for h in range(2):
        q_own[h] = q_in[:, h * QCOLS : (h + 1) * QCOLS]
    for h, d in both:
        start(q_copy(h, d))

    for c in loads[3:]:
        c.wait()
    meta_own[...] = jnp.zeros_like(meta_own)
    meta_own[0, 0:2, 0:FMAX] = owners_in[...]
    owners = meta_own[0]
    shard = (at["y"] * NZ + at["z"]) * NX + at["x"]
    listed = pairs_in[pl.ds(jnp.minimum(shard, SHARDS - 1 - shard), 1), :]
    half = jnp.take_along_axis(jnp.broadcast_to(listed, (8, 128)), owners, axis=1) & 1
    row = lax.broadcasted_iota(jnp.int32, (8, 128), 0)
    lane = lax.broadcasted_iota(jnp.int32, (8, 128), 1)
    count = jnp.where(row == 0, counts_in[0], jnp.where(row == 1, counts_in[1], 0))
    place, rest = lane >> 4, lane & (FMAX - 1)
    lists = [jnp.zeros((8, 128), jnp.int32)] * 2
    found = [jnp.zeros((8, 128), jnp.int32)] * 2
    for j in range(FMAX):
        owner, which, live = (
            jnp.sum(jnp.where(lane == j, v, 0), axis=1, keepdims=True)
            for v in (owners, half, (lane < count).astype(jnp.int32))
        )
        oy, oz, ox = owner >> 5, (owner >> 2) & 7, owner & 3
        for h, (holder, spot) in enumerate(((ox, oy), (oy, ox))):
            hit = jnp.logical_and(holder == place, live > 0)
            put = jnp.logical_and(hit, jnp.logical_or(found[h] == 0, found[h] == rest))
            lists[h] = jnp.where(put, oz * 8 + spot * 2 + which, lists[h])
            found[h] = found[h] + hit.astype(jnp.int32)
    for h in range(2):
        meta_own[h, 0:2] = lists[h][0:2]
        meta_own[h, 2:4] = found[h][0:2]
    for h, d in both:
        start(t_copy(h, d, 0))
    for h in range(2):
        keep(q_own.at[h], q_all.at[h, at[cross[h]]])
        keep(meta_own.at[h], meta_all.at[h, at[cross[h]]])

    def arrived(kind, i, h):
        for d in range(2):
            if kind == "z":
                z_copy(d, i, h).wait_recv()
                if i < 4:
                    start(z_copy(d, i + 1, h))
                    for e in range(2):
                        start(near_copy(h, 2 * i - 1 + d, zs[2 * i - 1 + d], e))
                elif d == 1:
                    for e in range(2):
                        start(near_copy(h, 7, zs[7], e))
            elif kind == "near":
                near_copy(h, i, zs[i], d).wait_recv()
                start(far_copy(h, i, zs[i], d))
            elif kind == "q":
                q_copy(h, d).wait_recv()
                start(qf_copy(h, d))
            elif kind == "last near":
                last_near(h, d).wait_recv()
                start(last_far(h, d))
            elif kind == "last far":
                last_far(h, d).wait_recv()
                if d == 1:
                    local[h].wait()
                    for e in range(2):
                        start(last_z(e, 1, h))
            else:
                last_z(d, i, h).wait_recv()
                if i < 4:
                    start(last_z(d, i + 1, h))

    for event in ORDER:
        arrived(*event)
    for h in range(2):
        for d in range(2):
            t_copy(h, d, 0).wait_recv()
        start(t_copy(h, 0, 1))
    for h, d in both:
        qf_copy(h, d).wait_recv()
        for i in range(8):
            far_copy(h, i, zs[i], d).wait_recv()
    for h in range(2):
        t_copy(h, 0, 1).wait_recv()
    for c in sends:
        c.wait_send()
    for c in local[2:]:
        c.wait()


def gather_all(q, k, v, owners, counts, pairs):
    dma = pltpu.SemaphoreType.DMA
    any_spec = pl.BlockSpec(memory_space=pl.ANY)
    arrays = [pltpu.with_memory_space_constraint(a, pltpu.HBM) for a in (q, k, v, owners, pairs, counts)]
    return pl.pallas_call(
        gather_kernel,
        in_specs=[any_spec] * 6,
        out_specs=[any_spec] * 3,
        out_shape=[
            jax.ShapeDtypeStruct((2, 4, 2 * BLOCK_TOKENS, QCOLS), jnp.bfloat16),
            jax.ShapeDtypeStruct((2, SLOTS, MAIN + LAST, HEAD_WIDTH), jnp.bfloat16),
            jax.ShapeDtypeStruct((2, 4, 8, 128), jnp.int32),
        ],
        scratch_shapes=[pltpu.VMEM(a.shape, a.dtype) for a in (q, k, v, owners, pairs)]
        + [
            pltpu.SMEM(counts.shape, counts.dtype),
            pltpu.VMEM((2, 2 * BLOCK_TOKENS, QCOLS), jnp.bfloat16),
            pltpu.VMEM((2, MAIN + LAST, HEAD_WIDTH), jnp.bfloat16),
            pltpu.VMEM((2, 8, 128), jnp.int32),
        ]
        + [dma((n,)) for n in (6, 6, 16, 16, 32, 32, 32, 32, 16, 16, 4, 4, 4, 4, 4, 4, 4, 4, 8, 8)],
        compiler_params=pltpu.CompilerParams(
            collective_id=0, has_side_effects=True, vmem_limit_bytes=16 * 1024 * 1024
        ),
    )(*arrays)


def on_device(queries, keys, values, far_owners, far_counts, pair_blocks):
    q, kv, codes = gather_all(queries, keys, values, far_owners, far_counts, pair_blocks)
    o, stats = attend(codes.reshape(-1), q, kv)
    return send_back(o, stats)


def solution(mesh):
    grid = Mesh(mesh.devices.reshape(NY, NZ, NX, 2), ("y", "z", "x", "head"))
    ctx = ("y", "z", "x")
    placed = (P(ctx, "head"), P(ctx, "head"), P(ctx, "head"), P(ctx, None), P(ctx), P())
    return jax.shard_map(
        on_device,
        mesh=grid,
        in_specs=placed,
        out_specs=P((*ctx, "head"), None),
        check_vma=False,
    )
```

```python
import functools

import jax
import jax.numpy as jnp
from jax import lax
from jax.experimental import pallas as pl
from jax.experimental.pallas import tpu as pltpu
from jax.sharding import Mesh, PartitionSpec as P

HEAD_WIDTH = 128
BLOCK_TOKENS = 128
GROUP = 5
QCOLS = GROUP * HEAD_WIDTH
NY, NZ, NX = 4, 8, 4
SHARDS = NY * NZ * NX
FMAX = 16
SLOTS = 32
ITEMS = 16
UNROLL = 4
NEG = -1e30
EXP_SCALE = 1.4426950408889634 * HEAD_WIDTH ** (-0.5)


def attend_kernel(
    codes_ref, q_in, kv_in, o_ref, stat_ref,
    count_ref, chunk_ref, single_ref, q_ref, kv_ref, acc_ref, m_ref, l_ref, sem,
):
    y, z, x = (lax.axis_index(a) for a in ("y", "z", "x"))

    def loads(pattern):
        return [
            pltpu.make_async_copy(src.at[pattern], dst.at[pattern], sem.at[i, pattern])
            for i, (src, dst) in enumerate(((q_in, q_ref), (kv_in, kv_ref)))
        ]

    for c in loads(0):
        c.start()

    def base_of(pattern, item):
        return (item >> 1) * 1024 + (item & 1) * 128 + (x if pattern == 0 else y) * FMAX

    def build(pattern, item, ends):
        n = codes_ref[base_of(pattern, item) + 2 * 128]
        count_ref[item] = n

        def note(i, chunks):
            chunk_ref[chunks] = item * 16 + i
            return chunks + 1

        single_ref[ends[1]] = item
        return lax.fori_loop(0, n >> 1, note, ends[0]), ends[1] + (n & 1)

    none = (jnp.int32(0), jnp.int32(0))
    middle = lax.fori_loop(0, 8, functools.partial(build, 0), none)
    end = lax.fori_loop(8, 16, functools.partial(build, 1), middle)

    def clear(item, carry):
        @pl.when(((item >> 1) & 3) != jnp.where(item < 8, x, y))
        def _():
            m_ref[item] = jnp.full((QCOLS, HEAD_WIDTH), NEG, jnp.float32)
            l_ref[item] = jnp.zeros((QCOLS, HEAD_WIDTH), jnp.float32)
            acc_ref[item] = jnp.zeros((QCOLS, HEAD_WIDTH), jnp.float32)

        return carry

    lax.fori_loop(0, ITEMS, clear, 0)

    def score(pattern, item, blocks):
        tokens = pl.ds(pl.multiple_of((item & 1) * BLOCK_TOKENS, BLOCK_TOKENS), BLOCK_TOKENS)
        q = q_ref.at[pattern, (item >> 1) & 3, tokens]
        heads = [q[:, g * HEAD_WIDTH : (g + 1) * HEAD_WIDTH] for g in range(GROUP)]
        return lax.dot_general(
            jnp.concatenate(heads, 0), rows_of(pattern, 0, blocks), (((1,), (1,)), ((), ())),
            preferred_element_type=jnp.float32,
        )

    def rows_of(pattern, kind, blocks):
        starts = [
            pl.multiple_of((2 * kind + (b & 1)) * BLOCK_TOKENS, BLOCK_TOKENS) for b in blocks
        ]
        return jnp.concatenate(
            [kv_ref[pattern, b >> 1, pl.ds(i, BLOCK_TOKENS)] for b, i in zip(blocks, starts)], 0
        )

    def split(s):
        return [
            s[:, i : i + BLOCK_TOKENS] for i in range(0, s.shape[1], BLOCK_TOKENS)
        ]

    def top_of(parts):
        return jnp.max(functools.reduce(jnp.maximum, parts), axis=1, keepdims=True)

    def mix(pattern, blocks, p):
        return jnp.dot(
            jnp.concatenate(p, 1).astype(jnp.bfloat16), rows_of(pattern, 1, blocks),
            preferred_element_type=jnp.float32,
        )

    def own_blocks(pattern, row):
        place = y if pattern == 0 else x
        item = (pattern * 4 + (x if pattern == 0 else y)) * 2 + row
        blocks = [(z * 4 + place) * 2 + i for i in range(row + 1)]
        parts = split(score(pattern, item, blocks))
        query_pos = lax.broadcasted_iota(jnp.int32, parts[0].shape, 0) & (BLOCK_TOKENS - 1)
        key_pos = lax.broadcasted_iota(jnp.int32, parts[0].shape, 1)
        parts[-1] = jnp.where(key_pos <= query_pos, parts[-1], NEG)
        m = top_of(parts) * EXP_SCALE
        p = [jnp.exp2(v * EXP_SCALE - m) for v in parts]
        m_ref[item] = jnp.broadcast_to(m, (QCOLS, HEAD_WIDTH))
        l_ref[item] = functools.reduce(jnp.add, p)
        acc_ref[item] = mix(pattern, blocks, p)

    def fetch_pair(pattern, c):
        code = chunk_ref[c]
        item, i = code >> 4, code & 15
        at = base_of(pattern, item) + i * 2
        return item, [codes_ref[at], codes_ref[at + 1]]

    def fetch_single(pattern, c):
        item = single_ref[c]
        return item, [codes_ref[base_of(pattern, item) + count_ref[item] - 1]]

    def absorb(pattern, s, item, blocks):
        parts = split(s)
        m_old = m_ref[item]
        m_new = jnp.maximum(m_old, top_of(parts) * EXP_SCALE)
        alpha = jnp.exp2(m_old - m_new)
        p = [jnp.exp2(v * EXP_SCALE - m_new) for v in parts]
        m_ref[item] = m_new
        l_ref[item] = l_ref[item] * alpha + functools.reduce(jnp.add, p)
        acc_ref[item] = acc_ref[item] * alpha + mix(pattern, blocks, p)

    for pattern, begins, stops in ((0, none, middle), (1, middle, end)):
        for c in loads(pattern):
            c.wait()
        if pattern == 0:
            for c in loads(1):
                c.start()
        for row in range(2):
            own_blocks(pattern, row)
        for fetch, begin, stop in zip((fetch_pair, fetch_single), begins, stops):
            for width in (UNROLL, 2, 1):

                def several(j, carry, pattern=pattern, fetch=fetch, begin=begin, width=width):
                    got = [fetch(pattern, begin + j * width + u) for u in range(width)]
                    scores = [score(pattern, *g) for g in got]
                    for g, s in zip(got, scores):
                        absorb(pattern, s, *g)
                    return carry

                turns = (stop - begin) // width
                lax.fori_loop(0, turns, several, 0)
                begin = begin + turns * width

    lane = lax.broadcasted_iota(jnp.int32, (BLOCK_TOKENS, BLOCK_TOKENS), 1)

    def close(item, carry):
        tops = jnp.zeros((BLOCK_TOKENS, BLOCK_TOKENS), jnp.float32)
        sums = jnp.zeros((BLOCK_TOKENS, BLOCK_TOKENS), jnp.float32)
        for g in range(GROUP):
            part = slice(g * HEAD_WIDTH, (g + 1) * HEAD_WIDTH)
            o_ref[item, :, part] = acc_ref[item, part].astype(jnp.bfloat16)
            tops = jnp.where(lane == g, m_ref[item, part], tops)
            sums = jnp.where(lane == g, jnp.sum(l_ref[item, part], axis=1, keepdims=True), sums)
        stat_ref[item, 0:8] = tops.T[:8]
        stat_ref[item, 8:16] = sums.T[:8]
        return carry

    lax.fori_loop(0, ITEMS, close, 0, unroll=2)


def attend(codes, q, kv):
    any_spec = pl.BlockSpec(memory_space=pl.ANY)
    blocks = pl.BlockSpec(memory_space=pltpu.VMEM)
    state = pltpu.VMEM((ITEMS, QCOLS, HEAD_WIDTH), jnp.float32)
    return pl.pallas_call(
        attend_kernel,
        in_specs=[pl.BlockSpec(memory_space=pltpu.SMEM), any_spec, any_spec],
        out_specs=[blocks, blocks],
        out_shape=[
            jax.ShapeDtypeStruct((ITEMS, BLOCK_TOKENS, QCOLS), jnp.bfloat16),
            jax.ShapeDtypeStruct((ITEMS, 16, BLOCK_TOKENS), jnp.float32),
        ],
        scratch_shapes=[
            pltpu.SMEM((ITEMS,), jnp.int32),
            pltpu.SMEM((ITEMS * FMAX,), jnp.int32),
            pltpu.SMEM((ITEMS + 1,), jnp.int32),
            pltpu.VMEM(q.shape, q.dtype),
            pltpu.VMEM(kv.shape, kv.dtype),
            state, state, state,
            pltpu.SemaphoreType.DMA((2, 2)),
        ],
        compiler_params=pltpu.CompilerParams(vmem_limit_bytes=40 * 1024 * 1024),
    )(codes, q, kv)


def columns(rows):
    rest = jnp.zeros((BLOCK_TOKENS - 8 * len(rows), BLOCK_TOKENS), jnp.float32)
    return jnp.concatenate([*rows, rest], 0).T


def combine(parts, w, g):
    cols = slice(g * HEAD_WIDTH, (g + 1) * HEAD_WIDTH)
    return sum(
        part[:, cols].astype(jnp.float32) * w[:, i * 8 + g : i * 8 + g + 1]
        for i, part in enumerate(parts)
    )


def return_kernel(
    o_in, stat_in, out_ref,
    o_got, stat_got, o_early, o_relay, stat_relay, o_mine, stat_mine, o_sum, stat_sum,
    send, recv, relay_send, relay_recv, own_sem,
):
    at = {"x": lax.axis_index("x"), "y": lax.axis_index("y")}
    core = lax.axis_index("head")
    axes = ("x", "y")

    def chip(p, step):
        return (at[axes[p]] + step) % 4

    barrier = pltpu.get_barrier_semaphore()
    met = [{axes[p]: chip(p, step), "head": k} for p in range(2) for step in (1, 3) for k in range(2)]
    met.append({"head": 1 - core})
    for device in met:
        pl.semaphore_signal(barrier, inc=1, device_id=device, device_id_type=pl.DeviceIdType.MESH)

    def item(p, step, row):
        return (p * 4 + chip(p, step)) * 2 + row

    def own_copies(p, row):
        i = item(p, 3 if row == 0 else 1, row)
        return [
            pltpu.make_async_copy(o_in.at[i], o_mine.at[p, row], own_sem.at[p, row, 0]),
            pltpu.make_async_copy(stat_in.at[i], stat_mine.at[p, row], own_sem.at[p, row, 1]),
        ]

    def kept_copies(p):
        i = item(p, 0, core)
        return [
            pltpu.make_async_copy(o_in.at[i], o_got.at[p, core, 2], own_sem.at[p, 2, 0]),
            pltpu.make_async_copy(stat_in.at[i], stat_got.at[p, core, 2], own_sem.at[p, 2, 1]),
        ]

    def relay_copies(p, row):
        i = item(p, 2, row)
        device = {axes[p]: chip(p, 3 if row == 0 else 1)}
        return [
            copy_to(src.at[i], dst.at[p, row], (relay_send.at[p, row, n], relay_recv.at[p, row, n]), device)
            for n, (src, dst) in enumerate(((o_in, o_relay), (stat_in, stat_relay)))
        ]

    def copies(p, place, row, o_src, stat_src, n):
        device = {"head": row} if place == 2 else {axes[p]: chip(p, 3 - 2 * place), "head": row}
        return [
            copy_to(src, dst.at[p, core, place], (send.at[p, n, k], recv.at[p, place, core, k]), device)
            for k, (src, dst) in enumerate(((o_src, o_got), (stat_src, stat_got)))
        ]

    def plain(p, place):
        row = (1, 0, 1 - core)[place]
        i = item(p, (3, 1, 0)[place], row)
        return copies(p, place, row, o_in.at[i], stat_in.at[i], place)

    def summed(p, row):
        return copies(p, row, row, o_sum.at[p, row], stat_sum.at[p, row], 3 + row)

    both = [(p, row) for row in range(2) for p in range(2)]
    for p, row in both:
        for c in own_copies(p, row):
            c.start()
    for p in range(2):
        for c in kept_copies(p):
            c.start()
    pl.semaphore_wait(barrier, len(met))
    for p, row in both:
        for c in relay_copies(p, row):
            c.start()
    for place in range(3):
        for p in range(2):
            for c in plain(p, place):
                c.start()
    for p, row in both:
        for c in own_copies(p, row):
            c.wait()
        for c in relay_copies(p, row):
            c.wait_recv()
        stats = [stat_mine[p, row], stat_relay[p, row]]
        top = jnp.maximum(stats[0][:8], stats[1][:8])
        f = [jnp.exp2(v[:8] - top) for v in stats]
        stat_sum[p, row, 0:8] = top
        stat_sum[p, row, 8:16] = stats[0][8:] * f[0] + stats[1][8:] * f[1]
        w = columns(f)
        for g in range(GROUP):
            cols = slice(g * HEAD_WIDTH, (g + 1) * HEAD_WIDTH)
            mixed = combine([o_mine.at[p, row], o_relay.at[p, row]], w, g)
            o_sum[p, row, :, cols] = mixed.astype(jnp.bfloat16)
        for c in summed(p, row):
            c.start()

    def arrival(p, place, c, k):
        dst = (o_got, stat_got)[k].at[p, c, place]
        return copy_to(dst, dst, (send.at[p, 0, k], recv.at[p, place, c, k]), {"head": 1 - core})

    tops, sums = {}, {}
    for p in range(2):
        for c in kept_copies(p):
            c.wait()
        for k in range(2):
            arrival(p, 2, 1 - core, k).wait_recv()
            for c in range(2):
                arrival(p, 1 - core, c, k).wait_recv()
        for c in range(2):
            stats = [stat_got[p, c, 2], stat_got[p, c, 1 - core]]
            tops[p, c] = jnp.maximum(stats[0][:8], stats[1][:8])
            f = [jnp.exp2(v[:8] - tops[p, c]) for v in stats]
            sums[p, c] = stats[0][8:] * f[0] + stats[1][8:] * f[1]
            w = columns(f)
            for g in range(GROUP):
                cols = slice(g * HEAD_WIDTH, (g + 1) * HEAD_WIDTH)
                o_early[p, c, :, cols] = combine(
                    [o_got.at[p, c, 2], o_got.at[p, c, 1 - core]], w, g
                )
    for p in range(2):
        for c in range(2):
            for k in range(2):
                arrival(p, core, c, k).wait_recv()
            stat = stat_got[p, c, core]
            top = jnp.maximum(tops[p, c], stat[:8])
            f = [jnp.exp2(tops[p, c] - top), jnp.exp2(stat[:8] - top)]
            total = sums[p, c] * f[0] + stat[8:] * f[1]
            inv = 1.0 / jnp.where(total > 0, total, 1.0)
            w = columns([v * inv for v in f])
            for g in range(GROUP):
                start = (c * 2 + p) * QCOLS + g * HEAD_WIDTH
                mixed = combine([o_early.at[p, c], o_got.at[p, c, core]], w, g)
                out_ref[:, start : start + HEAD_WIDTH] = mixed.astype(jnp.bfloat16)
    for p, row in both:
        for c in relay_copies(p, row) + summed(p, row):
            c.wait_send()
    for p in range(2):
        for place in range(3):
            for c in plain(p, place):
                c.wait_send()


def send_back(o, stats):
    dma = pltpu.SemaphoreType.DMA
    any_spec = pl.BlockSpec(memory_space=pl.ANY)
    partial, figures = (BLOCK_TOKENS, QCOLS), (16, BLOCK_TOKENS)
    pairs = [pltpu.VMEM((2, 2, *partial), jnp.bfloat16), pltpu.VMEM((2, 2, *figures), jnp.float32)]
    return pl.pallas_call(
        return_kernel,
        in_specs=[any_spec] * 2,
        out_specs=pl.BlockSpec(memory_space=pltpu.VMEM),
        out_shape=jax.ShapeDtypeStruct((BLOCK_TOKENS, 4 * QCOLS), jnp.bfloat16),
        scratch_shapes=[
            pltpu.VMEM((2, 2, 3, *partial), jnp.bfloat16),
            pltpu.VMEM((2, 2, 3, *figures), jnp.float32),
            pltpu.VMEM((2, 2, *partial), jnp.float32),
            *(pairs * 3),
            dma((2, 5, 2)), dma((2, 3, 2, 2)), dma((2, 2, 2)), dma((2, 2, 2)), dma((2, 3, 2)),
        ],
        compiler_params=pltpu.CompilerParams(
            collective_id=1, has_side_effects=True, vmem_limit_bytes=16 * 1024 * 1024
        ),
    )(o, stats)


def copy_to(src, dst, sems, device):
    return pltpu.make_async_remote_copy(
        src_ref=src, dst_ref=dst, send_sem=sems[0], recv_sem=sems[1],
        device_id=device, device_id_type=pl.DeviceIdType.MESH,
    )


MAIN = 3 * BLOCK_TOKENS
LAST = BLOCK_TOKENS
ORDER = (
    ("last near", 0, 0), ("last near", 0, 1), ("z", 1, 0), ("near", 0, 0), ("near", 0, 1),
    ("z", 1, 1), ("z", 2, 0), ("z", 2, 1), ("q", 0, 1), ("q", 0, 0), ("last far", 0, 0),
    ("z", 3, 0), ("last far", 0, 1), ("near", 1, 0), ("z", 3, 1), ("near", 1, 1), ("near", 2, 0),
    ("last z", 1, 0), ("near", 2, 1), ("z", 4, 0), ("near", 3, 0), ("near", 3, 1),
    ("last z", 1, 1), ("near", 4, 0), ("near", 4, 1), ("z", 4, 1), ("last z", 2, 0),
    ("near", 5, 0), ("near", 5, 1), ("last z", 2, 1), ("near", 6, 0), ("near", 6, 1),
    ("last z", 3, 0), ("last z", 3, 1), ("near", 7, 0), ("last z", 4, 0), ("near", 7, 1),
    ("last z", 4, 1),
)


def gather_kernel(
    q_hbm, k_hbm, v_hbm, owners_hbm, pairs_hbm, counts_hbm, q_all, kv_all, meta_all,
    q_in, k_in, v_in, owners_in, pairs_in, counts_in, q_own, kv_own, meta_own, in_sem, local_sem,
    z_send, z_recv, near_send, near_recv, far_send, far_recv,
    lz_send, lz_recv, ln_send, ln_recv, lf_send, lf_recv,
    q_send, q_recv, qf_send, qf_recv, t_send, t_recv,
):
    at = {a: lax.axis_index(a) for a in ("y", "z", "x")}
    size = {"y": NY, "z": NZ, "x": NX}
    ring = {a: ((at[a] + 1) % size[a], (at[a] + size[a] - 1) % size[a]) for a in at}

    barrier = pltpu.get_barrier_semaphore()
    for a in at:
        for n in ring[a]:
            pl.semaphore_signal(
                barrier, inc=1, device_id={a: n}, device_id_type=pl.DeviceIdType.MESH
            )

    loads = [
        pltpu.make_async_copy(src, dst, in_sem.at[i])
        for i, (src, dst) in enumerate(
            (
                (k_hbm, k_in), (v_hbm, v_in), (q_hbm, q_in),
                (owners_hbm, owners_in), (pairs_hbm, pairs_in), (counts_hbm, counts_in),
            )
        )
    ]
    for c in loads:
        c.start()

    side = ("y", "x")
    cross = ("x", "y")

    def slot(h, place, zo):
        return zo * 4 + place

    local = []

    def keep(src, dst):
        c = pltpu.make_async_copy(src, dst, local_sem.at[len(local)])
        c.start()
        local.append(c)

    sends = []

    def part(d):
        return pl.ds(d * (MAIN // 2), MAIN // 2)

    def z_copy(d, s, h):
        back = at["z"] - (s - 1) if d == 0 else at["z"] + (s - 1)
        rows = part(d) if s == 4 else pl.ds(0, MAIN)
        ref = kv_all.at[h, slot(h, at[side[h]], (back + NZ) % NZ), rows]
        i = (d * 4 + s - 1) * 2 + h
        src = kv_own.at[h, rows] if s == 1 else ref
        return copy_to(src, ref, (z_send.at[i], z_recv.at[i]), {"z": ring["z"][d]})

    def near_copy(h, i, zo, d):
        rows = pl.ds(0, MAIN)
        ref = kv_all.at[h, slot(h, at[side[h]], zo), rows]
        n = (h * 8 + i) * 2 + d
        src = kv_own.at[h, rows] if i == 0 else ref
        return copy_to(src, ref, (near_send.at[n], near_recv.at[n]), {side[h]: ring[side[h]][d]})

    def far_copy(h, i, zo, d):
        a = side[h]
        ref = kv_all.at[h, slot(h, ring[a][1 - d], zo), part(d)]
        n = (h * 8 + i) * 2 + d
        return copy_to(ref, ref, (far_send.at[n], far_recv.at[n]), {a: ring[a][d]})

    def last_near(h, d):
        a = side[h]
        rows = pl.ds(MAIN, LAST)
        ref = kv_all.at[h, slot(h, at[a], at["z"]), rows]
        n = h * 2 + d
        return copy_to(kv_own.at[h, rows], ref, (ln_send.at[n], ln_recv.at[n]), {a: ring[a][d]})

    def last_far(h, d):
        a = side[h]
        rows = pl.ds(MAIN + d * (LAST // 2), LAST // 2)
        ref = kv_all.at[h, slot(h, ring[a][1 - d], at["z"]), rows]
        n = h * 2 + d
        return copy_to(ref, ref, (lf_send.at[n], lf_recv.at[n]), {a: ring[a][d]})

    def last_z(d, s, h):
        back = at["z"] - (s - 1) if d == 0 else at["z"] + (s - 1)
        first = ((back + NZ) % NZ) * 4
        places = pl.ds(first + 2 * d, 2) if s == 4 else pl.ds(first, 4)
        ref = kv_all.at[h, places, pl.ds(MAIN, LAST)]
        i = (d * 4 + s - 1) * 2 + h
        return copy_to(ref, ref, (lz_send.at[i], lz_recv.at[i]), {"z": ring["z"][d]})

    def q_copy(h, d):
        a = cross[h]
        ref = q_all.at[h, at[a]]
        return copy_to(
            q_own.at[h], ref, (q_send.at[h * 2 + d], q_recv.at[h * 2 + d]), {a: ring[a][d]}
        )

    def qf_copy(h, d):
        a = cross[h]
        ref = q_all.at[h, ring[a][1 - d], pl.ds(d * BLOCK_TOKENS, BLOCK_TOKENS)]
        return copy_to(
            ref, ref, (qf_send.at[h * 2 + d], qf_recv.at[h * 2 + d]), {a: ring[a][d]}
        )

    def t_copy(h, d, relay):
        a = cross[h]
        ref = meta_all.at[h, ring[a][1 - d] if relay else at[a]]
        i = (h * 2 + d) * 2 + relay
        return copy_to(
            ref if relay else meta_own.at[h], ref, (t_send.at[i], t_recv.at[i]), {a: ring[a][d]}
        )

    def start(c):
        c.start()
        sends.append(c)

    both = [(h, d) for h in range(2) for d in range(2)]
    zs = [at["z"]]
    for s in range(1, 5):
        zs.append((at["z"] - s + NZ) % NZ)
        zs.append((at["z"] + s) % NZ)
    zs = zs[:8]

    for i, ref in enumerate((k_in, v_in)):
        loads[i].wait()
        for h in range(2):
            kv_own[h, i * 256 : i * 256 + 256] = ref[:, h * HEAD_WIDTH : (h + 1) * HEAD_WIDTH]
    pl.semaphore_wait(barrier, 6)
    for h, d in both:
        start(z_copy(d, 1, h))
    for h, d in both:
        start(last_near(h, d))
    for h, d in both:
        start(near_copy(h, 0, zs[0], d))
    for h in range(2):
        keep(kv_own.at[h], kv_all.at[h, slot(h, at[side[h]], at["z"])])
    loads[2].wait()
    for h in range(2):
        q_own[h] = q_in[:, h * QCOLS : (h + 1) * QCOLS]
    for h, d in both:
        start(q_copy(h, d))

    for c in loads[3:]:
        c.wait()
    meta_own[...] = jnp.zeros_like(meta_own)
    meta_own[0, 0:2, 0:FMAX] = owners_in[...]
    owners = meta_own[0]
    shard = (at["y"] * NZ + at["z"]) * NX + at["x"]
    listed = pairs_in[pl.ds(jnp.minimum(shard, SHARDS - 1 - shard), 1), :]
    half = jnp.take_along_axis(jnp.broadcast_to(listed, (8, 128)), owners, axis=1) & 1
    row = lax.broadcasted_iota(jnp.int32, (8, 128), 0)
    lane = lax.broadcasted_iota(jnp.int32, (8, 128), 1)
    count = jnp.where(row == 0, counts_in[0], jnp.where(row == 1, counts_in[1], 0))
    place, rest = lane >> 4, lane & (FMAX - 1)
    lists = [jnp.zeros((8, 128), jnp.int32)] * 2
    found = [jnp.zeros((8, 128), jnp.int32)] * 2
    for j in range(FMAX):
        owner, which, live = (
            jnp.sum(jnp.where(lane == j, v, 0), axis=1, keepdims=True)
            for v in (owners, half, (lane < count).astype(jnp.int32))
        )
        oy, oz, ox = owner >> 5, (owner >> 2) & 7, owner & 3
        for h, (holder, spot) in enumerate(((ox, oy), (oy, ox))):
            hit = jnp.logical_and(holder == place, live > 0)
            put = jnp.logical_and(hit, jnp.logical_or(found[h] == 0, found[h] == rest))
            lists[h] = jnp.where(put, oz * 8 + spot * 2 + which, lists[h])
            found[h] = found[h] + hit.astype(jnp.int32)
    for h in range(2):
        meta_own[h, 0:2] = lists[h][0:2]
        meta_own[h, 2:4] = found[h][0:2]
    for h, d in both:
        start(t_copy(h, d, 0))
    for h in range(2):
        keep(q_own.at[h], q_all.at[h, at[cross[h]]])
        keep(meta_own.at[h], meta_all.at[h, at[cross[h]]])

    def arrived(kind, i, h):
        for d in range(2):
            if kind == "z":
                z_copy(d, i, h).wait_recv()
                if i < 4:
                    start(z_copy(d, i + 1, h))
                    for e in range(2):
                        start(near_copy(h, 2 * i - 1 + d, zs[2 * i - 1 + d], e))
                elif d == 1:
                    for e in range(2):
                        start(near_copy(h, 7, zs[7], e))
            elif kind == "near":
                near_copy(h, i, zs[i], d).wait_recv()
                start(far_copy(h, i, zs[i], d))
            elif kind == "q":
                q_copy(h, d).wait_recv()
                start(qf_copy(h, d))
            elif kind == "last near":
                last_near(h, d).wait_recv()
                start(last_far(h, d))
            elif kind == "last far":
                last_far(h, d).wait_recv()
                if d == 1:
                    local[h].wait()
                    for e in range(2):
                        start(last_z(e, 1, h))
            else:
                last_z(d, i, h).wait_recv()
                if i < 4:
                    start(last_z(d, i + 1, h))

    for event in ORDER:
        arrived(*event)
    for h in range(2):
        for d in range(2):
            t_copy(h, d, 0).wait_recv()
        start(t_copy(h, 0, 1))
    for h, d in both:
        qf_copy(h, d).wait_recv()
        for i in range(8):
            far_copy(h, i, zs[i], d).wait_recv()
    for h in range(2):
        t_copy(h, 0, 1).wait_recv()
    for c in sends:
        c.wait_send()
    for c in local[2:]:
        c.wait()


def gather_all(q, k, v, owners, counts, pairs):
    dma = pltpu.SemaphoreType.DMA
    any_spec = pl.BlockSpec(memory_space=pl.ANY)
    arrays = [pltpu.with_memory_space_constraint(a, pltpu.HBM) for a in (q, k, v, owners, pairs, counts)]
    return pl.pallas_call(
        gather_kernel,
        in_specs=[any_spec] * 6,
        out_specs=[any_spec] * 3,
        out_shape=[
            jax.ShapeDtypeStruct((2, 4, 2 * BLOCK_TOKENS, QCOLS), jnp.bfloat16),
            jax.ShapeDtypeStruct((2, SLOTS, MAIN + LAST, HEAD_WIDTH), jnp.bfloat16),
            jax.ShapeDtypeStruct((2, 4, 8, 128), jnp.int32),
        ],
        scratch_shapes=[pltpu.VMEM(a.shape, a.dtype) for a in (q, k, v, owners, pairs)]
        + [
            pltpu.SMEM(counts.shape, counts.dtype),
            pltpu.VMEM((2, 2 * BLOCK_TOKENS, QCOLS), jnp.bfloat16),
            pltpu.VMEM((2, MAIN + LAST, HEAD_WIDTH), jnp.bfloat16),
            pltpu.VMEM((2, 8, 128), jnp.int32),
        ]
        + [dma((n,)) for n in (6, 6, 16, 16, 32, 32, 32, 32, 16, 16, 4, 4, 4, 4, 4, 4, 4, 4, 8, 8)],
        compiler_params=pltpu.CompilerParams(
            collective_id=0, has_side_effects=True, vmem_limit_bytes=16 * 1024 * 1024
        ),
    )(*arrays)


def on_device(queries, keys, values, far_owners, far_counts, pair_blocks):
    q, kv, codes = gather_all(queries, keys, values, far_owners, far_counts, pair_blocks)
    o, stats = attend(codes.reshape(-1), q, kv)
    return send_back(o, stats)


def solution(mesh):
    grid = Mesh(mesh.devices.reshape(NY, NZ, NX, 2), ("y", "z", "x", "head"))
    ctx = ("y", "z", "x")
    placed = (P(ctx, "head"), P(ctx, "head"), P(ctx, "head"), P(ctx, None), P(ctx), P())
    return jax.shard_map(
        on_device,
        mesh=grid,
        in_specs=placed,
        out_specs=P((*ctx, "head"), None),
        check_vma=False,
    )
```
